128 devices in a mesh: dp: 2 (over x_hi), row: 8 (over x_lo, y), col: 8 (over z, core).
Axes of the slice: x: 4 (x_hi: 2, x_lo: 2; x = x_hi * 2 + x_lo), y: 4, z: 4, core: 2. Of those that a mesh axis runs over, the one named last changes fastest.
Arguments:
- inputs: bfloat16 [2, 4, 2048, 2048], P(None, 'dp', 'col', 'row'), may hold values from -6 to 6
- lengths: int32 [2, 4], P(None, 'dp'), may hold values from 512 to 2048, as said below
- ln1_gain: float32 [2048], P('row'), may hold values from 0.5 to 1.5
- ln1_bias: float32 [2048], P('row'), may hold values from -4 to 4
- w_qkv: bfloat16 [3, 2048, 2048], P(None, 'row', 'col'), may hold values from -0.125 to 0.125
- qv_bias: float32 [2, 2048], P(None, 'col'), may hold values from -4 to 4
- w_out: bfloat16 [2048, 2048], P('col', 'row'), may hold values from -0.75 to 0.75
- out_bias: float32 [2048], P('row'), may hold values from -4 to 4
- ln2_gain: float32 [2048], P('row'), may hold values from 0.5 to 1.5
- ln2_bias: float32 [2048], P('row'), may hold values from -4 to 4
- w_up: bfloat16 [2048, 8192], P('row', 'col'), may hold values from -0.125 to 0.125
- up_bias: float32 [8192], P('col'), may hold values from -4 to 4
- w_down: bfloat16 [8192, 2048], P('col', 'row'), may hold values from -0.0625 to 0.0625
- down_bias: float32 [2048], P('row'), may hold values from -4 to 4
- cotangent: bfloat16 [2, 4, 2048, 2048], P(None, 'dp', 'col', 'row'), may hold values from -6 to 6
Outputs:
- mixed: bfloat16 [2, 4, 2048, 2048], P(None, 'dp', 'col', 'row')
- input_grad: float32 [2, 4, 2048, 2048], P(None, 'dp', 'col', 'row')
- ln1_gain_grad: float32 [2048], P('row')
- ln1_bias_grad: float32 [2048], P('row')
- qkv_grad: float32 [3, 2048, 2048], P(None, 'row', 'col')
- qv_bias_grad: float32 [2, 2048], P(None, 'col')
- out_grad: float32 [2048, 2048], P('col', 'row')
- out_bias_grad: float32 [2048], P('row')
- ln2_gain_grad: float32 [2048], P('row')
- ln2_bias_grad: float32 [2048], P('row')
- up_grad: float32 [2048, 8192], P('row', 'col')
- up_bias_grad: float32 [8192], P('col')
- down_grad: float32 [8192, 2048], P('col', 'row')
- down_bias_grad: float32 [2048], P('row')
The draws below stay inside these ranges and needn't reach their ends.
Inputs may be any that keep to these rules, and one draw needn't show every extreme that they name: `lengths`: in every micro-batch, each run of 2 sequences that one index of dp holds has one of length 2048.
All inputs are finite; a program needn't handle non-finite values.
Results may differ from the reference program's by a relative error of at most 0.035.
Values may be sent and summed in bfloat16 or wider, within the bound.
A program may use at most 256 MiB of HBM per device.

```python
import jax
import jax.numpy as jnp
from jax import lax

D = 2048
HEADS = 16
HEAD_DIM = 128
FF = 8192
S = 2048
MIN_LEN = 512
MB = 2
SEQ_MB = 2
SEQS = 4


def draw_lengths(key, part):
    key = jax.random.fold_in(key, 11)
    first, second = jax.random.split(key)
    base = jax.random.randint(first, (MB, SEQS), MIN_LEN, S + 1)
    groups = SEQS // SEQ_MB
    chosen = jax.random.randint(second, (MB, groups), 0, SEQ_MB)
    index = jnp.arange(SEQS)
    full = (index % SEQ_MB)[None, :] == jnp.repeat(chosen, SEQ_MB, axis=1)
    return jnp.where(full, S, base).astype(jnp.int32)


def steps_of(own_key, shape, cuts, smallest, largest):
    factor_of, own = 1.0, jax.random.fold_in(own_key, 6)
    for position, shards_of in cuts:
        steps = jnp.exp(jax.random.uniform(jax.random.fold_in(own, position), (shards_of,), jnp.float32, smallest / len(cuts), largest / len(cuts)))
        factor_of = factor_of * jnp.repeat(steps, shape[position] // shards_of).reshape([-1 if axis == position else 1 for axis in range(len(shape))])
    return factor_of


def noise(key, extent, scale, reach, shards=(), kind=jnp.bfloat16):
    factor_of = steps_of(key, extent, shards, -0.22, 0.18) if shards else 1.0
    values = jax.random.normal(key, extent, jnp.float32) * scale * factor_of
    return jnp.minimum(jnp.maximum(values, -reach), reach).astype(kind)


def setup_inputs(seed: int = 0) -> dict:
    streams_of = jax.random.split(jax.random.key(seed), 16)
    return {
        "inputs": noise(streams_of[0], (MB, SEQS, S, D), 1.0, 6.0, ((1, 2), (2, 8), (3, 8))),
        "lengths": draw_lengths(jax.random.fold_in(streams_of[15], 71), 0),
        "ln1_gain": jnp.clip(1.0 + 0.1 * jax.random.normal(streams_of[2], (D,), jnp.float32), 0.5, 1.5),
        "ln1_bias": noise(streams_of[3], (D,), 0.3, 4.0, ((0, 8),), jnp.float32),
        "w_qkv": noise(streams_of[4], (3, D, D), D ** -0.5, 0.125, ((1, 8), (2, 8))),
        "qv_bias": noise(streams_of[5], (2, D), 0.3, 4.0, ((1, 8),), jnp.float32),
        "w_out": noise(streams_of[6], (D, D), (D // 32) ** -0.5, 0.75, ((0, 8), (1, 8))),
        "out_bias": noise(streams_of[7], (D,), 0.3, 4.0, ((0, 8),), jnp.float32),
        "ln2_gain": jnp.clip(1.0 + 0.1 * jax.random.normal(streams_of[8], (D,), jnp.float32), 0.5, 1.5),
        "ln2_bias": noise(streams_of[9], (D,), 0.3, 4.0, ((0, 8),), jnp.float32),
        "w_up": noise(streams_of[10], (D, FF), D ** -0.5, 0.125, ((0, 8), (1, 8))),
        "up_bias": noise(streams_of[11], (FF,), 0.3, 4.0, ((0, 8),), jnp.float32),
        "w_down": noise(streams_of[12], (FF, D), FF ** -0.5, 0.0625, ((0, 8), (1, 8))),
        "down_bias": noise(streams_of[13], (D,), 0.3, 4.0, ((0, 8),), jnp.float32),
        "cotangent": noise(streams_of[14], (MB, SEQS, S, D), 1.0, 6.0, ((1, 2), (2, 8), (3, 8))),
    }


@jax.custom_vjp
def low(v):
    return lax.optimization_barrier(v.astype(jnp.bfloat16)).astype(jnp.float32)

@jax.custom_vjp
def low_back(v):
    return v

def low_keep(v):
    return (low(v), None)

def low_pass(kept, grad):
    return (grad,)

def back_keep(v):
    return (v, None)

def back_low(kept, grad):
    return (low(grad),)
low.defvjp(low_keep, low_pass)
low_back.defvjp(back_keep, back_low)

def matmul(left, right):
    return jnp.dot(left, right, precision=lax.Precision.HIGHEST)

def layer_norm(values, gain, bias):
    middle = lax.optimization_barrier(jnp.mean(values, -1, keepdims=True))
    spread = lax.optimization_barrier(jnp.mean(values * values, -1, keepdims=True)) - middle * middle
    return (values - middle) * lax.rsqrt(spread + 1e-05) * gain + bias

def attention(queries, keys, values, length):
    block_rows = min(512, S)
    positions = jnp.arange(S).astype(jnp.int32)

    def block(start):
        query_block = lax.dynamic_slice_in_dim(queries, start, block_rows, 0)
        query_pos = start + jnp.arange(block_rows).astype(jnp.int32)
        raw = jnp.einsum('qhd,khd->hqk', query_block, keys, precision=lax.Precision.HIGHEST) * HEAD_DIM ** (-0.5)
        scores = low_back(raw)
        allowed = (positions[None, :] <= query_pos[:, None]) & (positions[None, :] < length)
        masked = jnp.where(allowed[None], scores, -1e+30)
        highest = lax.optimization_barrier(jnp.max(masked, -1, keepdims=True))
        weights = jnp.where(allowed[None], jnp.exp(masked - highest), 0.0)
        probs = low(weights / lax.optimization_barrier(jnp.sum(weights, -1, keepdims=True)))
        return jnp.einsum('hqk,khd->qhd', probs, values, precision=lax.Precision.HIGHEST)
    starts = (jnp.arange(S // block_rows) * block_rows).astype(jnp.int32)
    result = lax.map(jax.checkpoint(block), starts)
    return result.reshape(S, HEADS * HEAD_DIM)

def layer(tokens, length, params):
    gain_one, bias_one, w_qkv, qv_bias, w_out, out_bias, gain_two, bias_two, w_up, up_bias, w_down, down_bias = params
    normed1 = low(layer_norm(tokens, gain_one, bias_one))
    queries = low(low_back(matmul(normed1, w_qkv[0]) + qv_bias[0]))
    keys = low(low_back(matmul(normed1, w_qkv[1])))
    values = low(low_back(matmul(normed1, w_qkv[2]) + qv_bias[1]))
    shaped = (S, HEADS, HEAD_DIM)
    attended = attention(queries.reshape(shaped), keys.reshape(shaped), values.reshape(shaped), length)
    att_low = low(low_back(attended))
    middle = tokens + low_back(matmul(att_low, w_out) + out_bias)
    normed2 = low(layer_norm(middle, gain_two, bias_two))
    hidden = low_back(matmul(normed2, w_up) + up_bias)
    activation = low(jax.nn.gelu(hidden, approximate=False))
    return middle + low_back(matmul(activation, w_down) + down_bias)

def forward(tokens, params, lengths):
    flat = tokens.reshape(-1, S, D)
    flat_lengths = lengths.reshape(-1)

    def one(item):
        return layer(item[0], item[1], params)
    result = lax.map(jax.checkpoint(one), (flat, flat_lengths))
    return result.reshape(tokens.shape)

def reference(inputs, lengths, ln1_gain, ln1_bias, w_qkv, qv_bias, w_out, out_bias, ln2_gain, ln2_bias, w_up, up_bias, w_down, down_bias, cotangent):
    params = tuple((p.astype(jnp.float32) for p in (ln1_gain, ln1_bias, w_qkv, qv_bias, w_out, out_bias, ln2_gain, ln2_bias, w_up, up_bias, w_down, down_bias)))
    tokens = inputs.astype(jnp.float32)
    result, pullback = jax.vjp(lambda values, weights: forward(values, weights, lengths), tokens, params)
    input_grad, grads = pullback(cotangent.astype(jnp.float32))
    g_ln1_gain, g_ln1_bias, g_qkv, g_qv_bias, g_out, g_out_bias, g_ln2_gain, g_ln2_bias, g_up, g_up_bias, g_down, g_down_bias = grads
    return (result.astype(jnp.bfloat16), input_grad, g_ln1_gain, g_ln1_bias, g_qkv, g_qv_bias, g_out, g_out_bias, g_ln2_gain, g_ln2_bias, g_up, g_up_bias, g_down, g_down_bias)
```

```python
import functools

import jax
import jax.numpy as jnp
from jax import lax
from jax.experimental import pallas as pl
from jax.experimental.pallas import tpu as pltpu
from jax.sharding import PartitionSpec as P

D = 2048
HEAD = 128
SCALE = HEAD**-0.5
EPSILON = 1e-05
HUGE = 1e30
LOW = jnp.bfloat16
OWN = 128
VMEM_LIMIT = 56 * 2**20


def dot(a, b, contract):
    return lax.dot_general(a, b, ((contract[0], contract[1]), ((), ())), preferred_element_type=jnp.float32)


NN = ((1,), (0,))
NT = ((1,), (1,))
TN = ((0,), (0,))


def place_rows(group, half):
    row = lax.broadcasted_iota(jnp.int32, (256, 1), 0)
    return (2 * group + row // OWN) * 256 + half * OWN + row % OWN


def allowed_keys(group, extent, half, length):
    slot = lax.broadcasted_iota(jnp.int32, (256, extent), 1)
    return (slot <= place_rows(group, half)) & (slot < length)


def attend_kernel(meta_ref, q_ref, k_ref, v_ref, o_ref, lse_ref):
    half, length = meta_ref[0], meta_ref[1]
    for head in range(2):
        cols = pl.ds(head * HEAD, HEAD)
        for group in range(4):
            rows, extent = pl.ds(group * 256, 256), 512 * (group + 1)
            scores = dot(q_ref[rows, cols], k_ref[:extent, cols], NT) * SCALE
            allowed = allowed_keys(group, extent, half, length)
            scores = jnp.where(allowed, scores, -HUGE)
            highest = jnp.max(scores, -1, keepdims=True)
            weights = jnp.exp(scores - highest)
            total = jnp.sum(weights, -1, keepdims=True)
            out = dot(weights.astype(LOW), v_ref[:extent, cols], NN) / total
            o_ref[rows, cols] = out.astype(LOW)
            lse_ref[head, rows, :] = highest + jnp.log(total)


def attend(meta, q, k, v):
    vm = pl.BlockSpec(memory_space=pltpu.VMEM)
    return pl.pallas_call(
        attend_kernel,
        out_shape=(
            jax.ShapeDtypeStruct((1024, 256), LOW),
            jax.ShapeDtypeStruct((2, 1024, 1), jnp.float32),
        ),
        in_specs=[pl.BlockSpec(memory_space=pltpu.SMEM), vm, vm, vm],
        out_specs=(vm, vm),
        compiler_params=pltpu.CompilerParams(vmem_limit_bytes=VMEM_LIMIT),
        cost_estimate=pl.CostEstimate(flops=4 * 10**9, bytes_accessed=4 * 10**6, transcendentals=2 * 10**6),
    )(meta, q, k, v)


def attend_back_kernel(meta_ref, q_ref, k_ref, v_ref, do_ref, lse_ref, dq_ref, dk_ref, dv_ref):
    half, length = meta_ref[0], meta_ref[1]
    for head in range(2):
        cols = pl.ds(head * HEAD, HEAD)
        for group in reversed(range(4)):
            rows, extent = pl.ds(group * 256, 256), 512 * (group + 1)
            q, k, v, do = q_ref[rows, cols], k_ref[:extent, cols], v_ref[:extent, cols], do_ref[rows, cols]
            scores = dot(q, k, NT) * SCALE
            allowed = allowed_keys(group, extent, half, length)
            probs = jnp.exp(jnp.where(allowed, scores, -HUGE) - lse_ref[head, rows, :])
            dprobs = dot(do, v, NT)
            weighted = probs * dprobs
            delta = jnp.sum(weighted, -1, keepdims=True)
            dscores = (weighted - probs * delta).astype(LOW)
            dq_ref[rows, cols] = (dot(dscores, k, NN) * SCALE).astype(LOW)
            dk = dot(dscores, q, TN) * SCALE
            dv = dot(probs.astype(LOW), do, TN)
            if group == 3:
                dk_ref[:, cols] = dk
                dv_ref[:, cols] = dv
            else:
                dk_ref[:extent, cols] += dk
                dv_ref[:extent, cols] += dv


def attend_back(meta, q, k, v, do, lse):
    vm = pl.BlockSpec(memory_space=pltpu.VMEM)
    return pl.pallas_call(
        attend_back_kernel,
        out_shape=(
            jax.ShapeDtypeStruct((1024, 256), LOW),
            jax.ShapeDtypeStruct((2048, 256), jnp.float32),
            jax.ShapeDtypeStruct((2048, 256), jnp.float32),
        ),
        in_specs=[pl.BlockSpec(memory_space=pltpu.SMEM), vm, vm, vm, vm, vm],
        out_specs=(vm, vm, vm),
        compiler_params=pltpu.CompilerParams(vmem_limit_bytes=VMEM_LIMIT),
        cost_estimate=pl.CostEstimate(flops=10 * 10**9, bytes_accessed=8 * 10**6, transcendentals=2 * 10**6),
    )(meta, q, k, v, do, lse)


def to_own(a):
    sent = a.reshape(2, 2, 2, OWN, 256).transpose(2, 0, 1, 3, 4).reshape(8, OWN, 256)
    got = lax.all_to_all(sent, "row", 0, 0, tiled=True)
    return got.transpose(1, 0, 2).reshape(OWN, D)


def from_own(a):
    sent = a.reshape(OWN, 8, 256).transpose(1, 0, 2)
    got = lax.all_to_all(sent, "row", 0, 0, tiled=True)
    return got.reshape(2, 2, 2, OWN, 256).transpose(1, 2, 0, 3, 4).reshape(2, 2, 256, 256)


def norm(values, gain, bias):
    middle = jnp.mean(values, -1, keepdims=True)
    spread = jnp.mean(values * values, -1, keepdims=True) - middle * middle
    inverse = lax.rsqrt(spread + EPSILON)
    centred = (values - middle) * inverse
    return centred, inverse, (centred * gain + bias).astype(LOW)


def norm_back(grad, centred, inverse, gain):
    scaled = grad * gain
    return inverse * (
        scaled - jnp.mean(scaled, -1, keepdims=True) - centred * jnp.mean(scaled * centred, -1, keepdims=True)
    )


def col_gather(a):
    return lax.all_gather(a, "col", axis=0, tiled=True)


def col_reduce(a):
    return lax.psum_scatter(a.astype(LOW), "col", scatter_dimension=0, tiled=True).astype(jnp.float32)


def partner_swap(a):
    return lax.ppermute(a, "row", [(i, (i + 4) % 8) for i in range(8)])


def total_grad(a, axis):
    part = lax.psum_scatter(a.astype(LOW), "row", scatter_dimension=axis, tiled=True)
    other = lax.ppermute(part, "dp", [(0, 1), (1, 0)])
    return part.astype(jnp.float32) + other.astype(jnp.float32)


def shards(
    inputs,
    lengths,
    ln1_gain,
    ln1_bias,
    w_qkv,
    qv_bias,
    w_out,
    out_bias,
    ln2_gain,
    ln2_bias,
    w_up,
    up_bias,
    w_down,
    down_bias,
    cotangent,
):
    row = lax.axis_index("row")
    half, micro, seq = row // 4, (row // 2) % 2, row % 2
    meta = jnp.stack([half, lengths[micro, seq]]).astype(jnp.int32)
    small = jnp.stack([ln1_gain, ln1_bias, out_bias, ln2_gain, ln2_bias, down_bias])
    small = lax.all_gather(small, "row", axis=1, tiled=True)
    gain1, bias1, bias_out, gain2, bias2, bias_down = [small[i] for i in range(6)]
    wq = lax.all_gather(w_qkv, "row", axis=1, tiled=True)
    wo = lax.all_gather(w_out, "row", axis=1, tiled=True)
    wu = lax.all_gather(w_up, "row", axis=0, tiled=True)
    wd = lax.all_gather(w_down, "row", axis=1, tiled=True)

    x = to_own(inputs).astype(jnp.float32)
    dy_low = to_own(cotangent)
    dy = dy_low.astype(jnp.float32)
    centred1, inverse1, low1 = norm(x, gain1, bias1)
    all1 = col_gather(low1)
    q = (dot(all1, wq[0], NN) + qv_bias[0]).astype(LOW)
    k = dot(all1, wq[1], NN).astype(LOW)
    v = (dot(all1, wq[2], NN) + qv_bias[1]).astype(LOW)
    other = partner_swap(jnp.concatenate([k, v], 1))

    def in_place(mine, theirs):
        first = jnp.where(half == 0, mine, theirs).reshape(8, 1, OWN, 256)
        second = jnp.where(half == 0, theirs, mine).reshape(8, 1, OWN, 256)
        return jnp.concatenate([first, second], 1).reshape(2048, 256)

    k_all, v_all = in_place(k, other[:, :256]), in_place(v, other[:, 256:])
    att, lse = attend(meta, q, k_all, v_all)
    mid = x + col_reduce(dot(att, wo, NN)) + bias_out
    centred2, inverse2, low2 = norm(mid, gain2, bias2)
    all2 = col_gather(low2)
    hidden = dot(all2, wu, NN) + up_bias
    act = jax.nn.gelu(hidden, approximate=False).astype(LOW)
    second = col_reduce(dot(act, wd, NN)) + bias_down
    mixed = from_own((mid + second).astype(LOW))

    all_dy = col_gather(dy_low)
    g_down = total_grad(dot(act, all_dy, TN), 1)
    dact = dot(all_dy, wd, NT)
    _, pull = jax.vjp(lambda inner: jax.nn.gelu(inner, approximate=False), hidden)
    dhidden = pull(dact)[0].astype(LOW)
    g_up = total_grad(dot(all2, dhidden, TN), 0)
    dlow2 = col_reduce(dot(dhidden, wu, NT))
    dmid = dy + norm_back(dlow2, centred2, inverse2, gain2)
    dbranch = dmid.astype(LOW)
    all_db = col_gather(dbranch)
    g_out = total_grad(dot(att, all_db, TN), 1)
    datt = dot(all_db, wo, NT).astype(LOW)
    dq, dk, dv = attend_back(meta, q, k_all, v_all, datt, lse)
    dkv = jnp.concatenate([dk, dv], 1).reshape(8, 2, OWN, 512)
    mine = jnp.where(half == 0, dkv[:, 0], dkv[:, 1]).reshape(1024, 512)
    theirs = jnp.where(half == 0, dkv[:, 1], dkv[:, 0]).reshape(1024, 512)
    dkv = mine + partner_swap(theirs.astype(LOW)).astype(jnp.float32)
    dqkv = jnp.concatenate([dq, dkv.astype(LOW)], 1)
    g_qkv = total_grad(
        jnp.stack([dot(all1, dqkv[:, i * 256 : (i + 1) * 256], TN) for i in range(3)]), 1
    )
    dlow1 = col_reduce(
        dot(dqkv[:, :256], wq[0], NT) + dot(dqkv[:, 256:512], wq[1], NT) + dot(dqkv[:, 512:], wq[2], NT)
    )
    input_grad = from_own(dmid + norm_back(dlow1, centred1, inverse1, gain1))

    wide = jnp.stack(
        [
            jnp.sum(dlow1 * centred1, 0),
            jnp.sum(dlow1, 0),
            jnp.sum(dbranch.astype(jnp.float32), 0),
            jnp.sum(dlow2 * centred2, 0),
            jnp.sum(dlow2, 0),
            jnp.sum(dy, 0),
        ]
    )
    wide = lax.psum(wide, ("dp", "row", "col"))
    wide = lax.dynamic_slice_in_dim(wide, row * 256, 256, 1)
    lone = jnp.concatenate(
        [
            jnp.sum(dqkv[:, :256].astype(jnp.float32), 0),
            jnp.sum(dqkv[:, 512:].astype(jnp.float32), 0),
            jnp.sum(dhidden.astype(jnp.float32), 0),
        ]
    )
    lone = lax.psum(lone, ("dp", "row"))
    return (
        mixed,
        input_grad,
        wide[0],
        wide[1],
        g_qkv,
        lone[:512].reshape(2, 256),
        g_out,
        wide[2],
        wide[3],
        wide[4],
        g_up,
        lone[512:],
        g_down,
        wide[5],
    )


def solution(mesh):
    tokens = P(None, "dp", "col", "row")
    in_specs = (
        tokens,
        P(None, "dp"),
        P("row"),
        P("row"),
        P(None, "row", "col"),
        P(None, "col"),
        P("col", "row"),
        P("row"),
        P("row"),
        P("row"),
        P("row", "col"),
        P("col"),
        P("col", "row"),
        P("row"),
        tokens,
    )
    out_specs = (
        tokens,
        tokens,
        P("row"),
        P("row"),
        P(None, "row", "col"),
        P(None, "col"),
        P("col", "row"),
        P("row"),
        P("row"),
        P("row"),
        P("row", "col"),
        P("col"),
        P("col", "row"),
        P("row"),
    )
    return jax.shard_map(shards, mesh=mesh, in_specs=in_specs, out_specs=out_specs, check_vma=False)
```

```python
import functools

import jax
import jax.numpy as jnp
from jax import lax
from jax.experimental import pallas as pl
from jax.experimental.pallas import tpu as pltpu
from jax.sharding import PartitionSpec as P

D = 2048
HEAD = 128
SCALE = HEAD**-0.5
EPSILON = 1e-05
HUGE = 1e30
LOW = jnp.bfloat16
OWN = 128
VMEM_LIMIT = 56 * 2**20


def dot(a, b, contract):
    return lax.dot_general(a, b, ((contract[0], contract[1]), ((), ())), preferred_element_type=jnp.float32)


NN = ((1,), (0,))
NT = ((1,), (1,))
TN = ((0,), (0,))


def place_rows(group, half):
    row = lax.broadcasted_iota(jnp.int32, (256, 1), 0)
    return (2 * group + row // OWN) * 256 + half * OWN + row % OWN


def allowed_keys(group, extent, half, length):
    slot = lax.broadcasted_iota(jnp.int32, (256, extent), 1)
    return (slot <= place_rows(group, half)) & (slot < length)


def attend_kernel(meta_ref, q_ref, k_ref, v_ref, o_ref, lse_ref):
    half, length = meta_ref[0], meta_ref[1]
    for head in range(2):
        cols = pl.ds(head * HEAD, HEAD)
        for group in range(4):
            rows, extent = pl.ds(group * 256, 256), 512 * (group + 1)
            scores = dot(q_ref[rows, cols], k_ref[:extent, cols], NT) * SCALE
            allowed = allowed_keys(group, extent, half, length)
            scores = jnp.where(allowed, scores, -HUGE)
            highest = jnp.max(scores, -1, keepdims=True)
            weights = jnp.exp(scores - highest)
            total = jnp.sum(weights, -1, keepdims=True)
            out = dot(weights.astype(LOW), v_ref[:extent, cols], NN) / total
            o_ref[rows, cols] = out.astype(LOW)
            lse_ref[head, rows, :] = highest + jnp.log(total)


def attend(meta, q, k, v):
    vm = pl.BlockSpec(memory_space=pltpu.VMEM)
    return pl.pallas_call(
        attend_kernel,
        out_shape=(
            jax.ShapeDtypeStruct((1024, 256), LOW),
            jax.ShapeDtypeStruct((2, 1024, 1), jnp.float32),
        ),
        in_specs=[pl.BlockSpec(memory_space=pltpu.SMEM), vm, vm, vm],
        out_specs=(vm, vm),
        compiler_params=pltpu.CompilerParams(vmem_limit_bytes=VMEM_LIMIT),
        cost_estimate=pl.CostEstimate(flops=4 * 10**9, bytes_accessed=4 * 10**6, transcendentals=2 * 10**6),
    )(meta, q, k, v)


def attend_back_kernel(meta_ref, q_ref, k_ref, v_ref, do_ref, lse_ref, dq_ref, dk_ref, dv_ref):
    half, length = meta_ref[0], meta_ref[1]
    for head in range(2):
        cols = pl.ds(head * HEAD, HEAD)
        for group in reversed(range(4)):
            rows, extent = pl.ds(group * 256, 256), 512 * (group + 1)
            q, k, v, do = q_ref[rows, cols], k_ref[:extent, cols], v_ref[:extent, cols], do_ref[rows, cols]
            scores = dot(q, k, NT) * SCALE
            allowed = allowed_keys(group, extent, half, length)
            probs = jnp.exp(jnp.where(allowed, scores, -HUGE) - lse_ref[head, rows, :])
            dprobs = dot(do, v, NT)
            weighted = probs * dprobs
            delta = jnp.sum(weighted, -1, keepdims=True)
            dscores = (weighted - probs * delta).astype(LOW)
            dq_ref[rows, cols] = (dot(dscores, k, NN) * SCALE).astype(LOW)
            dk = dot(dscores, q, TN) * SCALE
            dv = dot(probs.astype(LOW), do, TN)
            if group == 3:
                dk_ref[:, cols] = dk
                dv_ref[:, cols] = dv
            else:
                dk_ref[:extent, cols] += dk
                dv_ref[:extent, cols] += dv


def attend_back(meta, q, k, v, do, lse):
    vm = pl.BlockSpec(memory_space=pltpu.VMEM)
    return pl.pallas_call(
        attend_back_kernel,
        out_shape=(
            jax.ShapeDtypeStruct((1024, 256), LOW),
            jax.ShapeDtypeStruct((2048, 256), jnp.float32),
            jax.ShapeDtypeStruct((2048, 256), jnp.float32),
        ),
        in_specs=[pl.BlockSpec(memory_space=pltpu.SMEM), vm, vm, vm, vm, vm],
        out_specs=(vm, vm, vm),
        compiler_params=pltpu.CompilerParams(vmem_limit_bytes=VMEM_LIMIT),
        cost_estimate=pl.CostEstimate(flops=10 * 10**9, bytes_accessed=8 * 10**6, transcendentals=2 * 10**6),
    )(meta, q, k, v, do, lse)


MESH = pl.DeviceIdType.MESH
HBM = pl.BlockSpec(memory_space=pl.ANY)
VM = pl.BlockSpec(memory_space=pltpu.VMEM)
SM = pl.BlockSpec(memory_space=pltpu.SMEM)


def part(start, size):
    return pl.ds(pl.multiple_of(start, size), size)


class Net:
    def __init__(self, send, recv, local):
        self.send, self.recv, self.local = send, recv, local
        self.used, self.local_used, self.live, self.own = 0, 0, [], []
        self.dp, self.row, self.col = (lax.axis_index(a) for a in ("dp", "row", "col"))
        self.half, self.y = self.row // 4, self.row % 4
        self.x = self.dp * 2 + self.half
        self.z, self.core = self.col // 2, self.col % 2

    def at(self, dx=0, dy=0, dz=0, other_core=False):
        x, y, z = (self.x + dx) % 4, (self.y + dy) % 4, (self.z + dz) % 4
        core = 1 - self.core if other_core else self.core
        return {"dp": x // 2, "row": (x % 2) * 4 + y, "col": z * 2 + core}

    def mate(self, shift):
        return {"dp": self.dp, "row": (self.row + shift) % 8, "col": self.col}

    def partner(self):
        return self.mate(4)

    def greet(self, more=()):
        devices = [self.mate(d) for d in range(1, 8)]
        devices += [{"dp": 1 - self.dp, "row": (self.row + 4) % 8, "col": self.col}]
        devices += [self.at(dz=1), self.at(dz=3), self.at(other_core=True), *more]
        barrier = pltpu.get_barrier_semaphore()
        for device in devices:
            pl.semaphore_signal(barrier, inc=1, device_id=device, device_id_type=MESH)
        pl.semaphore_wait(barrier, len(devices))

    def slots(self, count):
        self.used += count
        return self.used - count

    def _copy(self, slot, src, dst, device):
        return pltpu.make_async_remote_copy(
            src_ref=src,
            dst_ref=dst,
            send_sem=self.send.at[slot],
            recv_sem=self.recv.at[slot],
            device_id=device,
            device_id_type=MESH,
        )

    def push(self, slot, src, dst, device):
        copy = self._copy(slot, src, dst, device)
        copy.start()
        self.live.append(copy)

    def got(self, slot, ref):
        self._copy(slot, ref, ref, self.at(other_core=True)).wait_recv()

    def move(self, src, dst):
        copy = pltpu.make_async_copy(src, dst, self.local.at[self.local_used])
        self.local_used += 1
        copy.start()
        return copy

    def store(self, src, dst):
        self.own.append(self.move(src, dst))

    def drain(self):
        for copy in self.live:
            copy.wait_send()
        for copy in self.own:
            copy.wait()


class ColGather:
    def __init__(self, net, buf):
        self.net, self.buf, self.slot = net, buf, net.slots(14)

    def rows(self, dz, other_core, piece):
        net = self.net
        core = 1 - net.core if other_core else net.core
        return self.buf.at[part(((net.z + dz) % 4 * 2 + core) * OWN + 64 * piece, 64)]

    def move(self, slot, where, piece, **to):
        ref = self.rows(where, False, piece)
        self.net.push(self.slot + slot, ref, ref, self.net.at(**to))

    def got(self, slot, dz, piece, other_core=False):
        self.net.got(self.slot + slot, self.rows(dz, other_core, piece))

    def begin(self):
        self.move(0, 0, 0, dz=1)
        self.move(3, 0, 1, dz=3)
        self.move(1, 0, 1, dz=1)
        self.move(2, 0, 0, dz=3)
        self.move(6, 0, 0, other_core=True)
        self.move(7, 0, 1, other_core=True)

    def hop(self):
        self.got(0, 3, 0)
        self.move(4, 3, 0, dz=1)
        self.got(3, 1, 1)
        self.move(5, 1, 1, dz=3)
        self.move(8, 3, 0, other_core=True)
        self.move(11, 1, 1, other_core=True)
        self.got(1, 3, 1)
        self.move(9, 3, 1, other_core=True)
        self.got(2, 1, 0)
        self.move(10, 1, 0, other_core=True)

    def far(self):
        self.got(4, 2, 0)
        self.move(12, 2, 0, other_core=True)
        self.got(5, 2, 1)
        self.move(13, 2, 1, other_core=True)

    def pair(self, dz):
        slot = {0: 6, 3: 8, 1: 10, 2: 12}[dz]
        self.got(slot, dz, 0, True)
        self.got(slot + 1, dz, 1, True)


class RowGather:
    def __init__(self, net, src, buf, whole, halves):
        self.net, self.src, self.buf, self.whole, self.halves = net, src, buf, whole, halves
        self.slot = net.slots(11)

    def place(self, dy, other=False):
        net = self.net
        half = 1 - net.half if other else net.half
        return self.whole(self.buf, half * 4 + (net.y + dy) % 4)

    def sideways(self, dy, src):
        net, there = self.net, self.place(dy)
        for side, dx in enumerate((1, 3)):
            net.push(self.slot + 3 + dy * 2 + side, self.halves(src, side), self.halves(there, side), net.at(dx=dx))

    def begin(self):
        net, mine = self.net, self.place(0)
        for dy in (1, 3, 2):
            net.push(self.slot + dy - 1, self.src, mine, net.at(dy=dy))
        self.sideways(0, self.src)
        self.copy = net.move(self.src, mine)

    def step(self, dy):
        ref = self.place(4 - dy)
        self.net.got(self.slot + dy - 1, ref)
        self.sideways(4 - dy, ref)

    def steps(self):
        for dy in (1, 3, 2):
            self.step(dy)

    def finish(self):
        self.copy.wait()
        for dy in range(4):
            for side in range(2):
                self.net.got(self.slot + 3 + dy * 2 + side, self.halves(self.place(dy, True), side))


class Swap:
    def __init__(self, net, src_of, dst_of):
        self.net, self.src_of, self.dst_of, self.slot = net, src_of, dst_of, net.slots(7)

    def begin(self):
        net = self.net
        for shift in range(1, 8):
            net.push(self.slot + shift - 1, self.src_of((net.row + shift) % 8), self.dst_of(net.row), net.mate(shift))
        self.copy = net.move(self.src_of(net.row), self.dst_of(net.row))

    def finish(self):
        net = self.net
        self.copy.wait()
        for shift in range(1, 8):
            net.got(self.slot + shift - 1, self.dst_of((net.row + 8 - shift) % 8))


def norm_rows(values, gain, bias):
    middle = jnp.mean(values, -1, keepdims=True)
    spread = jnp.mean(values * values, -1, keepdims=True) - middle * middle
    inverse = lax.rsqrt(spread + EPSILON)
    centred = (values - middle) * inverse
    return centred * gain + bias


def attend_group(q, kv, head, group, half, length):
    cols, rows, extent = pl.ds(head * HEAD, HEAD), pl.ds(group * 256, 256), 512 * (group + 1)
    scores = dot(q[rows, cols], kv[0, :extent, cols], NT) * SCALE
    scores = jnp.where(allowed_keys(group, extent, half, length), scores, -HUGE)
    highest = jnp.max(scores, -1, keepdims=True)
    weights = jnp.exp(scores - highest)
    total = jnp.sum(weights, -1, keepdims=True)
    out = dot(weights.astype(LOW), kv[1, :extent, cols], NN) / total
    return out, highest + jnp.log(total)


def first_kernel(
    meta, inputs, cotangent, small, w_qkv, w_out, qv_bias,
    x_out, dy_out, n1_out, q_out, kv_out, att_out, lse, wq_out, wo_out, small_out,
    x, dy, n1, q, kv, att, wq, wo, wide, send, recv, local,
):
    net = Net(send, recv, local)
    net.greet()
    mine = part(net.col * OWN, OWN)

    def token_block(ref):
        return lambda r: ref.at[(r // 2) % 2, r % 2, part(r // 4 * OWN, OWN)]

    def feature_block(ref):
        return lambda r: ref.at[:, part(r * 256, 256)]

    params = Swap(net, lambda r: small, feature_block(wide))
    tokens = Swap(net, token_block(inputs), feature_block(x))
    upstream = Swap(net, token_block(cotangent), lambda r: dy.at[mine, part(r * 256, 256)])
    gather_wq = RowGather(
        net, w_qkv, wq, lambda ref, r: ref.at[:, part(r * 256, 256)], lambda ref, h: ref.at[:, pl.ds(h * 128, 128)]
    )
    gather_wo = RowGather(
        net, w_out, wo, lambda ref, r: ref.at[:, part(r * 256, 256)], lambda ref, h: ref.at[pl.ds(h * 128, 128)]
    )
    all_n1, all_dy = ColGather(net, n1), ColGather(net, dy)
    keys = net.slots(8)

    params.begin()
    tokens.begin()
    gather_wq.begin()
    upstream.begin()
    params.finish()
    tokens.finish()
    for piece in range(4):
        rows = pl.ds(piece * 32, 32)
        low = norm_rows(x[rows, :].astype(jnp.float32), wide[0:1, :], wide[1:2, :]).astype(LOW)
        n1[part(net.col * OWN + piece * 32, 32), :] = low
    all_n1.begin()
    gather_wq.steps()
    gather_wo.begin()
    upstream.finish()
    all_n1.hop()
    all_dy.begin()
    gather_wq.finish()
    for dz in (0, 3, 1, 2):
        if dz == 2:
            all_n1.far()
        all_n1.pair(dz)
        block = (net.z + dz) % 4
        rows = part(block * 256, 256)
        values = n1[rows, :]
        k = dot(values, wq[1], NN).astype(LOW)
        v = (dot(values, wq[2], NN) + qv_bias[1:2, :]).astype(LOW)
        for i in range(2):
            there = part((block * 2 + i) * 256 + net.half * OWN, OWN)
            kv[0, there, :] = k[i * OWN : (i + 1) * OWN]
            kv[1, there, :] = v[i * OWN : (i + 1) * OWN]
            ref = kv.at[:, there]
            net.push(keys + dz * 2 + i, ref, ref, net.partner())
        q[rows, :] = (dot(values, wq[0], NN) + qv_bias[0:1, :]).astype(LOW)
    net.store(n1, n1_out)
    net.store(wq, wq_out)
    net.store(q, q_out)
    net.store(x, x_out)
    net.store(wide, small_out)
    gather_wo.steps()
    all_dy.hop()
    for dz in (0, 3, 1, 2):
        for i in range(2):
            block = (net.z + dz) % 4 * 2 + i
            net.got(keys + dz * 2 + i, kv.at[:, part(block * 256 + (1 - net.half) * OWN, OWN)])
    net.store(kv, kv_out)
    for head in range(2):
        for group in range(4):
            out, logsum = attend_group(q, kv, head, group, net.half, meta[0])
            rows = pl.ds(group * 256, 256)
            att[rows, pl.ds(head * HEAD, HEAD)] = out.astype(LOW)
            lse[head, rows, :] = logsum
        if head == 0:
            all_dy.far()
            gather_wo.finish()
            net.store(wo, wo_out)
    net.store(att, att_out)
    for dz in range(4):
        all_dy.pair(dz)
    net.store(dy, dy_out)
    net.drain()


def low_shape(*shape):
    return jax.ShapeDtypeStruct(shape, LOW)


def full_shape(*shape):
    return jax.ShapeDtypeStruct(shape, jnp.float32)


def sems(remote, local):
    return [
        pltpu.SemaphoreType.DMA((remote,)),
        pltpu.SemaphoreType.DMA((remote,)),
        pltpu.SemaphoreType.DMA((local,)),
    ]


def first(meta, inputs, cotangent, small, w_qkv, w_out, qv_bias):
    return pl.pallas_call(
        first_kernel,
        out_shape=(
            low_shape(OWN, D),
            low_shape(1024, D),
            low_shape(1024, D),
            low_shape(1024, 256),
            low_shape(2, 2048, 256),
            low_shape(1024, 256),
            full_shape(2, 1024, 1),
            low_shape(3, D, 256),
            low_shape(256, D),
            full_shape(8, D),
        ),
        in_specs=[SM, HBM, HBM, HBM, HBM, HBM, VM],
        out_specs=(HBM, HBM, HBM, HBM, HBM, HBM, VM, HBM, HBM, HBM),
        scratch_shapes=[
            pltpu.VMEM((OWN, D), LOW),
            pltpu.VMEM((1024, D), LOW),
            pltpu.VMEM((1024, D), LOW),
            pltpu.VMEM((1024, 256), LOW),
            pltpu.VMEM((2, 2048, 256), LOW),
            pltpu.VMEM((1024, 256), LOW),
            pltpu.VMEM((3, D, 256), LOW),
            pltpu.VMEM((256, D), LOW),
            pltpu.VMEM((8, D), jnp.float32),
            *sems(96, 24),
        ],
        compiler_params=pltpu.CompilerParams(
            collective_id=1, has_side_effects=True, vmem_limit_bytes=VMEM_LIMIT
        ),
        cost_estimate=pl.CostEstimate(flops=40 * 10**9, bytes_accessed=30 * 10**6, transcendentals=2 * 10**6),
    )(meta, inputs, cotangent, small, w_qkv, w_out, qv_bias)


def to_own(a):
    sent = a.reshape(2, 2, 2, OWN, 256).transpose(2, 0, 1, 3, 4).reshape(8, OWN, 256)
    got = lax.all_to_all(sent, "row", 0, 0, tiled=True)
    return got.transpose(1, 0, 2).reshape(OWN, D)


def from_own(a):
    sent = a.reshape(OWN, 8, 256).transpose(1, 0, 2)
    got = lax.all_to_all(sent, "row", 0, 0, tiled=True)
    return got.reshape(2, 2, 2, OWN, 256).transpose(1, 2, 0, 3, 4).reshape(2, 2, 256, 256)


def norm(values, gain, bias):
    middle = jnp.mean(values, -1, keepdims=True)
    spread = jnp.mean(values * values, -1, keepdims=True) - middle * middle
    inverse = lax.rsqrt(spread + EPSILON)
    centred = (values - middle) * inverse
    return centred, inverse, (centred * gain + bias).astype(LOW)


def norm_back(grad, centred, inverse, gain):
    scaled = grad * gain
    return inverse * (
        scaled - jnp.mean(scaled, -1, keepdims=True) - centred * jnp.mean(scaled * centred, -1, keepdims=True)
    )


def col_gather(a):
    return lax.all_gather(a, "col", axis=0, tiled=True)


def col_reduce(a):
    return lax.psum_scatter(a.astype(LOW), "col", scatter_dimension=0, tiled=True).astype(jnp.float32)


def partner_swap(a):
    return lax.ppermute(a, "row", [(i, (i + 4) % 8) for i in range(8)])


def total_grad(a, axis):
    part = lax.psum_scatter(a.astype(LOW), "row", scatter_dimension=axis, tiled=True)
    other = lax.ppermute(part, "dp", [(0, 1), (1, 0)])
    return part.astype(jnp.float32) + other.astype(jnp.float32)


def shards(
    inputs,
    lengths,
    ln1_gain,
    ln1_bias,
    w_qkv,
    qv_bias,
    w_out,
    out_bias,
    ln2_gain,
    ln2_bias,
    w_up,
    up_bias,
    w_down,
    down_bias,
    cotangent,
):
    row = lax.axis_index("row")
    half, micro, seq = row // 4, (row // 2) % 2, row % 2
    length = lengths[micro, seq].reshape(1)
    meta = jnp.stack([half, lengths[micro, seq]]).astype(jnp.int32)
    zero = jnp.zeros_like(ln1_gain)
    small = jnp.stack([ln1_gain, ln1_bias, out_bias, ln2_gain, ln2_bias, down_bias, zero, zero])
    x, all_dy, all1, q, kv, att, lse, wq, wo, wide = first(length, inputs, cotangent, small, w_qkv, w_out, qv_bias)
    gain1, bias1, bias_out, gain2, bias2, bias_down = [wide[i] for i in range(6)]
    wu = lax.all_gather(w_up, "row", axis=0, tiled=True)
    wd = lax.all_gather(w_down, "row", axis=1, tiled=True)
    x = x.astype(jnp.float32)
    dy = lax.dynamic_slice_in_dim(all_dy, lax.axis_index("col") * OWN, OWN, 0).astype(jnp.float32)
    centred1, inverse1, _ = norm(x, gain1, bias1)
    k_all, v_all = kv[0], kv[1]
    mid = x + col_reduce(dot(att, wo, NN)) + bias_out
    centred2, inverse2, low2 = norm(mid, gain2, bias2)
    all2 = col_gather(low2)
    hidden = dot(all2, wu, NN) + up_bias
    act = jax.nn.gelu(hidden, approximate=False).astype(LOW)
    second = col_reduce(dot(act, wd, NN)) + bias_down
    mixed = from_own((mid + second).astype(LOW))

    g_down = total_grad(dot(act, all_dy, TN), 1)
    dact = dot(all_dy, wd, NT)
    _, pull = jax.vjp(lambda inner: jax.nn.gelu(inner, approximate=False), hidden)
    dhidden = pull(dact)[0].astype(LOW)
    g_up = total_grad(dot(all2, dhidden, TN), 0)
    dlow2 = col_reduce(dot(dhidden, wu, NT))
    dmid = dy + norm_back(dlow2, centred2, inverse2, gain2)
    dbranch = dmid.astype(LOW)
    all_db = col_gather(dbranch)
    g_out = total_grad(dot(att, all_db, TN), 1)
    datt = dot(all_db, wo, NT).astype(LOW)
    dq, dk, dv = attend_back(meta, q, k_all, v_all, datt, lse)
    dkv = jnp.concatenate([dk, dv], 1).reshape(8, 2, OWN, 512)
    mine = jnp.where(half == 0, dkv[:, 0], dkv[:, 1]).reshape(1024, 512)
    theirs = jnp.where(half == 0, dkv[:, 1], dkv[:, 0]).reshape(1024, 512)
    dkv = mine + partner_swap(theirs.astype(LOW)).astype(jnp.float32)
    dqkv = jnp.concatenate([dq, dkv.astype(LOW)], 1)
    g_qkv = total_grad(
        jnp.stack([dot(all1, dqkv[:, i * 256 : (i + 1) * 256], TN) for i in range(3)]), 1
    )
    dlow1 = col_reduce(
        dot(dqkv[:, :256], wq[0], NT) + dot(dqkv[:, 256:512], wq[1], NT) + dot(dqkv[:, 512:], wq[2], NT)
    )
    input_grad = from_own(dmid + norm_back(dlow1, centred1, inverse1, gain1))

    wide = jnp.stack(
        [
            jnp.sum(dlow1 * centred1, 0),
            jnp.sum(dlow1, 0),
            jnp.sum(dbranch.astype(jnp.float32), 0),
            jnp.sum(dlow2 * centred2, 0),
            jnp.sum(dlow2, 0),
            jnp.sum(dy, 0),
        ]
    )
    wide = lax.psum(wide, ("dp", "row", "col"))
    wide = lax.dynamic_slice_in_dim(wide, row * 256, 256, 1)
    lone = jnp.concatenate(
        [
            jnp.sum(dqkv[:, :256].astype(jnp.float32), 0),
            jnp.sum(dqkv[:, 512:].astype(jnp.float32), 0),
            jnp.sum(dhidden.astype(jnp.float32), 0),
        ]
    )
    lone = lax.psum(lone, ("dp", "row"))
    return (
        mixed,
        input_grad,
        wide[0],
        wide[1],
        g_qkv,
        lone[:512].reshape(2, 256),
        g_out,
        wide[2],
        wide[3],
        wide[4],
        g_up,
        lone[512:],
        g_down,
        wide[5],
    )


def solution(mesh):
    tokens = P(None, "dp", "col", "row")
    in_specs = (
        tokens,
        P(None, "dp"),
        P("row"),
        P("row"),
        P(None, "row", "col"),
        P(None, "col"),
        P("col", "row"),
        P("row"),
        P("row"),
        P("row"),
        P("row", "col"),
        P("col"),
        P("col", "row"),
        P("row"),
        tokens,
    )
    out_specs = (
        tokens,
        tokens,
        P("row"),
        P("row"),
        P(None, "row", "col"),
        P(None, "col"),
        P("col", "row"),
        P("row"),
        P("row"),
        P("row"),
        P("row", "col"),
        P("col"),
        P("col", "row"),
        P("row"),
    )
    return jax.shard_map(shards, mesh=mesh, in_specs=in_specs, out_specs=out_specs, check_vma=False)
```

```python
import functools

import jax
import jax.numpy as jnp
from jax import lax
from jax.experimental import pallas as pl
from jax.experimental.pallas import tpu as pltpu
from jax.sharding import PartitionSpec as P

D = 2048
HEAD = 128
SCALE = HEAD**-0.5
EPSILON = 1e-05
HUGE = 1e30
LOW = jnp.bfloat16
OWN = 128
VMEM_LIMIT = 56 * 2**20


def dot(a, b, contract):
    return lax.dot_general(a, b, ((contract[0], contract[1]), ((), ())), preferred_element_type=jnp.float32)


NN = ((1,), (0,))
NT = ((1,), (1,))
TN = ((0,), (0,))


def place_rows(group, half):
    row = lax.broadcasted_iota(jnp.int32, (256, 1), 0)
    return (2 * group + row // OWN) * 256 + half * OWN + row % OWN


def allowed_keys(group, extent, half, length):
    slot = lax.broadcasted_iota(jnp.int32, (256, extent), 1)
    return (slot <= place_rows(group, half)) & (slot < length)


MESH = pl.DeviceIdType.MESH
HBM = pl.BlockSpec(memory_space=pl.ANY)
VM = pl.BlockSpec(memory_space=pltpu.VMEM)
SM = pl.BlockSpec(memory_space=pltpu.SMEM)


def part(start, size):
    return pl.ds(pl.multiple_of(start, size), size)


class Net:
    def __init__(self, send, recv, local):
        self.send, self.recv, self.local = send, recv, local
        self.used, self.local_used, self.live, self.own = 0, 0, [], []
        self.dp, self.row, self.col = (lax.axis_index(a) for a in ("dp", "row", "col"))
        self.half, self.y = self.row // 4, self.row % 4
        self.x = self.dp * 2 + self.half
        self.z, self.core = self.col // 2, self.col % 2

    def at(self, dx=0, dy=0, dz=0, other_core=False):
        x, y, z = (self.x + dx) % 4, (self.y + dy) % 4, (self.z + dz) % 4
        core = 1 - self.core if other_core else self.core
        return {"dp": x // 2, "row": (x % 2) * 4 + y, "col": z * 2 + core}

    def mate(self, shift):
        return {"dp": self.dp, "row": (self.row + shift) % 8, "col": self.col}

    def partner(self):
        return self.mate(4)

    def greet(self, more=(), cols=()):
        devices = [self.mate(d) for d in range(1, 8)]
        devices += [{"dp": 1 - self.dp, "row": (self.row + 4) % 8, "col": self.col}]
        devices += cols or [self.at(dz=1), self.at(dz=3), self.at(other_core=True)]
        devices += more
        barrier = pltpu.get_barrier_semaphore()
        for device in devices:
            pl.semaphore_signal(barrier, inc=1, device_id=device, device_id_type=MESH)
        pl.semaphore_wait(barrier, len(devices))

    def slots(self, count):
        self.used += count
        return self.used - count

    def _copy(self, slot, src, dst, device):
        return pltpu.make_async_remote_copy(
            src_ref=src,
            dst_ref=dst,
            send_sem=self.send.at[slot],
            recv_sem=self.recv.at[slot],
            device_id=device,
            device_id_type=MESH,
        )

    def push(self, slot, src, dst, device):
        copy = self._copy(slot, src, dst, device)
        copy.start()
        self.live.append(copy)

    def got(self, slot, ref):
        self._copy(slot, ref, ref, self.at(other_core=True)).wait_recv()

    def move(self, src, dst):
        copy = pltpu.make_async_copy(src, dst, self.local.at[self.local_used])
        self.local_used += 1
        copy.start()
        return copy

    def store(self, src, dst):
        self.own.append(self.move(src, dst))

    def drain(self):
        for copy in self.live:
            copy.wait_send()
        for copy in self.own:
            copy.wait()


class ColGather:
    def __init__(self, net, buf):
        self.net, self.buf, self.slot = net, buf, net.slots(14)

    def rows(self, dz, other_core, piece):
        net = self.net
        core = 1 - net.core if other_core else net.core
        return self.buf.at[part(((net.z + dz) % 4 * 2 + core) * OWN + 64 * piece, 64)]

    def move(self, slot, where, piece, **to):
        ref = self.rows(where, False, piece)
        self.net.push(self.slot + slot, ref, ref, self.net.at(**to))

    def got(self, slot, dz, piece, other_core=False):
        self.net.got(self.slot + slot, self.rows(dz, other_core, piece))

    def begin(self):
        self.move(0, 0, 0, dz=1)
        self.move(3, 0, 1, dz=3)
        self.move(1, 0, 1, dz=1)
        self.move(2, 0, 0, dz=3)
        self.move(6, 0, 0, other_core=True)
        self.move(7, 0, 1, other_core=True)

    def hop(self):
        self.got(0, 3, 0)
        self.move(4, 3, 0, dz=1)
        self.got(3, 1, 1)
        self.move(5, 1, 1, dz=3)
        self.move(8, 3, 0, other_core=True)
        self.move(11, 1, 1, other_core=True)
        self.got(1, 3, 1)
        self.move(9, 3, 1, other_core=True)
        self.got(2, 1, 0)
        self.move(10, 1, 0, other_core=True)

    def far(self):
        self.got(4, 2, 0)
        self.move(12, 2, 0, other_core=True)
        self.got(5, 2, 1)
        self.move(13, 2, 1, other_core=True)

    def pair(self, dz):
        slot = {0: 6, 3: 8, 1: 10, 2: 12}[dz]
        self.got(slot, dz, 0, True)
        self.got(slot + 1, dz, 1, True)


class RowGather:
    def __init__(self, net, src, buf, whole, halves):
        self.net, self.src, self.buf, self.whole, self.halves = net, src, buf, whole, halves
        self.slot = net.slots(11)

    def place(self, dy, other=False):
        net = self.net
        half = 1 - net.half if other else net.half
        return self.whole(self.buf, half * 4 + (net.y + dy) % 4)

    def sideways(self, dy, src):
        net, there = self.net, self.place(dy)
        for side, dx in enumerate((1, 3)):
            net.push(self.slot + 3 + dy * 2 + side, self.halves(src, side), self.halves(there, side), net.at(dx=dx))

    def begin(self):
        net, mine = self.net, self.place(0)
        for dy in (1, 3, 2):
            net.push(self.slot + dy - 1, self.src, mine, net.at(dy=dy))
        self.sideways(0, self.src)
        self.copy = net.move(self.src, mine)

    def step(self, dy):
        ref = self.place(4 - dy)
        self.net.got(self.slot + dy - 1, ref)
        self.sideways(4 - dy, ref)

    def steps(self):
        for dy in (1, 3, 2):
            self.step(dy)

    def finish(self):
        self.copy.wait()
        for dy in range(4):
            for side in range(2):
                self.net.got(self.slot + 3 + dy * 2 + side, self.halves(self.place(dy, True), side))


class Swap:
    def __init__(self, net, src_of, dst_of):
        self.net, self.src_of, self.dst_of, self.slot = net, src_of, dst_of, net.slots(7)

    def begin(self):
        net = self.net
        for shift in range(1, 8):
            net.push(self.slot + shift - 1, self.src_of((net.row + shift) % 8), self.dst_of(net.row), net.mate(shift))
        self.copy = net.move(self.src_of(net.row), self.dst_of(net.row))

    def finish(self):
        net = self.net
        self.copy.wait()
        for shift in range(1, 8):
            net.got(self.slot + shift - 1, self.dst_of((net.row + 8 - shift) % 8))


def norm_rows(values, gain, bias):
    middle = jnp.mean(values, -1, keepdims=True)
    spread = jnp.mean(values * values, -1, keepdims=True) - middle * middle
    inverse = lax.rsqrt(spread + EPSILON)
    centred = (values - middle) * inverse
    return centred * gain + bias


def attend_group(q, kv, head, group, half, length):
    cols, rows, extent = pl.ds(head * HEAD, HEAD), pl.ds(group * 256, 256), 512 * (group + 1)
    scores = dot(q[rows, cols], kv[0, :extent, cols], NT) * SCALE
    scores = jnp.where(allowed_keys(group, extent, half, length), scores, -HUGE)
    highest = jnp.max(scores, -1, keepdims=True)
    weights = jnp.exp(scores - highest)
    total = jnp.sum(weights, -1, keepdims=True)
    out = dot(weights.astype(LOW), kv[1, :extent, cols], NN) / total
    return out, highest + jnp.log(total)


def first_kernel(
    meta, inputs, cotangent, small, w_qkv, w_out, qv_bias,
    x_out, dy_out, n1_out, q_out, kv_out, att_out, lse, wq_out, wo_out, small_out,
    x, dy, n1, q, kv, att, wq, wo, wide, send, recv, local,
):
    net = Net(send, recv, local)
    net.greet()
    mine = part(net.col * OWN, OWN)

    def token_block(ref):
        return lambda r: ref.at[(r // 2) % 2, r % 2, part(r // 4 * OWN, OWN)]

    def feature_block(ref):
        return lambda r: ref.at[:, part(r * 256, 256)]

    params = Swap(net, lambda r: small, feature_block(wide))
    tokens = Swap(net, token_block(inputs), feature_block(x))
    upstream = Swap(net, token_block(cotangent), lambda r: dy.at[mine, part(r * 256, 256)])
    gather_wq = RowGather(
        net, w_qkv, wq, lambda ref, r: ref.at[:, part(r * 256, 256)], lambda ref, h: ref.at[:, pl.ds(h * 128, 128)]
    )
    gather_wo = RowGather(
        net, w_out, wo, lambda ref, r: ref.at[:, part(r * 256, 256)], lambda ref, h: ref.at[pl.ds(h * 128, 128)]
    )
    all_n1, all_dy = ColGather(net, n1), ColGather(net, dy)
    keys = net.slots(8)

    params.begin()
    tokens.begin()
    gather_wq.begin()
    upstream.begin()
    params.finish()
    tokens.finish()
    for piece in range(4):
        rows = pl.ds(piece * 32, 32)
        low = norm_rows(x[rows, :].astype(jnp.float32), wide[0:1, :], wide[1:2, :]).astype(LOW)
        n1[part(net.col * OWN + piece * 32, 32), :] = low
    all_n1.begin()
    gather_wq.steps()
    gather_wo.begin()
    upstream.finish()
    all_n1.hop()
    all_dy.begin()
    gather_wq.finish()
    for dz in (0, 3, 1, 2):
        if dz == 2:
            all_n1.far()
        all_n1.pair(dz)
        block = (net.z + dz) % 4
        rows = part(block * 256, 256)
        values = n1[rows, :]
        k = dot(values, wq[1], NN).astype(LOW)
        v = (dot(values, wq[2], NN) + qv_bias[1:2, :]).astype(LOW)
        for i in range(2):
            there = part((block * 2 + i) * 256 + net.half * OWN, OWN)
            kv[0, there, :] = k[i * OWN : (i + 1) * OWN]
            kv[1, there, :] = v[i * OWN : (i + 1) * OWN]
            ref = kv.at[:, there]
            net.push(keys + dz * 2 + i, ref, ref, net.partner())
        q[rows, :] = (dot(values, wq[0], NN) + qv_bias[0:1, :]).astype(LOW)
    net.store(n1, n1_out)
    net.store(wq, wq_out)
    net.store(q, q_out)
    net.store(x, x_out)
    net.store(wide, small_out)
    gather_wo.steps()
    all_dy.hop()
    for dz in (0, 3, 1, 2):
        for i in range(2):
            block = (net.z + dz) % 4 * 2 + i
            net.got(keys + dz * 2 + i, kv.at[:, part(block * 256 + (1 - net.half) * OWN, OWN)])
    net.store(kv, kv_out)
    for head in range(2):
        for group in range(4):
            out, logsum = attend_group(q, kv, head, group, net.half, meta[0])
            rows = pl.ds(group * 256, 256)
            att[rows, pl.ds(head * HEAD, HEAD)] = out.astype(LOW)
            lse[head, rows, :] = logsum
        if head == 0:
            all_dy.far()
            gather_wo.finish()
            net.store(wo, wo_out)
    net.store(att, att_out)
    for dz in range(4):
        all_dy.pair(dz)
    net.store(dy, dy_out)
    net.drain()


def low_shape(*shape):
    return jax.ShapeDtypeStruct(shape, LOW)


def full_shape(*shape):
    return jax.ShapeDtypeStruct(shape, jnp.float32)


def sems(remote, local):
    return [
        pltpu.SemaphoreType.DMA((remote,)),
        pltpu.SemaphoreType.DMA((remote,)),
        pltpu.SemaphoreType.DMA((local,)),
    ]


def first(meta, inputs, cotangent, small, w_qkv, w_out, qv_bias):
    return pl.pallas_call(
        first_kernel,
        out_shape=(
            low_shape(OWN, D),
            low_shape(1024, D),
            low_shape(1024, D),
            low_shape(1024, 256),
            low_shape(2, 2048, 256),
            low_shape(1024, 256),
            full_shape(2, 1024, 1),
            low_shape(3, D, 256),
            low_shape(256, D),
            full_shape(8, D),
        ),
        in_specs=[SM, HBM, HBM, HBM, HBM, HBM, VM],
        out_specs=(HBM, HBM, HBM, HBM, HBM, HBM, VM, HBM, HBM, HBM),
        scratch_shapes=[
            pltpu.VMEM((OWN, D), LOW),
            pltpu.VMEM((1024, D), LOW),
            pltpu.VMEM((1024, D), LOW),
            pltpu.VMEM((1024, 256), LOW),
            pltpu.VMEM((2, 2048, 256), LOW),
            pltpu.VMEM((1024, 256), LOW),
            pltpu.VMEM((3, D, 256), LOW),
            pltpu.VMEM((256, D), LOW),
            pltpu.VMEM((8, D), jnp.float32),
            *sems(96, 24),
        ],
        compiler_params=pltpu.CompilerParams(
            collective_id=1, has_side_effects=True, vmem_limit_bytes=VMEM_LIMIT
        ),
        cost_estimate=pl.CostEstimate(flops=40 * 10**9, bytes_accessed=30 * 10**6, transcendentals=2 * 10**6),
    )(meta, inputs, cotangent, small, w_qkv, w_out, qv_bias)


class ColReduce:
    def __init__(self, net, terms, near, left, right, ends):
        self.net, self.terms, self.near, self.left, self.right, self.ends = net, terms, near, left, right, ends
        self.slot = net.slots(10)
        self.sent = []

    def push(self, *copy):
        self.net.push(*copy)
        self.sent.append(self.net.live[-1])

    def flush(self):
        for copy in self.sent:
            copy.wait_send()
        self.net.live = [copy for copy in self.net.live if not any(copy is other for other in self.sent)]

    def block(self, dz, other_core=False):
        net = self.net
        core = 1 - net.core if other_core else net.core
        return part(((net.z + dz) % 4 * 2 + core) * OWN, OWN)

    def rows(self, dz, piece):
        net = self.net
        return part(((net.z + dz) % 4 * 2 + net.core) * OWN + 64 * piece, 64)

    def give(self, dz):
        self.push(
            self.slot + dz, self.terms.at[self.block(dz, True)], self.near.at[pl.ds(dz * OWN, OWN)], self.net.at(other_core=True)
        )

    def fold(self, dz):
        near = self.near.at[pl.ds(dz * OWN, OWN)]
        self.net.got(self.slot + dz, near)
        block = self.block(dz)
        self.terms[block, :] = (self.terms[block, :].astype(jnp.float32) + near[...].astype(jnp.float32)).astype(LOW)

    def send(self, slot, dz, piece, dst, side):
        self.push(self.slot + slot, self.terms.at[self.rows(dz, piece)], dst, self.net.at(dz=side))

    def far(self):
        self.fold(2)
        self.send(4, 2, 0, self.left, 1)
        self.send(5, 2, 1, self.right, 3)

    def beside(self, dz):
        self.fold(dz)
        side, mine, theirs = (0, 1, 0) if dz == 1 else (1, 0, 1)
        end = self.ends.at[side]
        self.send(6 + side * 2 + mine, dz, mine, end.at[pl.ds(mine * 64, 64)], dz)
        inbox = self.left if dz == 1 else self.right
        self.net.got(self.slot + 4 + side, inbox)
        rows = self.rows(dz, theirs)
        self.terms[rows, :] = (self.terms[rows, :].astype(jnp.float32) + inbox[...].astype(jnp.float32)).astype(LOW)
        self.send(6 + side * 2 + theirs, dz, theirs, end.at[pl.ds(theirs * 64, 64)], dz)

    def finish(self):
        self.net.got(self.slot, self.near.at[pl.ds(0, OWN)])
        for side in range(2):
            for piece in range(2):
                self.net.got(self.slot + 6 + side * 2 + piece, self.ends.at[side, pl.ds(piece * 64, 64)])

    def result(self, start, size):
        block = part(self.net.col * OWN + start, size)
        total = self.terms[block, :].astype(jnp.float32) + self.near[pl.ds(start, size), :].astype(jnp.float32)
        for side in range(2):
            total += self.ends[side, pl.ds(start, size), :].astype(jnp.float32)
        return total


def reduce_scratch():
    return [
        pltpu.VMEM((1024, D), LOW),
        pltpu.VMEM((4 * OWN, D), LOW),
        pltpu.VMEM((64, D), LOW),
        pltpu.VMEM((64, D), LOW),
        pltpu.VMEM((2, OWN, D), LOW),
    ]


def tiles(count, body):
    lax.fori_loop(0, count, lambda t, c: (body(t), c)[1], 0)


def second_kernel(
    att, wo, x, wide, w_up, w_down, up_bias,
    mid_out, n2_out, act_out, slope_out, wu_out, wd_out,
    terms, near, left, right, ends, mid, n2, act, slope, wu, wd, send, recv, local,
):
    net = Net(send, recv, local)
    net.greet()
    by_rows = lambda ref, r: ref.at[part(r * 256, 256)]
    by_columns = lambda ref, r: ref.at[:, part(r * 256, 256)]
    gather_wu = RowGather(net, w_up, wu, by_rows, lambda ref, h: ref.at[pl.ds(h * 128, 128)])
    gather_wd = RowGather(net, w_down, wd, by_columns, lambda ref, h: ref.at[pl.ds(h * 512, 512)])
    branch = ColReduce(net, terms, near, left, right, ends)
    all_n2 = ColGather(net, n2)

    def project(dz):
        rows = part((net.z + dz) % 4 * 256, 256)

        def tile(t):
            cols = part(t * 512, 512)
            terms[rows, cols] = dot(att[rows, :], wo[:, cols], NN).astype(LOW)

        tiles(4, tile)
        branch.give(dz)

    gather_wu.begin()
    project(2)
    project(1)
    branch.far()
    project(3)
    gather_wu.steps()
    gather_wd.begin()
    branch.beside(1)
    project(0)
    branch.beside(3)
    branch.finish()
    for piece in range(4):
        rows = pl.ds(piece * 32, 32)
        total = x[rows, :].astype(jnp.float32) + branch.result(piece * 32, 32) + wide[2:3, :]
        mid[rows, :] = total
        low = norm_rows(total, wide[3:4, :], wide[4:5, :]).astype(LOW)
        n2[part(net.col * OWN + piece * 32, 32), :] = low
    all_n2.begin()
    net.store(mid, mid_out)
    gather_wd.steps()
    gather_wu.finish()
    net.store(wu, wu_out)

    def ascend(dz):
        all_n2.pair(dz)
        rows = part((net.z + dz) % 4 * 256, 256)

        def tile(t):
            cols = part(t * 256, 256)
            hidden = dot(n2[rows, :], wu[:, cols], NN) + up_bias[:, cols]
            share = 0.5 + 0.5 * lax.erf(hidden * 0.5**0.5)
            act[rows, cols] = (hidden * share).astype(LOW)
            density = jnp.exp(-0.5 * hidden * hidden) * (0.5 / jnp.pi) ** 0.5
            slope[rows, cols] = (share + hidden * density).astype(LOW)

        tiles(4, tile)

    ascend(0)
    all_n2.hop()
    ascend(3)
    ascend(1)
    all_n2.far()
    ascend(2)
    net.store(n2, n2_out)
    net.store(act, act_out)
    net.store(slope, slope_out)
    gather_wd.finish()
    net.store(wd, wd_out)
    net.drain()


def second(att, wo, x, wide, w_up, w_down, up_bias):
    return pl.pallas_call(
        second_kernel,
        out_shape=(
            full_shape(OWN, D),
            low_shape(1024, D),
            low_shape(1024, 1024),
            low_shape(1024, 1024),
            low_shape(D, 1024),
            low_shape(1024, D),
        ),
        in_specs=[VM, VM, VM, VM, HBM, HBM, VM],
        out_specs=(HBM,) * 6,
        scratch_shapes=[
            *reduce_scratch(),
            pltpu.VMEM((OWN, D), jnp.float32),
            pltpu.VMEM((1024, D), LOW),
            pltpu.VMEM((1024, 1024), LOW),
            pltpu.VMEM((1024, 1024), LOW),
            pltpu.VMEM((D, 1024), LOW),
            pltpu.VMEM((1024, D), LOW),
            *sems(48, 16),
        ],
        compiler_params=pltpu.CompilerParams(
            collective_id=2, has_side_effects=True, vmem_limit_bytes=VMEM_LIMIT
        ),
        cost_estimate=pl.CostEstimate(flops=40 * 10**9, bytes_accessed=30 * 10**6, transcendentals=2 * 10**6),
    )(att, wo, x, wide, w_up, w_down, up_bias)


def in_rows(ref, body):
    rows, width = ref.shape[-2:]
    step = min(rows, 2 ** ((32768 // width).bit_length() - 1))
    tiles(rows // step, lambda t: body(part(t * step, step)))


class SideReduce:
    def __init__(self, net, blocks, inbox):
        self.net, self.blocks, self.inbox, self.slot = net, blocks, inbox, net.slots(8)
        self.size = blocks.shape[1] // 2

    def other(self, dy):
        return (1 - self.net.half) * 4 + (self.net.y + dy) % 4

    def mine(self, dy):
        return self.net.half * 4 + (self.net.y + dy) % 4

    def give(self, dy):
        for side, dx in enumerate((1, 3)):
            rows = pl.ds(side * self.size, self.size)
            self.net.push(
                self.slot + dy * 2 + side,
                self.blocks.at[self.other(dy), rows],
                self.inbox.at[dy, rows],
                self.net.at(dx=dx),
            )

    def fold(self, dy):
        for side in range(2):
            self.net.got(self.slot + dy * 2 + side, self.inbox.at[dy, pl.ds(side * self.size, self.size)])
        r = self.mine(dy)

        def add(rows):
            total = self.blocks[r, rows, :].astype(jnp.float32) + self.inbox[dy, rows, :].astype(jnp.float32)
            self.blocks[r, rows, :] = total.astype(LOW)

        in_rows(self.blocks, add)


class LineReduce:
    def __init__(self, net, blocks, index, inbox, last):
        self.net, self.blocks, self.index, self.inbox, self.last = net, blocks, index, inbox, last
        self.slot = net.slots(4)

    def give(self, dy):
        self.net.push(self.slot + dy - 1, self.blocks.at[self.index(dy)], self.inbox.at[dy - 1], self.net.at(dy=dy))

    def close(self):
        for dy in (1, 2, 3):
            self.net.got(self.slot + dy - 1, self.inbox.at[dy - 1])
        mine = self.index(0)

        def add(rows):
            total = self.blocks[mine, rows, :].astype(jnp.float32)
            for i in range(3):
                total += self.inbox[i, rows, :].astype(jnp.float32)
            self.blocks[mine, rows, :] = total.astype(LOW)

        in_rows(self.last, add)
        self.net.push(self.slot + 3, self.blocks.at[mine], self.last, self.net.at(dx=2))

    def finish(self, emit):
        self.net.got(self.slot + 3, self.last)
        mine = self.index(0)
        in_rows(
            self.last,
            lambda rows: emit(
                rows, self.blocks[mine, rows, :].astype(jnp.float32) + self.last[rows, :].astype(jnp.float32)
            ),
        )


def norm_back(grad, centred, inverse, gain):
    scaled = grad * gain
    return inverse * (
        scaled - jnp.mean(scaled, -1, keepdims=True) - centred * jnp.mean(scaled * centred, -1, keepdims=True)
    )


def norm_parts(values):
    middle = jnp.mean(values, -1, keepdims=True)
    spread = jnp.mean(values * values, -1, keepdims=True) - middle * middle
    inverse = lax.rsqrt(spread + EPSILON)
    return (values - middle) * inverse, inverse


def column_sums(values):
    return jnp.sum(values, 0, keepdims=True)


def third_kernel(
    dy_in, wd_in, slope_in, wu_in, act_in, n2_in, mid_in, wide, wo_in, att_in,
    datt_out, dmid_out, ffn_out, gout_out, up_out, sums, lone, down_grad,
    dy, wd, slope, wu, act, n2, mid, wo, att, datt, db, gout, dmid,
    terms, near, left, right, ends, down, down_side, down_line, down_last, up, up_side,
    send, recv, local,
):
    net = Net(send, recv, local)
    loads = [
        net.move(a, b)
        for a, b in (
            (wd_in, wd), (dy_in, dy), (slope_in, slope), (wu_in, wu), (act_in, act), (n2_in, n2), (mid_in, mid), (wo_in, wo), (att_in, att),
        )
    ]
    net.greet([net.at(dx=2)])
    back = ColReduce(net, terms, near, left, right, ends)
    all_db = ColGather(net, db)
    side_down, side_up = SideReduce(net, down, down_side), SideReduce(net, up, up_side)
    line_down = LineReduce(net, down, side_down.mine, down_line, down_last)

    def pair(dz):
        return part((net.z + dz) % 4 * 256, 256)

    def descend(dz):
        rows = pair(dz)

        def into_hidden(t):
            cols = part(t * 512, 512)
            grad = dot(dy[rows, :], wd[cols, :], NT)
            slope[rows, cols] = (grad * slope[rows, cols].astype(jnp.float32)).astype(LOW)

        def into_width(t):
            cols = part(t * 512, 512)
            terms[rows, cols] = dot(slope[rows, :], wu[cols, :], NT).astype(LOW)

        tiles(2, into_hidden)
        tiles(4, into_width)
        back.give(dz)

    def down_block(r):
        cols = part(r * 256, 256)

        def tile(t):
            units = part(t * 512, 512)
            down[r, units, :] = dot(act[:, units], dy[:, cols], TN).astype(LOW)

        tiles(2, tile)

    def up_block(r):
        cols = part(r * 256, 256)

        def tile(t):
            units = part(t * 512, 512)
            up[r, :, units] = dot(n2[:, cols], slope[:, units], TN).astype(LOW)

        tiles(2, tile)

    def down_side_block(step):
        down_block(side_down.other(step))
        side_down.give(step)

    def low_rank(dz):
        all_db.pair(dz)
        rows = pair(dz)
        datt[rows, :] = dot(db[rows, :], wo[...], NT).astype(LOW)

    for copy in loads[:4]:
        copy.wait()
    descend(2)
    loads[4].wait()
    down_side_block(0)
    down_side_block(1)
    descend(1)
    back.far()
    down_side_block(2)
    down_side_block(3)
    descend(3)
    back.beside(1)
    descend(0)
    back.beside(3)
    loads[5].wait()
    for step in range(4):
        up_block(side_up.other(step))
        side_up.give(step)
    for copy in loads[6:]:
        copy.wait()
    back.finish()
    totals = [jnp.zeros((1, D), jnp.float32)] * 4
    for piece in range(4):
        rows = pl.ds(piece * 32, 32)
        own = part(net.col * OWN + piece * 32, 32)
        grad = back.result(piece * 32, 32)
        centred, inverse = norm_parts(mid[rows, :])
        upstream = dy[own, :].astype(jnp.float32)
        value = upstream + norm_back(grad, centred, inverse, wide[3:4, :])
        dmid[rows, :] = value
        low = value.astype(LOW)
        db[own, :] = low
        terms_of = (low.astype(jnp.float32), grad * centred, grad, upstream)
        totals = [a + column_sums(b) for a, b in zip(totals, terms_of)]
    all_db.begin()
    zero = jnp.zeros((2, D), jnp.float32)
    sums[...] = jnp.concatenate([zero, *totals, zero], 0)
    net.store(dmid, dmid_out)
    lone[...] = dot(jnp.ones((8, 1024), LOW), slope[...], NN)
    all_db.hop()
    for step in (1, 2, 3, 0):
        down_block(side_down.mine(step))
    low_rank(0)
    for step in (1, 2, 3, 0):
        up_block(side_up.mine(step))
    all_db.far()
    for dz in (3, 1):
        low_rank(dz)
    for step in (1, 2, 3):
        side_down.fold(step)
        line_down.give(step)
    side_down.fold(0)
    low_rank(2)
    net.store(datt, datt_out)

    def out_block(r):
        gout[r] = dot(att[...], db[:, part(r * 256, 256)], TN).astype(LOW)

    tiles(8, out_block)
    net.store(gout, gout_out)
    back.flush()

    def ascend(t):
        cols = part(t * 512, 512)
        for i in range(2):
            rows = pl.ds(i * 512, 512)
            terms[rows, cols] = dot(act[rows, :], wd[:, cols], NN).astype(LOW)

    tiles(4, ascend)
    net.store(terms, ffn_out)
    line_down.close()
    for step in range(4):
        side_up.fold(step)
        net.store(up.at[side_up.mine(step)], up_out.at[step])

    def emit(rows, values):
        down_grad[rows, :] = values

    line_down.finish(emit)
    net.drain()


def third(dy, wd, slope, wu, act, n2, mid, wide, wo, att):
    return pl.pallas_call(
        third_kernel,
        out_shape=(
            low_shape(1024, 256),
            full_shape(OWN, D),
            low_shape(1024, D),
            low_shape(8, 256, 256),
            low_shape(4, 256, 1024),
            full_shape(8, D),
            full_shape(8, 1024),
            full_shape(1024, 256),
        ),
        in_specs=[HBM] * 7 + [VM, HBM, HBM],
        out_specs=(HBM, HBM, HBM, HBM, HBM, VM, VM, VM),
        scratch_shapes=[
            pltpu.VMEM((1024, D), LOW),
            pltpu.VMEM((1024, D), LOW),
            pltpu.VMEM((1024, 1024), LOW),
            pltpu.VMEM((D, 1024), LOW),
            pltpu.VMEM((1024, 1024), LOW),
            pltpu.VMEM((1024, D), LOW),
            pltpu.VMEM((OWN, D), jnp.float32),
            pltpu.VMEM((256, D), LOW),
            pltpu.VMEM((1024, 256), LOW),
            pltpu.VMEM((1024, 256), LOW),
            pltpu.VMEM((1024, D), LOW),
            pltpu.VMEM((8, 256, 256), LOW),
            pltpu.VMEM((OWN, D), jnp.float32),
            *reduce_scratch(),
            pltpu.VMEM((8, 1024, 256), LOW),
            pltpu.VMEM((4, 1024, 256), LOW),
            pltpu.VMEM((3, 1024, 256), LOW),
            pltpu.VMEM((1024, 256), LOW),
            pltpu.VMEM((8, 256, 1024), LOW),
            pltpu.VMEM((4, 256, 1024), LOW),
            *sems(48, 24),
        ],
        compiler_params=pltpu.CompilerParams(
            collective_id=3, has_side_effects=True, vmem_limit_bytes=63 * 2**20
        ),
        cost_estimate=pl.CostEstimate(flops=40 * 10**9, bytes_accessed=30 * 10**6, transcendentals=2 * 10**6),
    )(dy, wd, slope, wu, act, n2, mid, wide, wo, att)


class Everyone:
    def __init__(self, net, axis, inbox):
        self.net, self.axis, self.inbox, self.slot = net, axis, inbox, net.slots(7)
        self.index = net.row if axis == "row" else net.col

    def device(self, shift):
        net, index = self.net, (self.index + shift) % 8
        row, col = (index, net.col) if self.axis == "row" else (net.row, index)
        return {"dp": net.dp, "row": row, "col": col}

    def begin(self, src_of):
        for shift in range(1, 8):
            to = (self.index + shift) % 8
            self.net.push(self.slot + shift - 1, src_of(to), self.inbox.at[self.index], self.device(shift))
        self.copy = self.net.move(src_of(self.index), self.inbox.at[self.index])

    def total(self):
        self.copy.wait()
        for shift in range(1, 8):
            self.net.got(self.slot + shift - 1, self.inbox.at[(self.index + 8 - shift) % 8])
        total = self.inbox[0]
        for i in range(1, 8):
            total += self.inbox[i]
        return total


def fourth_kernel(
    meta, q_in, kv_in, datt_in, lse, ffn_in, n1_in, wq_in, x_in, mid_in, dmid_in, wide, gout_in, up_in, sums, lone,
    mixed, input_grad, qkv_grad, out_grad, up_grad, wide_grad, lone_grad,
    q, kv, datt, n1, wq, x, mid, dmid, dkv, dkv_low, dkv_inbox, dqkv, mixed_own, grad_own, grad_low,
    terms, near, left, right, ends, terms2, near2, left2, right2, ends2,
    gout, gout_side, gout_line, gout_last, up, up_line, up_last, gqkv, gqkv_side, gqkv_line, gqkv_last,
    vector, wide_rows, wide_cols, wide_part, wide_sum, wide_last, single, single_rows, single_part, single_last,
    send, recv, local,
):
    net = Net(send, recv, local)
    load = {}
    for name, a, b in (
        ("ffn", ffn_in, terms), ("q", q_in, q), ("kv", kv_in, kv), ("datt", datt_in, datt), ("gout", gout_in, gout), ("up", up_in, up),
        ("mid", mid_in, mid), ("wq", wq_in, wq), ("n1", n1_in, n1), ("x", x_in, x), ("dmid", dmid_in, dmid),
    ):
        load[name] = net.move(a, b)
    cols = [{"dp": net.dp, "row": net.row, "col": (net.col + d) % 8} for d in range(1, 8)]
    net.greet([net.at(dx=2)], cols)
    ffn = ColReduce(net, terms, near, left, right, ends)
    back = ColReduce(net, terms2, near2, left2, right2, ends2)
    side_out, side_qkv = SideReduce(net, gout, gout_side), SideReduce(net, gqkv, gqkv_side)
    line_out = LineReduce(net, gout, side_out.mine, gout_line, gout_last)
    line_qkv = LineReduce(net, gqkv, side_qkv.mine, gqkv_line, gqkv_last)
    line_up = LineReduce(net, up, lambda dy: dy, up_line, up_last)
    keys = net.slots(8)
    wide_a, wide_b = Everyone(net, "row", wide_rows), Everyone(net, "col", wide_cols)
    single_a = Everyone(net, "row", single_rows)
    crossing = net.slots(2)

    def feature_block(ref):
        return lambda r: ref.at[:, part(r * 256, 256)]

    def token_block(ref):
        return lambda r: ref.at[(r // 2) % 2, r % 2, part(r // 4 * OWN, OWN)]

    mixed_swap = Swap(net, feature_block(mixed_own), token_block(mixed))
    grad_swap = Swap(net, feature_block(grad_own), token_block(grad_low))

    load["ffn"].wait()
    for dz in (2, 1, 3, 0):
        ffn.give(dz)
    load["gout"].wait()
    for dy in range(4):
        side_out.give(dy)
    load["up"].wait()
    for dy in (1, 2, 3):
        line_up.give(dy)
    ffn.far()
    for name in ("q", "kv", "datt"):
        load[name].wait()

    def attend_back_group(group):
        rows, extent = pl.ds(group * 256, 256), 512 * (group + 1)
        allowed = allowed_keys(group, extent, net.half, meta[0])
        for head in range(2):
            at = pl.ds(head * HEAD, HEAD)
            query, key, value, grad = q[rows, at], kv[0, :extent, at], kv[1, :extent, at], datt[rows, at]
            scores = dot(query, key, NT) * SCALE
            probs = jnp.exp(jnp.where(allowed, scores, -HUGE) - lse[head, rows, :])
            weighted = probs * dot(grad, value, NT)
            delta = jnp.sum(weighted, -1, keepdims=True)
            dscores = (weighted - probs * delta).astype(LOW)
            dqkv[rows, at] = (dot(dscores, key, NN) * SCALE).astype(LOW)
            dkey = dot(dscores, query, TN) * SCALE
            dvalue = dot(probs.astype(LOW), grad, TN)
            if group == 3:
                dkv[0, :, at] = dkey
                dkv[1, :, at] = dvalue
            else:
                dkv[0, :extent, at] += dkey
                dkv[1, :extent, at] += dvalue
        for i in range(2):
            block = group * 2 + i
            theirs = part(block * 256 + (1 - net.half) * OWN, OWN)
            place = pl.ds(block * OWN, OWN)
            dkv_low[:, place, :] = dkv[:, theirs, :].astype(LOW)
            net.push(keys + block, dkv_low.at[:, place], dkv_inbox.at[:, place], net.partner())

    attend_back_group(3)
    ffn.beside(1)
    attend_back_group(2)
    ffn.beside(3)
    attend_back_group(1)
    for dy in (1, 2, 3, 0):
        side_out.fold(dy)
        if dy:
            line_out.give(dy)
    attend_back_group(0)
    load["wq"].wait()
    load["n1"].wait()
    load["mid"].wait()
    ffn.finish()
    for piece in range(4):
        rows = pl.ds(piece * 32, 32)
        mixed_own[rows, :] = (mid[rows, :] + ffn.result(piece * 32, 32) + wide[5:6, :]).astype(LOW)
    mixed_swap.begin()
    for block in range(8):
        place = pl.ds(block * OWN, OWN)
        net.got(keys + block, dkv_inbox.at[:, place])
        mine = part(block * 256 + net.half * OWN, OWN)
        for i in range(2):
            total = dkv[i, mine, :] + dkv_inbox[i, place, :].astype(jnp.float32)
            dqkv[place, pl.ds(256 + i * 256, 256)] = total.astype(LOW)

    def descend(dz):
        rows = part((net.z + dz) % 4 * 256, 256)

        def tile(t):
            at = part(t * 512, 512)
            total = dot(dqkv[rows, pl.ds(0, 256)], wq[0, at, :], NT)
            for i in (1, 2):
                total += dot(dqkv[rows, pl.ds(i * 256, 256)], wq[i, at, :], NT)
            terms2[rows, at] = total.astype(LOW)

        tiles(4, tile)
        back.give(dz)

    def qkv_block(r):
        gqkv[r] = dot(n1[:, part(r * 256, 256)], dqkv[...], TN).astype(LOW)

    def qkv_side(dy):
        qkv_block(side_qkv.other(dy))
        side_qkv.give(dy)

    descend(2)
    qkv_side(0)
    descend(1)
    back.far()
    qkv_side(1)
    descend(3)
    back.beside(1)
    qkv_side(2)
    descend(0)
    back.beside(3)
    qkv_side(3)
    single[:, pl.ds(0, 1024)] = lone[...]
    single[:, pl.ds(1024, 768)] = dot(jnp.ones((8, 1024), LOW), dqkv[...], NN)
    single_a.begin(lambda r: single)
    line_up.close()
    line_out.close()
    for dy in (1, 2, 3, 0):
        qkv_block(side_qkv.mine(dy))
    load["x"].wait()
    load["dmid"].wait()
    back.finish()
    totals = [jnp.zeros((1, D), jnp.float32)] * 2
    for piece in range(4):
        rows = pl.ds(piece * 32, 32)
        grad = back.result(piece * 32, 32)
        centred, inverse = norm_parts(x[rows, :].astype(jnp.float32))
        value = dmid[rows, :] + norm_back(grad, centred, inverse, wide[0:1, :])
        grad_own[rows, :] = value.astype(LOW)
        totals = [a + column_sums(b) for a, b in zip(totals, (grad * centred, grad))]
    grad_swap.begin()
    vector[...] = sums[...] + jnp.concatenate([*totals, jnp.zeros((6, D), jnp.float32)], 0)
    wide_a.begin(feature_block(vector))
    for dy in (1, 2, 3, 0):
        side_qkv.fold(dy)
        if dy:
            line_qkv.give(dy)
    single_part[...] = single_a.total()
    net.push(crossing, single_part, single_last, net.at(dx=2))

    def emit_to(ref):
        def emit(rows, values):
            ref[rows, :] = values

        return emit

    line_up.finish(emit_to(up_grad))
    wide_part[...] = wide_a.total()
    wide_b.begin(lambda r: wide_part)
    line_out.finish(emit_to(out_grad))
    mixed_swap.finish()
    wide_sum[...] = wide_b.total()
    net.push(crossing + 1, wide_sum, wide_last, net.at(dx=2))
    line_qkv.close()
    grad_swap.finish()
    for i in range(2):
        for j in range(2):
            input_grad[i, j] = grad_low[i, j].astype(jnp.float32)
    net.got(crossing, single_last)
    lone_grad[...] = single_part[...] + single_last[...]
    net.got(crossing + 1, wide_last)
    wide_grad[...] = wide_sum[...] + wide_last[...]

    def emit_qkv(rows, values):
        for i in range(3):
            qkv_grad[i, rows, :] = values[:, i * 256 : (i + 1) * 256]

    line_qkv.finish(emit_qkv)
    net.drain()


def fourth(length, q, kv, datt, lse, ffn, n1, wq, x, mid, dmid, wide, gout, up, sums, lone):
    return pl.pallas_call(
        fourth_kernel,
        out_shape=(
            low_shape(2, 2, 256, 256),
            full_shape(2, 2, 256, 256),
            full_shape(3, 256, 256),
            full_shape(256, 256),
            full_shape(256, 1024),
            full_shape(8, 256),
            full_shape(8, 1792),
        ),
        in_specs=[SM, HBM, HBM, HBM, VM, HBM, HBM, HBM, HBM, HBM, HBM, VM, HBM, HBM, VM, VM],
        out_specs=(VM,) * 7,
        scratch_shapes=[
            pltpu.VMEM((1024, 256), LOW),
            pltpu.VMEM((2, 2048, 256), LOW),
            pltpu.VMEM((1024, 256), LOW),
            pltpu.VMEM((1024, D), LOW),
            pltpu.VMEM((3, D, 256), LOW),
            pltpu.VMEM((OWN, D), LOW),
            pltpu.VMEM((OWN, D), jnp.float32),
            pltpu.VMEM((OWN, D), jnp.float32),
            pltpu.VMEM((2, 2048, 256), jnp.float32),
            pltpu.VMEM((2, 1024, 256), LOW),
            pltpu.VMEM((2, 1024, 256), LOW),
            pltpu.VMEM((1024, 768), LOW),
            pltpu.VMEM((OWN, D), LOW),
            pltpu.VMEM((OWN, D), LOW),
            pltpu.VMEM((2, 2, 256, 256), LOW),
            *reduce_scratch(),
            *reduce_scratch(),
            pltpu.VMEM((8, 256, 256), LOW),
            pltpu.VMEM((4, 256, 256), LOW),
            pltpu.VMEM((3, 256, 256), LOW),
            pltpu.VMEM((256, 256), LOW),
            pltpu.VMEM((4, 256, 1024), LOW),
            pltpu.VMEM((3, 256, 1024), LOW),
            pltpu.VMEM((256, 1024), LOW),
            pltpu.VMEM((8, 256, 768), LOW),
            pltpu.VMEM((4, 256, 768), LOW),
            pltpu.VMEM((3, 256, 768), LOW),
            pltpu.VMEM((256, 768), LOW),
            pltpu.VMEM((8, D), jnp.float32),
            pltpu.VMEM((8, 8, 256), jnp.float32),
            pltpu.VMEM((8, 8, 256), jnp.float32),
            pltpu.VMEM((8, 256), jnp.float32),
            pltpu.VMEM((8, 256), jnp.float32),
            pltpu.VMEM((8, 256), jnp.float32),
            pltpu.VMEM((8, 1792), jnp.float32),
            pltpu.VMEM((8, 8, 1792), jnp.float32),
            pltpu.VMEM((8, 1792), jnp.float32),
            pltpu.VMEM((8, 1792), jnp.float32),
            *sems(112, 16),
        ],
        compiler_params=pltpu.CompilerParams(
            collective_id=4, has_side_effects=True, vmem_limit_bytes=63 * 2**20
        ),
        cost_estimate=pl.CostEstimate(flops=40 * 10**9, bytes_accessed=30 * 10**6, transcendentals=2 * 10**6),
    )(length, q, kv, datt, lse, ffn, n1, wq, x, mid, dmid, wide, gout, up, sums, lone)


def shards(
    inputs,
    lengths,
    ln1_gain,
    ln1_bias,
    w_qkv,
    qv_bias,
    w_out,
    out_bias,
    ln2_gain,
    ln2_bias,
    w_up,
    up_bias,
    w_down,
    down_bias,
    cotangent,
):
    row = lax.axis_index("row")
    micro, seq = (row // 2) % 2, row % 2
    length = lengths[micro, seq].reshape(1)
    zero = jnp.zeros_like(ln1_gain)
    small = jnp.stack([ln1_gain, ln1_bias, out_bias, ln2_gain, ln2_bias, down_bias, zero, zero])
    x, all_dy, all1, q, kv, att, lse, wq, wo, wide = first(length, inputs, cotangent, small, w_qkv, w_out, qv_bias)
    mid, all2, act, slope, wu, wd = second(att, wo, x, wide, w_up, w_down, up_bias.reshape(1, 1024))
    datt, dmid, ffn, gout, up, sums, lone, g_down = third(all_dy, wd, slope, wu, act, all2, mid, wide, wo, att)
    mixed, input_grad, g_qkv, g_out, g_up, wide_grad, lone_grad = fourth(
        length, q, kv, datt, lse, ffn, all1, wq, x, mid, dmid, wide, gout, up, sums, lone
    )
    qv_grad = jnp.stack([lone_grad[0, 1024:1280], lone_grad[0, 1536:1792]])
    return (
        mixed,
        input_grad,
        wide_grad[0],
        wide_grad[1],
        g_qkv,
        qv_grad,
        g_out,
        wide_grad[2],
        wide_grad[3],
        wide_grad[4],
        g_up,
        lone_grad[0, :1024],
        g_down,
        wide_grad[5],
    )


def solution(mesh):
    tokens = P(None, "dp", "col", "row")
    in_specs = (
        tokens,
        P(None, "dp"),
        P("row"),
        P("row"),
        P(None, "row", "col"),
        P(None, "col"),
        P("col", "row"),
        P("row"),
        P("row"),
        P("row"),
        P("row", "col"),
        P("col"),
        P("col", "row"),
        P("row"),
        tokens,
    )
    out_specs = (
        tokens,
        tokens,
        P("row"),
        P("row"),
        P(None, "row", "col"),
        P(None, "col"),
        P("col", "row"),
        P("row"),
        P("row"),
        P("row"),
        P("row", "col"),
        P("col"),
        P("col", "row"),
        P("row"),
    )
    return jax.shard_map(shards, mesh=mesh, in_specs=in_specs, out_specs=out_specs, check_vma=False)
```

```python
import functools

import jax
import jax.numpy as jnp
from jax import lax
from jax.experimental import pallas as pl
from jax.experimental.pallas import tpu as pltpu
from jax.sharding import PartitionSpec as P

D = 2048
HEAD = 128
SCALE = HEAD**-0.5
EPSILON = 1e-05
HUGE = 1e30
LOW = jnp.bfloat16
OWN = 128
VMEM_LIMIT = 56 * 2**20


def dot(a, b, contract):
    return lax.dot_general(a, b, ((contract[0], contract[1]), ((), ())), preferred_element_type=jnp.float32)


NN = ((1,), (0,))
NT = ((1,), (1,))
TN = ((0,), (0,))


def place_rows(group, half):
    row = lax.broadcasted_iota(jnp.int32, (256, 1), 0)
    return (2 * group + row // OWN) * 256 + half * OWN + row % OWN


def allowed_keys(group, extent, half, length):
    slot = lax.broadcasted_iota(jnp.int32, (256, extent), 1)
    return (slot <= place_rows(group, half)) & (slot < length)


MESH = pl.DeviceIdType.MESH
HBM = pl.BlockSpec(memory_space=pl.ANY)
VM = pl.BlockSpec(memory_space=pltpu.VMEM)
SM = pl.BlockSpec(memory_space=pltpu.SMEM)


def part(start, size):
    return pl.ds(pl.multiple_of(start, size), size)


class Net:
    def __init__(self, send, recv, local):
        self.send, self.recv, self.local = send, recv, local
        self.used, self.local_used, self.live, self.own = 0, 0, [], []
        self.dp, self.row, self.col = (lax.axis_index(a) for a in ("dp", "row", "col"))
        self.half, self.y = self.row // 4, self.row % 4
        self.x = self.dp * 2 + self.half
        self.z, self.core = self.col // 2, self.col % 2

    def at(self, dx=0, dy=0, dz=0, other_core=False):
        x, y, z = (self.x + dx) % 4, (self.y + dy) % 4, (self.z + dz) % 4
        core = 1 - self.core if other_core else self.core
        return {"dp": x // 2, "row": (x % 2) * 4 + y, "col": z * 2 + core}

    def mate(self, shift):
        return {"dp": self.dp, "row": (self.row + shift) % 8, "col": self.col}

    def partner(self):
        return self.mate(4)

    def cousin(self):
        return {"dp": 1 - self.dp, "row": (self.row + 4) % 8, "col": self.col}

    def greet(self, more=(), cols=()):
        devices = [self.mate(d) for d in range(1, 8)]
        devices += [self.cousin()]
        devices += cols or [self.at(dz=1), self.at(dz=3), self.at(other_core=True)]
        devices += more
        barrier = pltpu.get_barrier_semaphore()
        for device in devices:
            pl.semaphore_signal(barrier, inc=1, device_id=device, device_id_type=MESH)
        pl.semaphore_wait(barrier, len(devices))

    def slots(self, count):
        self.used += count
        return self.used - count

    def _copy(self, slot, src, dst, device):
        return pltpu.make_async_remote_copy(
            src_ref=src,
            dst_ref=dst,
            send_sem=self.send.at[slot],
            recv_sem=self.recv.at[slot],
            device_id=device,
            device_id_type=MESH,
        )

    def push(self, slot, src, dst, device):
        copy = self._copy(slot, src, dst, device)
        copy.start()
        self.live.append(copy)

    def got(self, slot, ref):
        self._copy(slot, ref, ref, self.at(other_core=True)).wait_recv()

    def move(self, src, dst):
        copy = pltpu.make_async_copy(src, dst, self.local.at[self.local_used])
        self.local_used += 1
        copy.start()
        return copy

    def store(self, src, dst):
        self.own.append(self.move(src, dst))

    def drain(self):
        for copy in self.live:
            copy.wait_send()
        for copy in self.own:
            copy.wait()


class ColGather:
    def __init__(self, net, buf):
        self.net, self.buf, self.slot = net, buf, net.slots(14)

    def rows(self, dz, other_core, piece):
        net = self.net
        core = 1 - net.core if other_core else net.core
        return self.buf.at[part(((net.z + dz) % 4 * 2 + core) * OWN + 64 * piece, 64)]

    def move(self, slot, where, piece, **to):
        ref = self.rows(where, False, piece)
        self.net.push(self.slot + slot, ref, ref, self.net.at(**to))

    def got(self, slot, dz, piece, other_core=False):
        self.net.got(self.slot + slot, self.rows(dz, other_core, piece))

    def begin(self):
        self.move(0, 0, 0, dz=1)
        self.move(3, 0, 1, dz=3)
        self.move(1, 0, 1, dz=1)
        self.move(2, 0, 0, dz=3)
        self.move(6, 0, 0, other_core=True)
        self.move(7, 0, 1, other_core=True)

    def hop(self):
        self.pass_on()
        self.take_rest()

    def pass_on(self):
        self.got(0, 3, 0)
        self.move(4, 3, 0, dz=1)
        self.got(3, 1, 1)
        self.move(5, 1, 1, dz=3)
        self.move(8, 3, 0, other_core=True)
        self.move(11, 1, 1, other_core=True)

    def take_rest(self):
        self.got(1, 3, 1)
        self.move(9, 3, 1, other_core=True)
        self.got(2, 1, 0)
        self.move(10, 1, 0, other_core=True)

    def far(self):
        self.got(4, 2, 0)
        self.move(12, 2, 0, other_core=True)
        self.got(5, 2, 1)
        self.move(13, 2, 1, other_core=True)

    def pair(self, dz):
        slot = {0: 6, 3: 8, 1: 10, 2: 12}[dz]
        self.got(slot, dz, 0, True)
        self.got(slot + 1, dz, 1, True)


class RowGather:
    def __init__(self, net, src, buf, whole, parts):
        self.net, self.src, self.buf, self.whole, self.parts = net, src, buf, whole, parts
        self.slot = net.slots(11)

    def place(self, dy, other=False):
        net = self.net
        half = 1 - net.half if other else net.half
        return self.whole(self.buf, half * 4 + (net.y + dy) % 4)

    def sideways(self, dy, src, sides=(0, 1)):
        net, there = self.net, self.place(dy)
        devices = (net.partner(), net.cousin())
        for side in sides:
            net.push(
                self.slot + 3 + dy * 2 + side, self.parts(src, side), self.parts(there, side), devices[side]
            )

    def begin(self):
        net, mine = self.net, self.place(0)
        for dy in (1, 3, 2):
            net.push(self.slot + dy - 1, self.src, mine, net.at(dy=dy))
        self.copy = net.move(self.src, mine)

    def begin_sideways(self, sides=(0, 1)):
        self.sideways(0, self.src, sides)

    def step(self, dy, sides=(0, 1)):
        ref = self.place(4 - dy)
        self.net.got(self.slot + dy - 1, ref)
        self.sideways(4 - dy, ref, sides)

    def follow(self, dy, sides):
        self.sideways(4 - dy, self.place(4 - dy), sides)

    def steps(self):
        for dy in (1, 3, 2):
            self.step(dy)

    def finish(self):
        self.copy.wait()
        for dy in range(4):
            for side in range(2):
                self.net.got(self.slot + 3 + dy * 2 + side, self.parts(self.place(dy, True), side))


def cut(rows):
    def parts(ref, side):
        total = ref.shape[-2]
        window = pl.ds(0, rows) if side == 0 else pl.ds(rows, total - rows)
        return ref.at[:, window] if len(ref.shape) == 3 else ref.at[window]

    return parts


class Swap:
    def __init__(self, net, src_of, dst_of):
        self.net, self.src_of, self.dst_of, self.slot = net, src_of, dst_of, net.slots(7)

    def begin(self):
        net = self.net
        for shift in range(1, 8):
            net.push(self.slot + shift - 1, self.src_of((net.row + shift) % 8), self.dst_of(net.row), net.mate(shift))
        self.copy = net.move(self.src_of(net.row), self.dst_of(net.row))

    def finish(self):
        net = self.net
        self.copy.wait()
        for shift in range(1, 8):
            net.got(self.slot + shift - 1, self.dst_of((net.row + 8 - shift) % 8))


def norm_rows(values, gain, bias):
    middle = jnp.mean(values, -1, keepdims=True)
    spread = jnp.mean(values * values, -1, keepdims=True) - middle * middle
    inverse = lax.rsqrt(spread + EPSILON)
    centred = (values - middle) * inverse
    return centred * gain + bias


def attend_group(q, kv, head, group, half, length):
    cols, rows, extent = pl.ds(head * HEAD, HEAD), pl.ds(group * 256, 256), 512 * (group + 1)
    scores = dot(q[rows, cols], kv[0, :extent, cols], NT) * SCALE
    scores = jnp.where(allowed_keys(group, extent, half, length), scores, -HUGE)
    highest = jnp.max(scores, -1, keepdims=True)
    weights = jnp.exp(scores - highest)
    total = jnp.sum(weights, -1, keepdims=True)
    out = dot(weights.astype(LOW), kv[1, :extent, cols], NN) / total
    return out, highest + jnp.log(total)


def low_shape(*shape):
    return jax.ShapeDtypeStruct(shape, LOW)


def full_shape(*shape):
    return jax.ShapeDtypeStruct(shape, jnp.float32)


def sems(remote, local):
    return [
        pltpu.SemaphoreType.DMA((remote,)),
        pltpu.SemaphoreType.DMA((remote,)),
        pltpu.SemaphoreType.DMA((local,)),
    ]


class ColReduce:
    def __init__(self, net, terms, near, left, right, ends):
        self.net, self.terms, self.near, self.left, self.right, self.ends = net, terms, near, left, right, ends
        self.slot = net.slots(10)
        self.sent = []

    def push(self, *copy):
        self.net.push(*copy)
        self.sent.append(self.net.live[-1])

    def flush(self):
        for copy in self.sent:
            copy.wait_send()
        self.net.live = [copy for copy in self.net.live if not any(copy is other for other in self.sent)]

    def block(self, dz, other_core=False):
        net = self.net
        core = 1 - net.core if other_core else net.core
        return part(((net.z + dz) % 4 * 2 + core) * OWN, OWN)

    def rows(self, dz, piece):
        net = self.net
        return part(((net.z + dz) % 4 * 2 + net.core) * OWN + 64 * piece, 64)

    def give(self, dz):
        self.push(
            self.slot + dz, self.terms.at[self.block(dz, True)], self.near.at[pl.ds(dz * OWN, OWN)], self.net.at(other_core=True)
        )

    def fold(self, dz):
        near = self.near.at[pl.ds(dz * OWN, OWN)]
        self.net.got(self.slot + dz, near)
        block = self.block(dz)
        self.terms[block, :] = (self.terms[block, :].astype(jnp.float32) + near[...].astype(jnp.float32)).astype(LOW)

    def send(self, slot, dz, piece, dst, side):
        self.push(self.slot + slot, self.terms.at[self.rows(dz, piece)], dst, self.net.at(dz=side))

    def far(self):
        self.fold(2)
        self.send(4, 2, 0, self.left, 1)
        self.send(5, 2, 1, self.right, 3)

    def own(self, dz):
        self.fold(dz)
        side = 0 if dz == 1 else 1
        self.send(6 + side * 2 + 1 - side, dz, 1 - side, self.ends.at[side, pl.ds((1 - side) * 64, 64)], dz)

    def forward(self, dz):
        side = 0 if dz == 1 else 1
        inbox = self.left if dz == 1 else self.right
        self.net.got(self.slot + 4 + side, inbox)
        rows = self.rows(dz, side)
        self.terms[rows, :] = (self.terms[rows, :].astype(jnp.float32) + inbox[...].astype(jnp.float32)).astype(LOW)
        self.send(6 + side * 2 + side, dz, side, self.ends.at[side, pl.ds(side * 64, 64)], dz)

    def finish(self):
        self.net.got(self.slot, self.near.at[pl.ds(0, OWN)])
        for side in range(2):
            for piece in range(2):
                self.net.got(self.slot + 6 + side * 2 + piece, self.ends.at[side, pl.ds(piece * 64, 64)])

    def result(self, start, size):
        block = part(self.net.col * OWN + start, size)
        total = self.terms[block, :].astype(jnp.float32) + self.near[pl.ds(start, size), :].astype(jnp.float32)
        for side in range(2):
            total += self.ends[side, pl.ds(start, size), :].astype(jnp.float32)
        return total


def reduce_scratch():
    return [
        pltpu.VMEM((1024, D), LOW),
        pltpu.VMEM((4 * OWN, D), LOW),
        pltpu.VMEM((64, D), LOW),
        pltpu.VMEM((64, D), LOW),
        pltpu.VMEM((2, OWN, D), LOW),
    ]


def tiles(count, body):
    lax.fori_loop(0, count, lambda t, c: (body(t), c)[1], 0)


def ahead_kernel(
    lengths, inputs, cotangent, gain1, bias1, bias_out, gain2, bias2, bias_down, w_qkv, w_out, w_up, w_down, qv_bias, up_bias,
    x_out, dy_out, n1_out, q_out, kv_out, att_out, lse_out, wq_out, wo_out, small_out,
    mid_out, n2_out, act_out, slope_out, wu_out, wd_out,
    x, dy, n1, q, kv, att, wq, wo, wide,
    terms, near, left, right, ends, mid, n2, act, slope, wu, wd, small, lse, send, recv, local,
):
    net = Net(send, recv, local)
    for i, ref in enumerate((gain1, bias1, bias_out, gain2, bias2, bias_down)):
        small[i : i + 1, :] = ref[...]
    small[6:8, :] = jnp.zeros((2, 256), jnp.float32)
    length = lengths[(net.row // 2) % 2, net.row % 2]
    net.greet()
    mine = part(net.col * OWN, OWN)

    def token_block(ref):
        return lambda r: ref.at[(r // 2) % 2, r % 2, part(r // 4 * OWN, OWN)]

    def feature_block(ref):
        return lambda r: ref.at[:, part(r * 256, 256)]

    def by_columns(ref, r):
        return ref.at[:, part(r * 256, 256)]

    def by_rows(ref, r):
        return ref.at[part(r * 256, 256)]

    params = Swap(net, lambda r: small, feature_block(wide))
    tokens = Swap(net, token_block(inputs), feature_block(x))
    upstream = Swap(net, token_block(cotangent), lambda r: dy.at[mine, part(r * 256, 256)])
    gather_kv = RowGather(net, w_qkv.at[pl.ds(1, 2)], wq.at[pl.ds(1, 2)], by_columns, cut(128))
    gather_q = RowGather(net, w_qkv.at[pl.ds(0, 1)], wq.at[pl.ds(0, 1)], by_columns, cut(32))
    gather_wo = RowGather(net, w_out, wo, by_columns, cut(16))
    gather_wu = RowGather(net, w_up, wu, by_rows, cut(128))
    gather_wd = RowGather(net, w_down, wd, by_columns, cut(512))
    all_n1, all_dy, all_n2 = ColGather(net, n1), ColGather(net, dy), ColGather(net, n2)
    branch = ColReduce(net, terms, near, left, right, ends)
    keys = net.slots(16)

    def pair(dz):
        return part((net.z + dz) % 4 * 256, 256)

    def project_keys(dz):
        all_n1.pair(dz)
        block = (net.z + dz) % 4
        values = n1[pair(dz), :]
        k = dot(values, wq[1], NN).astype(LOW)
        v = (dot(values, wq[2], NN) + qv_bias[1:2, :]).astype(LOW)
        for i in range(2):
            there = part((block * 2 + i) * 256 + net.half * OWN, OWN)
            kv[0, there, :] = k[i * OWN : (i + 1) * OWN]
            kv[1, there, :] = v[i * OWN : (i + 1) * OWN]

    def key_block(dz, i, half, head):
        there = part(((net.z + dz) % 4 * 2 + i) * 256 + half * OWN, OWN)
        return kv.at[:, there, pl.ds(head * HEAD, HEAD)]

    def swap_keys(dz, head):
        for i in range(2):
            ref = key_block(dz, i, net.half, head)
            net.push(keys + head * 8 + dz * 2 + i, ref, ref, net.partner())

    def take_keys(dz, head):
        for i in range(2):
            net.got(keys + head * 8 + dz * 2 + i, key_block(dz, i, 1 - net.half, head))

    params.begin()
    tokens.begin()
    gather_kv.begin()
    gather_kv.begin_sideways()
    params.finish()
    tokens.finish()
    for piece in range(4):
        rows = pl.ds(piece * 32, 32)
        low = norm_rows(x[rows, :].astype(jnp.float32), wide[0:1, :], wide[1:2, :]).astype(LOW)
        n1[part(net.col * OWN + piece * 32, 32), :] = low
    all_n1.begin()
    net.store(x, x_out)
    net.store(wide, small_out)
    all_n1.pass_on()
    gather_kv.steps()
    gather_q.begin()
    gather_q.begin_sideways()
    all_n1.take_rest()
    upstream.begin()
    gather_kv.finish()
    for dz in (0, 3, 1):
        project_keys(dz)
        swap_keys(dz, 0)
    all_n1.far()
    project_keys(2)
    swap_keys(2, 0)
    gather_wo.begin()
    gather_wo.begin_sideways()
    gather_wu.begin()
    gather_wd.begin()
    upstream.finish()
    all_dy.begin()
    gather_q.steps()
    gather_wu.begin_sideways((1,))
    all_dy.pass_on()
    take_keys(0, 0)
    take_keys(3, 0)
    for dz in (0, 3, 1, 2):
        swap_keys(dz, 1)
    gather_q.finish()

    def project_queries(t):
        rows = part(t * 256, 256)
        q[rows, :] = (dot(n1[rows, :], wq[0], NN) + qv_bias[0:1, :]).astype(LOW)

    tiles(4, project_queries)
    def attend(head):
        for dz in (0, 3, 1, 2):
            if head or dz in (1, 2):
                take_keys(dz, head)
        for group in range(4):
            out, logsum = attend_group(q, kv, head, group, net.half, length)
            rows = pl.ds(group * 256, 256)
            att[rows, pl.ds(head * HEAD, HEAD)] = out.astype(LOW)
            lse[head, rows, :] = logsum

    gather_wo.steps()
    attend(0)
    all_dy.take_rest()
    all_dy.far()
    attend(1)
    gather_wu.begin_sideways((0,))
    gather_wo.finish()

    def project(dz):
        rows = pair(dz)

        def tile(t):
            cols = part(t * 512, 512)
            terms[rows, cols] = dot(att[rows, :], wo[:, cols], NN).astype(LOW)

        tiles(4, tile)
        branch.give(dz)

    project(2)
    project(1)
    branch.far()
    gather_wu.step(1)
    gather_wu.step(3)
    project(3)
    branch.own(1)
    branch.own(3)
    project(0)
    gather_wu.step(2)
    branch.forward(1)
    branch.forward(3)
    for a, b in ((n1, n1_out), (wq, wq_out), (q, q_out), (kv, kv_out), (att, att_out), (lse, lse_out), (wo, wo_out)):
        net.store(a, b)
    branch.finish()
    for piece in range(4):
        rows = pl.ds(piece * 32, 32)
        total = x[rows, :].astype(jnp.float32) + branch.result(piece * 32, 32) + wide[2:3, :]
        mid[rows, :] = total
        low = norm_rows(total, wide[3:4, :], wide[4:5, :]).astype(LOW)
        n2[part(net.col * OWN + piece * 32, 32), :] = low
    all_n2.begin()
    gather_wd.begin_sideways()
    gather_wd.step(1)
    gather_wd.step(3)
    gather_wu.finish()

    def ascend(dz):
        all_n2.pair(dz)
        rows = pair(dz)

        def tile(t):
            cols = part(t * 256, 256)
            hidden = dot(n2[rows, :], wu[:, cols], NN) + up_bias[:, cols]
            share = 0.5 + 0.5 * lax.erf(hidden * 0.5**0.5)
            act[rows, cols] = (hidden * share).astype(LOW)
            density = jnp.exp(-0.5 * hidden * hidden) * (0.5 / jnp.pi) ** 0.5
            slope[rows, cols] = (share + hidden * density).astype(LOW)

        tiles(4, tile)
        for a, b in ((act, act_out), (slope, slope_out), (n2, n2_out)):
            net.store(a.at[rows], b.at[rows])

    ascend(0)
    all_n2.pass_on()
    gather_wd.step(2)
    all_n2.take_rest()
    ascend(3)
    for dz in range(4):
        all_dy.pair(dz)
    for a, b in ((mid, mid_out), (wu, wu_out), (dy, dy_out)):
        net.store(a, b)
    all_n2.far()
    ascend(1)
    ascend(2)
    gather_wd.finish()
    net.store(wd, wd_out)
    net.drain()


def ahead(lengths, inputs, cotangent, small, w_qkv, w_out, w_up, w_down, qv_bias, up_bias):
    return pl.pallas_call(
        ahead_kernel,
        out_shape=(
            low_shape(OWN, D),
            low_shape(1024, D),
            low_shape(1024, D),
            low_shape(1024, 256),
            low_shape(2, 2048, 256),
            low_shape(1024, 256),
            full_shape(2, 1024, 1),
            low_shape(3, D, 256),
            low_shape(256, D),
            full_shape(8, D),
            full_shape(OWN, D),
            low_shape(1024, D),
            low_shape(1024, 1024),
            low_shape(1024, 1024),
            low_shape(D, 1024),
            low_shape(1024, D),
        ),
        in_specs=[SM, HBM, HBM, *[VM] * 6, HBM, HBM, HBM, HBM, VM, VM],
        out_specs=(HBM,) * 16,
        scratch_shapes=[
            pltpu.VMEM((OWN, D), LOW),
            pltpu.VMEM((1024, D), LOW),
            pltpu.VMEM((1024, D), LOW),
            pltpu.VMEM((1024, 256), LOW),
            pltpu.VMEM((2, 2048, 256), LOW),
            pltpu.VMEM((1024, 256), LOW),
            pltpu.VMEM((3, D, 256), LOW),
            pltpu.VMEM((256, D), LOW),
            pltpu.VMEM((8, D), jnp.float32),
            *reduce_scratch(),
            pltpu.VMEM((OWN, D), jnp.float32),
            pltpu.VMEM((1024, D), LOW),
            pltpu.VMEM((1024, 1024), LOW),
            pltpu.VMEM((1024, 1024), LOW),
            pltpu.VMEM((D, 1024), LOW),
            pltpu.VMEM((1024, D), LOW),
            pltpu.VMEM((8, 256), jnp.float32),
            pltpu.VMEM((2, 1024, 1), jnp.float32),
            *sems(152, 48),
        ],
        compiler_params=pltpu.CompilerParams(
            collective_id=1, has_side_effects=True, vmem_limit_bytes=63 * 2**20
        ),
        cost_estimate=pl.CostEstimate(flops=40 * 10**9, bytes_accessed=30 * 10**6, transcendentals=2 * 10**6),
    )(lengths, inputs, cotangent, *small, w_qkv, w_out, w_up, w_down, qv_bias, up_bias)


def in_rows(ref, body):
    rows, width = ref.shape[-2:]
    step = min(rows, 2 ** ((32768 // width).bit_length() - 1))
    tiles(rows // step, lambda t: body(part(t * step, step)))


class SideReduce:
    def __init__(self, net, blocks, inbox, first, index=lambda dy: dy):
        self.net, self.blocks, self.inbox, self.index, self.slot = net, blocks, inbox, index, net.slots(8)
        self.windows = (pl.ds(0, first), pl.ds(first, inbox.shape[1] - first))

    def other(self, dy):
        return (1 - self.net.half) * 4 + (self.net.y + dy) % 4

    def mine(self, dy):
        return self.net.half * 4 + (self.net.y + dy) % 4

    def give(self, dy):
        for side, device in enumerate((self.net.partner(), self.net.cousin())):
            rows = self.windows[side]
            self.net.push(
                self.slot + dy * 2 + side, self.blocks.at[self.index(dy), rows], self.inbox.at[dy, rows], device
            )

    def take(self, dy):
        for side in range(2):
            self.net.got(self.slot + dy * 2 + side, self.inbox.at[dy, self.windows[side]])


class LineReduce:
    def __init__(self, net, blocks, inbox, last):
        self.net, self.blocks, self.inbox, self.last = net, blocks, inbox, last
        self.slot = net.slots(4)

    def give(self, dy):
        self.net.push(self.slot + dy - 1, self.blocks.at[dy], self.inbox.at[dy - 1], self.net.at(dy=dy))

    def settle(self):
        for dy in (1, 2, 3):
            self.net.got(self.slot + dy - 1, self.inbox.at[dy - 1])

        def add(rows):
            total = self.blocks[0, rows, :].astype(jnp.float32)
            for i in range(3):
                total += self.inbox[i, rows, :].astype(jnp.float32)
            self.blocks[0, rows, :] = total.astype(LOW)

        in_rows(self.last, add)

    def close(self):
        self.settle()
        self.net.push(self.slot + 3, self.blocks.at[0], self.last, self.net.at(dx=2))

    def finish(self, emit):
        self.net.got(self.slot + 3, self.last)
        in_rows(
            self.last,
            lambda rows: emit(rows, self.blocks[0, rows, :].astype(jnp.float32) + self.last[rows, :].astype(jnp.float32)),
        )


class LineFirst:
    def __init__(self, net, blocks, inbox, total, side, last, first):
        self.net, self.blocks, self.inbox, self.total, self.side, self.last = net, blocks, inbox, total, side, last
        self.slot = net.slots(9)
        self.windows = (pl.ds(0, first), pl.ds(first, side.shape[0] - first))

    def owner(self, which, dy):
        half = 1 - self.net.half if which else self.net.half
        return half * 4 + (self.net.y + dy) % 4

    def give(self, which, dy):
        place = which * 3 + dy - 1
        self.net.push(self.slot + place, self.blocks.at[place], self.inbox.at[place], self.net.at(dy=dy))

    def take(self, which):
        for dy in (1, 2, 3):
            self.net.got(self.slot + which * 3 + dy - 1, self.inbox.at[which * 3 + dy - 1])

    def arrived(self, which, rows):
        return sum(self.inbox[which * 3 + i, rows, :].astype(jnp.float32) for i in range(3))

    def sideways(self):
        for i, device in enumerate((self.net.partner(), self.net.cousin())):
            rows = self.windows[i]
            self.net.push(self.slot + 6 + i, self.total.at[1, rows], self.side.at[rows], device)

    def close(self):
        for i in range(2):
            self.net.got(self.slot + 6 + i, self.side.at[self.windows[i]])

        def add(rows):
            total = self.total[0, rows, :].astype(jnp.float32) + self.side[rows, :].astype(jnp.float32)
            self.total[0, rows, :] = total.astype(LOW)

        in_rows(self.side, add)
        self.net.push(self.slot + 8, self.total.at[0], self.last, self.net.at(dx=2))

    def finish(self, emit):
        self.net.got(self.slot + 8, self.last)
        in_rows(
            self.last,
            lambda rows: emit(
                rows, self.total[0, rows, :].astype(jnp.float32) + self.last[rows, :].astype(jnp.float32)
            ),
        )


def emit_to(ref):
    def emit(rows, values):
        ref[rows, :] = values

    return emit


def norm_back(grad, centred, inverse, gain):
    scaled = grad * gain
    return inverse * (
        scaled - jnp.mean(scaled, -1, keepdims=True) - centred * jnp.mean(scaled * centred, -1, keepdims=True)
    )


def norm_parts(values):
    middle = jnp.mean(values, -1, keepdims=True)
    spread = jnp.mean(values * values, -1, keepdims=True) - middle * middle
    inverse = lax.rsqrt(spread + EPSILON)
    return (values - middle) * inverse, inverse


def column_sums(values):
    return jnp.sum(values, 0, keepdims=True)


def attend_back_chunk(chunk, q, kv, grad, att, lse, dq, dkv, half, length):
    slots = pl.ds(chunk * 512, 512)
    for head in range(2):
        at = pl.ds(head * HEAD, HEAD)
        key, value = kv(0, slots, head), kv(1, slots, head)
        dkey, dvalue = jnp.zeros((512, HEAD), jnp.float32), jnp.zeros((512, HEAD), jnp.float32)
        for group in range(chunk, 4):
            rows = pl.ds(group * 256, 256)
            query, upstream = q(rows, head), grad[rows, at]
            delta = jnp.sum(upstream.astype(jnp.float32) * att[rows, at].astype(jnp.float32), -1, keepdims=True)
            scores = dot(query, key, NT) * SCALE
            slot = chunk * 512 + lax.broadcasted_iota(jnp.int32, (1, 512), 1)
            allowed = slot < length
            if group == chunk:
                allowed = allowed & (slot <= place_rows(group, half))
            probs = jnp.exp(jnp.where(allowed, scores - lse[head, rows, :], -HUGE))
            dscores = (probs * (dot(upstream, value, NT) - delta)).astype(LOW)
            share = dot(dscores, key, NN)
            if group == chunk:
                dq[rows, at] = share
            else:
                dq[rows, at] += share
            dkey += dot(dscores, query, TN)
            dvalue += dot(probs.astype(LOW), upstream, TN)
        dkv(0, slots, head, (dkey * SCALE).astype(LOW))
        dkv(1, slots, head, dvalue.astype(LOW))


def third_kernel(
    lengths, dy_in, wd_in, slope_in, wu_in, act_in, n2_in, mid_in, wide, wo_in, att_in, q_in, kv_in, lse_in,
    dqkv_out, dmid_out, gout_out, mixed_out, up_out, down_out, sums, lone,
    dy, wd, slope, wu, act, n2, mid, dmid, wo, att, datt, db, gout, lse, dq, dkv_inbox, mixed_own,
    terms, near, left, right, ends, down, down_line, down_total, down_side, down_last, down_grad, up, up_side, up_line, up_last,
    send, recv, local,
):
    net = Net(send, recv, local)
    length = lengths[(net.row // 2) % 2, net.row % 2]
    loads = [net.move(a, b) for a, b in ((wd_in, wd), (dy_in, dy), (act_in, act), (slope_in, slope), (wu_in, wu))]
    net.greet([net.at(dx=2)])
    loads += [net.move(a, b) for a, b in ((n2_in, n2), (mid_in, mid), (wo_in, wo), (att_in, att), (lse_in, lse))]
    back = ColReduce(net, terms, near, left, right, ends)
    all_db = ColGather(net, db)
    ffn = ColReduce(net, terms, near, left, right, ends)
    sum_down = LineFirst(net, down, down_line, down_total, down_side, down_last, 512)
    side_up = SideReduce(net, up, up_side, 96)
    line_up = LineReduce(net, up_side, up_line, up_last)
    keys = net.slots(8)

    def pair(dz):
        return part((net.z + dz) % 4 * 256, 256)

    def descend(dz):
        rows = pair(dz)

        def into_hidden(t):
            cols = part(t * 512, 512)
            grad = dot(dy[rows, :], wd[cols, :], NT)
            slope[rows, cols] = (grad * slope[rows, cols].astype(jnp.float32)).astype(LOW)

        def into_width(t):
            cols = part(t * 512, 512)
            terms[rows, cols] = dot(slope[rows, :], wu[cols, :], NT).astype(LOW)

        tiles(2, into_hidden)
        tiles(4, into_width)
        back.give(dz)

    def down_tile(r, t):
        return dot(act[:, part(t * 512, 512)], dy[:, part(r * 256, 256)], TN)

    def up_tile(r, t):
        return dot(n2[:, part(r * 256, 256)], slope[:, part(t * 512, 512)], TN)

    def down_give(which, dy):
        r = sum_down.owner(which, dy)

        def tile(t):
            down[which * 3 + dy - 1, part(t * 512, 512), :] = down_tile(r, t).astype(LOW)

        tiles(2, tile)
        sum_down.give(which, dy)

    def down_add(which):
        sum_down.take(which)
        r = sum_down.owner(which, 0)

        def tile(t):
            units = part(t * 512, 512)
            down_total[which, units, :] = (down_tile(r, t) + sum_down.arrived(which, units)).astype(LOW)

        tiles(2, tile)

    def up_give(step):
        r = side_up.other(step)

        def tile(t):
            up[step, :, part(t * 512, 512)] = up_tile(r, t).astype(LOW)

        tiles(2, tile)
        side_up.give(step)

    def up_add(step):
        side_up.take(step)
        r = side_up.mine(step)

        def tile(t):
            units = part(t * 512, 512)
            up_side[step, :, units] = (up_tile(r, t) + up_side[step, :, units].astype(jnp.float32)).astype(LOW)

        tiles(2, tile)

    def low_rank(dz):
        all_db.pair(dz)
        rows = pair(dz)
        datt[rows, :] = dot(db[rows, :], wo[...], NT).astype(LOW)

    for copy in loads[:3]:
        copy.wait()
    down_give(1, 1)
    down_give(1, 3)
    for copy in loads[3:5]:
        copy.wait()
    descend(2)
    descend(1)
    back.far()
    down_give(1, 2)
    descend(3)
    back.own(1)
    back.own(3)
    descend(0)
    key_loads = [net.move(kv_in.at[i], wu.at[:, pl.ds(i * 256, 256)]) for i in range(2)]
    for copy in loads[5:]:
        copy.wait()
    down_give(0, 1)
    back.forward(1)
    back.forward(3)
    down_give(0, 3)
    down_give(0, 2)
    up_give(0)
    up_give(1)
    back.finish()
    totals = [jnp.zeros((1, D), jnp.float32)] * 4
    for piece in range(4):
        rows = pl.ds(piece * 32, 32)
        own = part(net.col * OWN + piece * 32, 32)
        grad = back.result(piece * 32, 32)
        centred, inverse = norm_parts(mid[rows, :])
        upstream = dy[own, :].astype(jnp.float32)
        value = upstream + norm_back(grad, centred, inverse, wide[3:4, :])
        dmid[rows, :] = value
        low = value.astype(LOW)
        db[own, :] = low
        terms_of = (low.astype(jnp.float32), grad * centred, grad, upstream)
        totals = [a + column_sums(b) for a, b in zip(totals, terms_of)]
    all_db.begin()
    zero = jnp.zeros((2, D), jnp.float32)
    sums[...] = jnp.concatenate([zero, *totals, zero], 0)
    net.store(dmid, dmid_out)
    down_add(1)
    sum_down.sideways()
    back.flush()

    def ascend(t):
        cols = part(t * 512, 512)
        for i in range(2):
            rows = pl.ds(i * 512, 512)
            terms[rows, cols] = dot(act[rows, :], wd[:, cols], NN).astype(LOW)

    tiles(4, ascend)
    query_load = net.move(q_in, wd.at[:, pl.ds(0, 256)])
    up_give(2)
    up_give(3)
    all_db.pass_on()
    all_db.take_rest()
    low_rank(0)
    for dz in (2, 1, 3, 0):
        ffn.give(dz)
    ffn.far()
    all_db.far()
    for dz in (3, 1, 2):
        low_rank(dz)
    ffn.own(1)
    ffn.own(3)
    for copy in (*key_loads, query_load):
        copy.wait()

    def of_keys(which, slots, head):
        return wu[slots, pl.ds(which * 256 + head * HEAD, HEAD)]

    def of_queries(rows, head):
        return wd[rows, pl.ds(head * HEAD, HEAD)]

    def keep(which, slots, head, values):
        wu[slots, pl.ds(512 + which * 256 + head * HEAD, HEAD)] = values

    def attend_back(chunk):
        attend_back_chunk(chunk, of_queries, of_keys, datt, att, lse, dq, keep, net.half, length)
        for block in (chunk * 2, chunk * 2 + 1):
            theirs = part(block * 256 + (1 - net.half) * OWN, OWN)
            net.push(
                keys + block,
                wu.at[theirs, pl.ds(512, 512)],
                dkv_inbox.at[pl.ds(block * OWN, OWN)],
                net.partner(),
            )

    attend_back(3)
    up_add(1)
    line_up.give(1)
    attend_back(2)
    up_add(3)
    line_up.give(3)
    ffn.forward(1)
    ffn.forward(3)
    down_add(0)
    sum_down.close()
    attend_back(1)
    up_add(2)
    line_up.give(2)
    attend_back(0)

    def out_block(which):
        for dy in range(4):
            r = sum_down.owner(which, dy)
            place = (1 - which) * 4 + dy
            gout[place] = dot(att[...], db[:, part(r * 256, 256)], TN).astype(LOW)

    out_block(0)
    out_block(1)
    net.store(gout, gout_out)
    up_add(0)
    lone[:, pl.ds(0, 1024)] = dot(jnp.ones((8, 1024), LOW), slope[...], NN)
    for piece in range(4):
        rows = pl.ds(piece * 256, 256)
        wd[rows, pl.ds(256, 256)] = (dq[rows, :] * SCALE).astype(LOW)
    ffn.finish()
    for piece in range(4):
        rows = pl.ds(piece * 32, 32)
        mixed_own[rows, :] = (mid[rows, :] + ffn.result(piece * 32, 32) + wide[5:6, :]).astype(LOW)
    net.store(mixed_own, mixed_out)
    line_up.settle()
    net.store(up_side.at[0], up_out)
    for chunk in (3, 2, 1, 0):
        for block in (chunk * 2, chunk * 2 + 1):
            place = pl.ds(block * OWN, OWN)
            net.got(keys + block, dkv_inbox.at[place])
            mine = part(block * 256 + net.half * OWN, OWN)
            total = wu[mine, pl.ds(512, 512)].astype(jnp.float32) + dkv_inbox[place, :].astype(jnp.float32)
            wd[place, pl.ds(512, 512)] = total.astype(LOW)
    dqkv = wd.at[:, pl.ds(256, 768)]
    net.store(dqkv, dqkv_out)
    lone[:, pl.ds(1024, 768)] = dot(jnp.ones((8, 1024), LOW), wd[:, pl.ds(256, 768)], NN)
    sum_down.finish(emit_to(down_grad))
    net.store(down_grad, down_out)
    net.drain()


def third(lengths, dy, wd, slope, wu, act, n2, mid, wide, wo, att, q, kv, lse):
    return pl.pallas_call(
        third_kernel,
        out_shape=(
            low_shape(1024, 768),
            full_shape(OWN, D),
            low_shape(8, 256, 256),
            low_shape(OWN, D),
            low_shape(256, 1024),
            full_shape(1024, 256),
            full_shape(8, D),
            full_shape(8, 1792),
        ),
        in_specs=[SM] + [HBM] * 7 + [VM] + [HBM] * 5,
        out_specs=(HBM, HBM, HBM, HBM, HBM, HBM, VM, VM),
        scratch_shapes=[
            pltpu.VMEM((1024, D), LOW),
            pltpu.VMEM((1024, D), LOW),
            pltpu.VMEM((1024, 1024), LOW),
            pltpu.VMEM((D, 1024), LOW),
            pltpu.VMEM((1024, 1024), LOW),
            pltpu.VMEM((1024, D), LOW),
            pltpu.VMEM((OWN, D), jnp.float32),
            pltpu.VMEM((OWN, D), jnp.float32),
            pltpu.VMEM((256, D), LOW),
            pltpu.VMEM((1024, 256), LOW),
            pltpu.VMEM((1024, 256), LOW),
            pltpu.VMEM((1024, D), LOW),
            pltpu.VMEM((8, 256, 256), LOW),
            pltpu.VMEM((2, 1024, 1), jnp.float32),
            pltpu.VMEM((1024, 256), jnp.float32),
            pltpu.VMEM((1024, 512), LOW),
            pltpu.VMEM((OWN, D), LOW),
            *reduce_scratch(),
            pltpu.VMEM((6, 1024, 256), LOW),
            pltpu.VMEM((6, 1024, 256), LOW),
            pltpu.VMEM((2, 1024, 256), LOW),
            pltpu.VMEM((1024, 256), LOW),
            pltpu.VMEM((1024, 256), LOW),
            pltpu.VMEM((1024, 256), jnp.float32),
            pltpu.VMEM((4, 256, 1024), LOW),
            pltpu.VMEM((4, 256, 1024), LOW),
            pltpu.VMEM((3, 256, 1024), LOW),
            pltpu.VMEM((256, 1024), LOW),
            *sems(80, 32),
        ],
        compiler_params=pltpu.CompilerParams(
            collective_id=3, has_side_effects=True, vmem_limit_bytes=63 * 2**20
        ),
        cost_estimate=pl.CostEstimate(flops=40 * 10**9, bytes_accessed=30 * 10**6, transcendentals=2 * 10**6),
    )(lengths, dy, wd, slope, wu, act, n2, mid, wide, wo, att, q, kv, lse)


class Everyone:
    def __init__(self, net, axis, inbox):
        self.net, self.axis, self.inbox, self.slot = net, axis, inbox, net.slots(7)
        self.index = net.row if axis == "row" else net.col

    def device(self, shift):
        net, index = self.net, (self.index + shift) % 8
        row, col = (index, net.col) if self.axis == "row" else (net.row, index)
        return {"dp": net.dp, "row": row, "col": col}

    def begin(self, src_of):
        for shift in range(1, 8):
            to = (self.index + shift) % 8
            self.net.push(self.slot + shift - 1, src_of(to), self.inbox.at[self.index], self.device(shift))
        self.copy = self.net.move(src_of(self.index), self.inbox.at[self.index])

    def total(self):
        self.copy.wait()
        for shift in range(1, 8):
            self.net.got(self.slot + shift - 1, self.inbox.at[(self.index + 8 - shift) % 8])
        total = self.inbox[0]
        for i in range(1, 8):
            total += self.inbox[i]
        return total


class Blocks:
    def __init__(self, net, src, inbox):
        self.net, self.src, self.inbox, self.slot = net, src, inbox, net.slots(15)

    def begin(self):
        net = self.net
        place = self.inbox.at[net.dp * 8 + net.row]
        for shift in range(16):
            row = (net.row + shift) % 8
            block = self.src.at[:, part(row * 256, 256)]
            if shift == 0:
                self.copy = net.move(block, place)
            else:
                dp = net.dp if shift < 8 else 1 - net.dp
                net.push(self.slot + shift - 1, block, place, {"dp": dp, "row": row, "col": net.col})

    def total(self):
        net = self.net
        self.copy.wait()
        for shift in range(1, 16):
            dp = net.dp if shift < 8 else 1 - net.dp
            net.got(self.slot + shift - 1, self.inbox.at[dp * 8 + (net.row + 16 - shift) % 8])
        total = self.inbox[0]
        for i in range(1, 16):
            total += self.inbox[i]
        return total


def fourth_kernel(
    dqkv_in, n1_in, wq_in, x_in, dmid_in, wide, gout_in, mixed_in, up_in, sums, single,
    grad_low, mixed, qkv_grad, out_grad, up_grad, wide_grad, lone_grad,
    dqkv, n1, wq, x, dmid, grad_own, mixed_own, up, up_last, terms, near, left, right, ends,
    gout, gout_side, gout_line, gout_last, gqkv, gqkv_side, gqkv_line, gqkv_last,
    vector, wide_cols, wide_part, wide_rows, packed, single_rows, single_part, single_last,
    send, recv, local,
):
    net = Net(send, recv, local)
    load = {}
    for name, a, b in (
        ("dqkv", dqkv_in, dqkv), ("wq", wq_in, wq), ("n1", n1_in, n1), ("gout", gout_in, gout), ("up", up_in, up),
        ("mixed", mixed_in, mixed_own), ("x", x_in, x), ("dmid", dmid_in, dmid),
    ):
        load[name] = net.move(a, b)
    cols = [{"dp": net.dp, "row": net.row, "col": (net.col + d) % 8} for d in range(1, 8)]
    across = [{"dp": 1 - net.dp, "row": (net.row + d) % 8, "col": net.col} for d in (0, 1, 2, 3, 5, 6, 7)]
    net.greet(across, cols)
    back = ColReduce(net, terms, near, left, right, ends)
    side_qkv = SideReduce(net, gqkv, gqkv_side, 128)
    side_out = SideReduce(net, gout, gout_side, 128)
    line_out = LineReduce(net, gout_side, gout_line, gout_last)
    line_qkv = LineReduce(net, gqkv_side, gqkv_line, gqkv_last)
    wide_a, wide_b = Everyone(net, "col", wide_cols), Blocks(net, wide_part, wide_rows)
    single_a = Everyone(net, "row", single_rows)
    crossing = net.slots(2)

    def feature_block(ref):
        return lambda r: ref.at[:, part(r * 256, 256)]

    def token_block(ref):
        return lambda r: ref.at[(r // 2) % 2, r % 2, part(r // 4 * OWN, OWN)]

    mixed_swap = Swap(net, feature_block(mixed_own), token_block(mixed))
    grad_swap = Swap(net, feature_block(grad_own), token_block(grad_low))

    def descend(dz):
        rows = part((net.z + dz) % 4 * 256, 256)

        def tile(t):
            at = part(t * 512, 512)
            total = dot(dqkv[rows, pl.ds(0, 256)], wq[0, at, :], NT)
            for i in (1, 2):
                total += dot(dqkv[rows, pl.ds(i * 256, 256)], wq[i, at, :], NT)
            terms[rows, at] = total.astype(LOW)

        tiles(4, tile)
        back.give(dz)

    def qkv_tile(r):
        return dot(n1[:, part(r * 256, 256)], dqkv[...], TN)

    def qkv_give(dy):
        gqkv[dy] = qkv_tile(side_qkv.other(dy)).astype(LOW)
        side_qkv.give(dy)

    def qkv_add(dy):
        side_qkv.take(dy)
        gqkv_side[dy] = (qkv_tile(side_qkv.mine(dy)) + gqkv_side[dy].astype(jnp.float32)).astype(LOW)

    for name in ("dqkv", "wq", "n1"):
        load[name].wait()
    qkv_give(0)
    descend(2)
    qkv_give(1)
    descend(1)
    back.far()
    qkv_give(2)
    descend(3)
    back.own(1)
    back.own(3)
    qkv_give(3)
    descend(0)
    for i in range(7):
        packed[i : i + 1, :] = single[0:1, i * 256 : (i + 1) * 256]
    packed[7:8, :] = jnp.zeros((1, 256), jnp.float32)
    single_a.begin(lambda r: packed)
    load["gout"].wait()
    for dy in range(4):
        side_out.give(dy)
    back.forward(1)
    back.forward(3)
    for dy in (1, 2, 3):
        qkv_add(dy)
        line_qkv.give(dy)
    load["up"].wait()
    net.push(crossing + 1, up, up_last, net.at(dx=2))
    load["x"].wait()
    load["dmid"].wait()
    back.finish()
    totals = [jnp.zeros((1, D), jnp.float32)] * 2
    for piece in range(4):
        rows = pl.ds(piece * 32, 32)
        grad = back.result(piece * 32, 32)
        centred, inverse = norm_parts(x[rows, :].astype(jnp.float32))
        value = dmid[rows, :] + norm_back(grad, centred, inverse, wide[0:1, :])
        grad_own[rows, :] = value.astype(LOW)
        totals = [a + column_sums(b) for a, b in zip(totals, (grad * centred, grad))]
    vector[...] = sums[...] + jnp.concatenate([*totals, jnp.zeros((6, D), jnp.float32)], 0)
    wide_a.begin(lambda r: vector)
    grad_swap.begin()
    qkv_add(0)
    for dy in (1, 2, 3, 0):
        side_out.take(dy)
        gout_side[dy] = (gout[4 + dy].astype(jnp.float32) + gout_side[dy].astype(jnp.float32)).astype(LOW)
        if dy:
            line_out.give(dy)
    load["mixed"].wait()
    mixed_swap.begin()
    wide_part[...] = wide_a.total()
    wide_b.begin()
    single_part[...] = single_a.total()
    net.push(crossing, single_part, single_last, net.at(dx=2))
    line_qkv.close()
    line_out.close()
    net.got(crossing + 1, up_last)
    in_rows(up_last, lambda rows: emit_to(up_grad)(rows, up[rows, :].astype(jnp.float32) + up_last[rows, :].astype(jnp.float32)))
    mixed_swap.finish()
    grad_swap.finish()
    wide_grad[...] = wide_b.total()
    net.got(crossing, single_last)
    lone_grad[...] = single_part[...] + single_last[...]

    def emit_qkv(rows, values):
        for i in range(3):
            qkv_grad[i, rows, :] = values[:, i * 256 : (i + 1) * 256]

    line_qkv.finish(emit_qkv)
    line_out.finish(emit_to(out_grad))
    net.drain()


def fourth(dqkv, n1, wq, x, dmid, wide, gout, mixed, up, sums, lone):
    return pl.pallas_call(
        fourth_kernel,
        out_shape=(
            low_shape(2, 2, 256, 256),
            low_shape(2, 2, 256, 256),
            full_shape(3, 256, 256),
            full_shape(256, 256),
            full_shape(256, 1024),
            full_shape(8, 256),
            full_shape(8, 256),
        ),
        in_specs=[HBM, HBM, HBM, HBM, HBM, VM, HBM, HBM, HBM, VM, VM],
        out_specs=(VM,) * 7,
        scratch_shapes=[
            pltpu.VMEM((1024, 768), LOW),
            pltpu.VMEM((1024, D), LOW),
            pltpu.VMEM((3, D, 256), LOW),
            pltpu.VMEM((OWN, D), LOW),
            pltpu.VMEM((OWN, D), jnp.float32),
            pltpu.VMEM((OWN, D), LOW),
            pltpu.VMEM((OWN, D), LOW),
            pltpu.VMEM((256, 1024), LOW),
            pltpu.VMEM((256, 1024), LOW),
            *reduce_scratch(),
            pltpu.VMEM((8, 256, 256), LOW),
            pltpu.VMEM((4, 256, 256), LOW),
            pltpu.VMEM((3, 256, 256), LOW),
            pltpu.VMEM((256, 256), LOW),
            pltpu.VMEM((4, 256, 768), LOW),
            pltpu.VMEM((4, 256, 768), LOW),
            pltpu.VMEM((3, 256, 768), LOW),
            pltpu.VMEM((256, 768), LOW),
            pltpu.VMEM((8, D), jnp.float32),
            pltpu.VMEM((8, 8, D), jnp.float32),
            pltpu.VMEM((8, D), jnp.float32),
            pltpu.VMEM((16, 8, 256), jnp.float32),
            pltpu.VMEM((8, 256), jnp.float32),
            pltpu.VMEM((8, 8, 256), jnp.float32),
            pltpu.VMEM((8, 256), jnp.float32),
            pltpu.VMEM((8, 256), jnp.float32),
            *sems(112, 24),
        ],
        compiler_params=pltpu.CompilerParams(
            collective_id=4, has_side_effects=True, vmem_limit_bytes=60 * 2**20
        ),
        cost_estimate=pl.CostEstimate(flops=40 * 10**9, bytes_accessed=30 * 10**6, transcendentals=2 * 10**6),
    )(dqkv, n1, wq, x, dmid, wide, gout, mixed, up, sums, lone)


def hand_over_kernel(
    mixed_in, grad_in, qkv_in, out_in, up_in, down_in, wide, lone,
    mixed, input_grad, gain1, bias1, qkv, qv, out, out_bias, gain2, bias2, up, up_bias, down, down_bias,
    *rest,
):
    between, done = rest[:-1], rest[-1]
    pairs = ((down_in, down), (up_in, up), (qkv_in, qkv), (mixed_in, mixed), (out_in, out))
    fetches = [pltpu.make_async_copy(a, m, done.at[i]) for i, ((a, b), m) in enumerate(zip(pairs, between))]
    copies = [pltpu.make_async_copy(m, b, done.at[5 + i]) for i, ((a, b), m) in enumerate(zip(pairs, between))]
    for fetch in fetches:
        fetch.start()
    for fetch, copy in zip(fetches, copies):
        fetch.wait()
        copy.start()
    for i, ref in enumerate((gain1, bias1, out_bias, gain2, bias2, down_bias)):
        ref[...] = wide[i : i + 1, :]
    for i in range(4):
        up_bias[:, i * 256 : (i + 1) * 256] = lone[i : i + 1, :]
    qv[0:1, :] = lone[4:5, :]
    qv[1:2, :] = lone[6:7, :]
    for i in range(2):
        for j in range(2):
            input_grad[i, j] = grad_in[i, j].astype(jnp.float32)
    for copy in copies:
        copy.wait()


def hand_over(mixed, grad, qkv, out, up, down, wide, lone):
    vector = full_shape(1, 256)
    return pl.pallas_call(
        hand_over_kernel,
        out_shape=(
            low_shape(2, 2, 256, 256),
            full_shape(2, 2, 256, 256),
            vector,
            vector,
            full_shape(3, 256, 256),
            full_shape(2, 256),
            full_shape(256, 256),
            vector,
            vector,
            vector,
            full_shape(256, 1024),
            full_shape(1, 1024),
            full_shape(1024, 256),
            vector,
        ),
        in_specs=[HBM, VM, HBM, HBM, HBM, HBM, VM, VM],
        out_specs=(HBM, VM, VM, VM, HBM, VM, HBM, VM, VM, VM, HBM, VM, HBM, VM),
        scratch_shapes=[
            pltpu.VMEM((1024, 256), jnp.float32),
            pltpu.VMEM((256, 1024), jnp.float32),
            pltpu.VMEM((3, 256, 256), jnp.float32),
            pltpu.VMEM((2, 2, 256, 256), LOW),
            pltpu.VMEM((256, 256), jnp.float32),
            pltpu.SemaphoreType.DMA((10,)),
        ],
        compiler_params=pltpu.CompilerParams(vmem_limit_bytes=63 * 2**20),
    )(mixed, grad, qkv, out, up, down, wide, lone)


def shards(
    inputs,
    lengths,
    ln1_gain,
    ln1_bias,
    w_qkv,
    qv_bias,
    w_out,
    out_bias,
    ln2_gain,
    ln2_bias,
    w_up,
    up_bias,
    w_down,
    down_bias,
    cotangent,
):
    small = [a.reshape(1, 256) for a in (ln1_gain, ln1_bias, out_bias, ln2_gain, ln2_bias, down_bias)]
    x, all_dy, all1, q, kv, att, lse, wq, wo, wide, mid, all2, act, slope, wu, wd = ahead(
        lengths, inputs, cotangent, small, w_qkv, w_out, w_up, w_down, qv_bias, up_bias.reshape(1, 1024)
    )
    dqkv, dmid, gout, mixed, up, g_down, sums, lone = third(
        lengths, all_dy, wd, slope, wu, act, all2, mid, wide, wo, att, q, kv, lse
    )
    grad, mixed, g_qkv, g_out, g_up, wide_grad, lone_grad = fourth(
        dqkv, all1, wq, x, dmid, wide, gout, mixed, up, sums, lone
    )
    outs = hand_over(mixed, grad, g_qkv, g_out, g_up, g_down, wide_grad, lone_grad)
    return tuple(a.reshape(-1) if a.shape[0] == 1 else a for a in outs)


def solution(mesh):
    tokens = P(None, "dp", "col", "row")
    in_specs = (
        tokens,
        P(None, "dp"),
        P("row"),
        P("row"),
        P(None, "row", "col"),
        P(None, "col"),
        P("col", "row"),
        P("row"),
        P("row"),
        P("row"),
        P("row", "col"),
        P("col"),
        P("col", "row"),
        P("row"),
        tokens,
    )
    out_specs = (
        tokens,
        tokens,
        P("row"),
        P("row"),
        P(None, "row", "col"),
        P(None, "col"),
        P("col", "row"),
        P("row"),
        P("row"),
        P("row"),
        P("row", "col"),
        P("col"),
        P("col", "row"),
        P("row"),
    )
    return jax.shard_map(shards, mesh=mesh, in_specs=in_specs, out_specs=out_specs, check_vma=False)
```

```python
import functools

import jax
import jax.numpy as jnp
from jax import lax
from jax.experimental import pallas as pl
from jax.experimental.pallas import tpu as pltpu
from jax.sharding import PartitionSpec as P

D = 2048
HEAD = 128
SCALE = HEAD**-0.5
EPSILON = 1e-05
HUGE = 1e30
LOW = jnp.bfloat16
OWN = 128
VMEM_LIMIT = 56 * 2**20


def dot(a, b, contract):
    return lax.dot_general(a, b, ((contract[0], contract[1]), ((), ())), preferred_element_type=jnp.float32)


NN = ((1,), (0,))
NT = ((1,), (1,))
TN = ((0,), (0,))


def place_rows(group, half):
    row = lax.broadcasted_iota(jnp.int32, (256, 1), 0)
    return (2 * group + row // OWN) * 256 + half * OWN + row % OWN


def allowed_keys(group, extent, half, length):
    slot = lax.broadcasted_iota(jnp.int32, (256, extent), 1)
    return (slot <= place_rows(group, half)) & (slot < length)


MESH = pl.DeviceIdType.MESH
HBM = pl.BlockSpec(memory_space=pl.ANY)
VM = pl.BlockSpec(memory_space=pltpu.VMEM)
SM = pl.BlockSpec(memory_space=pltpu.SMEM)


def part(start, size):
    return pl.ds(pl.multiple_of(start, size), size)


class Net:
    def __init__(self, send, recv, local):
        self.send, self.recv, self.local = send, recv, local
        self.used, self.local_used, self.live, self.own = 0, 0, [], []
        self.dp, self.row, self.col = (lax.axis_index(a) for a in ("dp", "row", "col"))
        self.half, self.y = self.row // 4, self.row % 4
        self.x = self.dp * 2 + self.half
        self.z, self.core = self.col // 2, self.col % 2

    def at(self, dx=0, dy=0, dz=0, other_core=False):
        x, y, z = (self.x + dx) % 4, (self.y + dy) % 4, (self.z + dz) % 4
        core = 1 - self.core if other_core else self.core
        return {"dp": x // 2, "row": (x % 2) * 4 + y, "col": z * 2 + core}

    def mate(self, shift):
        return {"dp": self.dp, "row": (self.row + shift) % 8, "col": self.col}

    def partner(self):
        return self.mate(4)

    def cousin(self):
        return {"dp": 1 - self.dp, "row": (self.row + 4) % 8, "col": self.col}

    def greet(self, more=(), cols=()):
        devices = [self.mate(d) for d in range(1, 8)]
        devices += [self.cousin()]
        devices += cols or [self.at(dz=1), self.at(dz=3), self.at(other_core=True)]
        devices += more
        barrier = pltpu.get_barrier_semaphore()
        for device in devices:
            pl.semaphore_signal(barrier, inc=1, device_id=device, device_id_type=MESH)
        pl.semaphore_wait(barrier, len(devices))

    def slots(self, count):
        self.used += count
        return self.used - count

    def _copy(self, slot, src, dst, device):
        return pltpu.make_async_remote_copy(
            src_ref=src,
            dst_ref=dst,
            send_sem=self.send.at[slot],
            recv_sem=self.recv.at[slot],
            device_id=device,
            device_id_type=MESH,
        )

    def push(self, slot, src, dst, device):
        copy = self._copy(slot, src, dst, device)
        copy.start()
        self.live.append(copy)

    def got(self, slot, ref):
        self._copy(slot, ref, ref, self.at(other_core=True)).wait_recv()

    def flush(self, copies):
        for copy in copies:
            copy.wait_send()
        self.live = [copy for copy in self.live if not any(copy is other for other in copies)]

    def move(self, src, dst):
        copy = pltpu.make_async_copy(src, dst, self.local.at[self.local_used])
        self.local_used += 1
        copy.start()
        return copy

    def store(self, src, dst):
        self.own.append(self.move(src, dst))

    def drain(self):
        for copy in self.live:
            copy.wait_send()
        for copy in self.own:
            copy.wait()


class ColGather:
    def __init__(self, net, buf):
        self.net, self.buf, self.slot = net, buf, net.slots(14)
        self.sent = []

    def rows(self, dz, other_core, piece):
        net = self.net
        core = 1 - net.core if other_core else net.core
        return self.buf.at[part(((net.z + dz) % 4 * 2 + core) * OWN + 64 * piece, 64)]

    def move(self, slot, where, piece, **to):
        ref = self.rows(where, False, piece)
        self.net.push(self.slot + slot, ref, ref, self.net.at(**to))
        self.sent.append(self.net.live[-1])

    def flush(self):
        self.net.flush(self.sent)

    def got(self, slot, dz, piece, other_core=False):
        self.net.got(self.slot + slot, self.rows(dz, other_core, piece))

    def begin(self):
        self.move(0, 0, 0, dz=1)
        self.move(3, 0, 1, dz=3)
        self.move(1, 0, 1, dz=1)
        self.move(2, 0, 0, dz=3)
        self.move(6, 0, 0, other_core=True)
        self.move(7, 0, 1, other_core=True)

    def hop(self):
        self.pass_on()
        self.take_rest()

    def pass_on(self):
        self.got(0, 3, 0)
        self.move(4, 3, 0, dz=1)
        self.got(3, 1, 1)
        self.move(5, 1, 1, dz=3)
        self.move(8, 3, 0, other_core=True)
        self.move(11, 1, 1, other_core=True)

    def take_rest(self):
        self.got(1, 3, 1)
        self.move(9, 3, 1, other_core=True)
        self.got(2, 1, 0)
        self.move(10, 1, 0, other_core=True)

    def far(self):
        self.got(4, 2, 0)
        self.move(12, 2, 0, other_core=True)
        self.got(5, 2, 1)
        self.move(13, 2, 1, other_core=True)

    def pair(self, dz):
        slot = {0: 6, 3: 8, 1: 10, 2: 12}[dz]
        self.got(slot, dz, 0, True)
        self.got(slot + 1, dz, 1, True)


class RowGather:
    def __init__(self, net, src, buf, whole, parts):
        self.net, self.src, self.buf, self.whole, self.parts = net, src, buf, whole, parts
        self.slot, self.sent = net.slots(11), []

    def place(self, dy, other=False):
        net = self.net
        half = 1 - net.half if other else net.half
        return self.whole(self.buf, half * 4 + (net.y + dy) % 4)

    def sideways(self, dy, src, sides=(0, 1)):
        net, there = self.net, self.place(dy)
        devices = (net.partner(), net.cousin())
        for side in sides:
            net.push(
                self.slot + 3 + dy * 2 + side, self.parts(src, side), self.parts(there, side), devices[side]
            )
            self.sent.append(net.live[-1])

    def flush(self):
        self.net.flush(self.sent)

    def begin(self):
        net, mine = self.net, self.place(0)
        for dy in (1, 3, 2):
            net.push(self.slot + dy - 1, self.src, mine, net.at(dy=dy))
            self.sent.append(net.live[-1])
        self.copy = net.move(self.src, mine)

    def begin_sideways(self, sides=(0, 1)):
        self.sideways(0, self.src, sides)

    def step(self, dy, sides=(0, 1)):
        ref = self.place(4 - dy)
        self.net.got(self.slot + dy - 1, ref)
        self.sideways(4 - dy, ref, sides)

    def follow(self, dy, sides):
        self.sideways(4 - dy, self.place(4 - dy), sides)

    def steps(self):
        for dy in (1, 3, 2):
            self.step(dy)

    def finish(self):
        self.copy.wait()
        for dy in range(4):
            for side in range(2):
                self.net.got(self.slot + 3 + dy * 2 + side, self.parts(self.place(dy, True), side))


def cut(rows):
    def parts(ref, side):
        total = ref.shape[-2]
        window = pl.ds(0, rows) if side == 0 else pl.ds(rows, total - rows)
        return ref.at[:, window] if len(ref.shape) == 3 else ref.at[window]

    return parts


class Swap:
    def __init__(self, net, src_of, dst_of):
        self.net, self.src_of, self.dst_of, self.slot = net, src_of, dst_of, net.slots(7)

    def begin(self):
        net = self.net
        for shift in range(1, 8):
            net.push(self.slot + shift - 1, self.src_of((net.row + shift) % 8), self.dst_of(net.row), net.mate(shift))
        self.copy = net.move(self.src_of(net.row), self.dst_of(net.row))

    def finish(self):
        net = self.net
        self.copy.wait()
        for shift in range(1, 8):
            net.got(self.slot + shift - 1, self.dst_of((net.row + 8 - shift) % 8))


def norm_rows(values, gain, bias):
    middle = jnp.mean(values, -1, keepdims=True)
    spread = jnp.mean(values * values, -1, keepdims=True) - middle * middle
    inverse = lax.rsqrt(spread + EPSILON)
    centred = (values - middle) * inverse
    return centred * gain + bias


def attend_group(q, kv, head, group, half, length):
    cols, rows, extent = pl.ds(head * HEAD, HEAD), pl.ds(group * 256, 256), 512 * (group + 1)
    scores = dot(q[rows, cols], kv[0, :extent, cols], NT) * SCALE
    scores = jnp.where(allowed_keys(group, extent, half, length), scores, -HUGE)
    highest = jnp.max(scores, -1, keepdims=True)
    weights = jnp.exp(scores - highest)
    total = jnp.sum(weights, -1, keepdims=True)
    out = dot(weights.astype(LOW), kv[1, :extent, cols], NN) / total
    return out, highest + jnp.log(total)


def low_shape(*shape):
    return jax.ShapeDtypeStruct(shape, LOW)


def full_shape(*shape):
    return jax.ShapeDtypeStruct(shape, jnp.float32)


def sems(remote, local):
    return [
        pltpu.SemaphoreType.DMA((remote,)),
        pltpu.SemaphoreType.DMA((remote,)),
        pltpu.SemaphoreType.DMA((local,)),
    ]


class ColReduce:
    def __init__(self, net, terms, near, left, right, ends):
        self.net, self.terms, self.near, self.left, self.right, self.ends = net, terms, near, left, right, ends
        self.slot = net.slots(10)
        self.sent = []

    def push(self, *copy):
        self.net.push(*copy)
        self.sent.append(self.net.live[-1])

    def flush(self):
        self.net.flush(self.sent)

    def block(self, dz, other_core=False):
        net = self.net
        core = 1 - net.core if other_core else net.core
        return part(((net.z + dz) % 4 * 2 + core) * OWN, OWN)

    def rows(self, dz, piece):
        net = self.net
        return part(((net.z + dz) % 4 * 2 + net.core) * OWN + 64 * piece, 64)

    def give(self, dz):
        self.push(
            self.slot + dz, self.terms.at[self.block(dz, True)], self.near.at[pl.ds(dz * OWN, OWN)], self.net.at(other_core=True)
        )

    def fold(self, dz):
        near = self.near.at[pl.ds(dz * OWN, OWN)]
        self.net.got(self.slot + dz, near)
        block = self.block(dz)
        self.terms[block, :] = (self.terms[block, :].astype(jnp.float32) + near[...].astype(jnp.float32)).astype(LOW)

    def send(self, slot, dz, piece, dst, side):
        self.push(self.slot + slot, self.terms.at[self.rows(dz, piece)], dst, self.net.at(dz=side))

    def far(self):
        self.fold(2)
        self.send(4, 2, 0, self.left, 1)
        self.send(5, 2, 1, self.right, 3)

    def own(self, dz):
        self.fold(dz)
        side = 0 if dz == 1 else 1
        self.send(6 + side * 2 + 1 - side, dz, 1 - side, self.ends.at[side, pl.ds((1 - side) * 64, 64)], dz)

    def forward(self, dz):
        side = 0 if dz == 1 else 1
        inbox = self.left if dz == 1 else self.right
        self.net.got(self.slot + 4 + side, inbox)
        rows = self.rows(dz, side)
        self.terms[rows, :] = (self.terms[rows, :].astype(jnp.float32) + inbox[...].astype(jnp.float32)).astype(LOW)
        self.send(6 + side * 2 + side, dz, side, self.ends.at[side, pl.ds(side * 64, 64)], dz)

    def finish(self):
        self.net.got(self.slot, self.near.at[pl.ds(0, OWN)])
        for side in range(2):
            for piece in range(2):
                self.net.got(self.slot + 6 + side * 2 + piece, self.ends.at[side, pl.ds(piece * 64, 64)])

    def result(self, start, size):
        block = part(self.net.col * OWN + start, size)
        total = self.terms[block, :].astype(jnp.float32) + self.near[pl.ds(start, size), :].astype(jnp.float32)
        for side in range(2):
            total += self.ends[side, pl.ds(start, size), :].astype(jnp.float32)
        return total


def reduce_scratch():
    return [
        pltpu.VMEM((1024, D), LOW),
        pltpu.VMEM((4 * OWN, D), LOW),
        pltpu.VMEM((64, D), LOW),
        pltpu.VMEM((64, D), LOW),
        pltpu.VMEM((2, OWN, D), LOW),
    ]


def tiles(count, body):
    lax.fori_loop(0, count, lambda t, c: (body(t), c)[1], 0)


def ahead_kernel(
    lengths, inputs, cotangent, gain1, bias1, bias_out, gain2, bias2, bias_down, w_qkv, w_out, w_up, w_down, qv_bias, up_bias,
    x_out, n1_out, wq_out, small_out, dqkv_out, dmid_out, gout_out, mixed_out, up_out, down_out, sums, lone,
    x, dy, n1, q, kv, att, wq, wo, wide,
    terms, near, left, right, ends, mid, n2, act, slope, wu, wd, small, lse,
    datt, dq, dkv_inbox, dmid, down_side, down_line, down_last, up, up_side, up_line, up_last,
    send, recv, local,
):
    net = Net(send, recv, local)
    for i, ref in enumerate((gain1, bias1, bias_out, gain2, bias2, bias_down)):
        small[i : i + 1, :] = ref[...]
    small[6:8, :] = jnp.zeros((2, 256), jnp.float32)
    length = lengths[(net.row // 2) % 2, net.row % 2]
    net.greet([net.at(dx=2)])
    mine = part(net.col * OWN, OWN)

    def token_block(ref):
        return lambda r: ref.at[(r // 2) % 2, r % 2, part(r // 4 * OWN, OWN)]

    def feature_block(ref):
        return lambda r: ref.at[:, part(r * 256, 256)]

    def by_columns(ref, r):
        return ref.at[:, part(r * 256, 256)]

    def by_rows(ref, r):
        return ref.at[part(r * 256, 256)]

    params = Swap(net, lambda r: small, feature_block(wide))
    tokens = Swap(net, token_block(inputs), feature_block(x))
    upstream = Swap(net, token_block(cotangent), lambda r: dy.at[mine, part(r * 256, 256)])
    gather_kv = RowGather(net, w_qkv.at[pl.ds(1, 2)], wq.at[pl.ds(1, 2)], by_columns, cut(128))
    gather_q = RowGather(net, w_qkv.at[pl.ds(0, 1)], wq.at[pl.ds(0, 1)], by_columns, cut(32))
    gather_wo = RowGather(net, w_out, wo, by_columns, cut(16))
    gather_wu = RowGather(net, w_up, wu, by_rows, cut(128))
    gather_wd = RowGather(net, w_down, wd, by_columns, cut(512))
    all_n1, all_dy, all_n2 = ColGather(net, n1), ColGather(net, dy), ColGather(net, n2)
    branch = ColReduce(net, terms, near, left, right, ends)
    keys = net.slots(16)

    def pair(dz):
        return part((net.z + dz) % 4 * 256, 256)

    def project_keys(dz):
        all_n1.pair(dz)
        block = (net.z + dz) % 4
        values = n1[pair(dz), :]
        k = dot(values, wq[1], NN).astype(LOW)
        v = (dot(values, wq[2], NN) + qv_bias[1:2, :]).astype(LOW)
        for i in range(2):
            there = part((block * 2 + i) * 256 + net.half * OWN, OWN)
            kv[0, there, :] = k[i * OWN : (i + 1) * OWN]
            kv[1, there, :] = v[i * OWN : (i + 1) * OWN]

    def key_block(dz, i, half, head):
        there = part(((net.z + dz) % 4 * 2 + i) * 256 + half * OWN, OWN)
        return kv.at[:, there, pl.ds(head * HEAD, HEAD)]

    def swap_keys(dz, head):
        for i in range(2):
            ref = key_block(dz, i, net.half, head)
            net.push(keys + head * 8 + dz * 2 + i, ref, ref, net.partner())

    def take_keys(dz, head):
        for i in range(2):
            net.got(keys + head * 8 + dz * 2 + i, key_block(dz, i, 1 - net.half, head))

    def second_head(group, half, act_on):
        for i in range(2):
            place = part((group * 2 + i) * 256 + half * OWN, OWN)
            ref = kv.at[:, place, pl.ds(HEAD, HEAD)]
            act_on(keys + 8 + group * 2 + i, ref)

    params.begin()
    tokens.begin()
    gather_kv.begin()
    gather_kv.begin_sideways()
    params.finish()
    tokens.finish()
    for piece in range(4):
        rows = pl.ds(piece * 32, 32)
        low = norm_rows(x[rows, :].astype(jnp.float32), wide[0:1, :], wide[1:2, :]).astype(LOW)
        n1[part(net.col * OWN + piece * 32, 32), :] = low
    all_n1.begin()
    keep_x = net.move(x, x_out)
    net.store(wide, small_out)
    all_n1.pass_on()
    gather_kv.steps()
    gather_q.begin()
    gather_q.begin_sideways()
    all_n1.take_rest()
    upstream.begin()
    gather_kv.finish()
    for dz in (0, 3, 1):
        project_keys(dz)
        swap_keys(dz, 0)
    all_n1.far()
    project_keys(2)
    swap_keys(2, 0)
    gather_wo.begin()
    gather_wo.begin_sideways()
    gather_wu.begin()
    gather_wd.begin()
    upstream.finish()
    all_dy.begin()
    gather_q.steps()
    gather_wu.begin_sideways((1,))
    all_dy.pass_on()
    take_keys(0, 0)
    take_keys(3, 0)
    for group in range(4):
        second_head(group, net.half, lambda slot, ref: net.push(slot, ref, ref, net.partner()))
    gather_q.finish()

    def project_queries(t):
        rows = part(t * 256, 256)
        q[rows, :] = (dot(n1[rows, :], wq[0], NN) + qv_bias[0:1, :]).astype(LOW)

    tiles(4, project_queries)
    def attend(head):
        if head == 0:
            take_keys(1, 0)
            take_keys(2, 0)
        for group in range(4):
            if head:
                second_head(group, 1 - net.half, net.got)
            out, logsum = attend_group(q, kv, head, group, net.half, length)
            rows = pl.ds(group * 256, 256)
            att[rows, pl.ds(head * HEAD, HEAD)] = out.astype(LOW)
            lse[rows, pl.ds(head, 1)] = logsum

    gather_wo.steps()
    attend(0)
    all_dy.take_rest()
    all_dy.far()
    attend(1)
    gather_wu.begin_sideways((0,))
    gather_wo.finish()

    def project(dz):
        rows = pair(dz)

        def tile(t):
            cols = part(t * 512, 512)
            terms[rows, cols] = dot(att[rows, :], wo[:, cols], NN).astype(LOW)

        tiles(4, tile)
        branch.give(dz)

    project(2)
    project(1)
    branch.far()
    project(3)
    branch.own(1)
    branch.own(3)
    project(0)
    gather_wu.step(1)
    gather_wu.step(3)
    branch.forward(1)
    branch.forward(3)
    gather_wu.step(2)
    keep_n1 = net.move(n1, n1_out)
    keep_wq = net.move(wq, wq_out)
    branch.finish()
    for piece in range(4):
        rows = pl.ds(piece * 32, 32)
        total = x[rows, :].astype(jnp.float32) + branch.result(piece * 32, 32) + wide[2:3, :]
        mid[rows, :] = total
        low = norm_rows(total, wide[3:4, :], wide[4:5, :]).astype(LOW)
        n2[part(net.col * OWN + piece * 32, 32), :] = low
    for copy in (keep_x, keep_n1, keep_wq):
        copy.wait()
    gather_kv.flush()
    gather_q.flush()
    all_n1.flush()
    all_n2.begin()
    gather_wd.begin_sideways()
    gather_wd.step(1)
    gather_wd.step(3)
    gather_wu.finish()

    def ascend(dz):
        all_n2.pair(dz)
        rows = pair(dz)

        def tile(t):
            cols = part(t * 256, 256)
            hidden = dot(n2[rows, :], wu[:, cols], NN) + up_bias[:, cols]
            share = 0.5 + 0.5 * lax.erf(hidden * 0.5**0.5)
            act[rows, cols] = (hidden * share).astype(LOW)
            density = jnp.exp(-0.5 * hidden * hidden) * (0.5 / jnp.pi) ** 0.5
            slope[rows, cols] = (share + hidden * density).astype(LOW)

        tiles(4, tile)

    ascend(0)
    all_n2.pass_on()
    gather_wd.step(2)
    all_n2.take_rest()
    ascend(3)
    for dz in range(4):
        all_dy.pair(dz)
    all_n2.far()
    ascend(1)
    ascend(2)
    gather_wd.finish()
    back = ColReduce(net, terms, near, left, right, ends)
    all_db, db = ColGather(net, n1), n1
    ffn = ColReduce(net, terms, near, left, right, ends)
    side_down = SideReduce(net, lambda dy: wq.at[dy // 2, pl.ds(dy % 2 * 1024, 1024)], down_side, 512)
    line_down = LineReduce(net, down_side, down_line, down_last)
    side_up = SideReduce(net, lambda dy: up.at[dy], up_side, 96)
    line_up = LineReduce(net, up_side, up_line, up_last)
    key_grads = net.slots(8)

    def descend(dz):
        rows = pair(dz)

        def into_hidden(t):
            cols = part(t * 512, 512)
            grad = dot(dy[rows, :], wd[cols, :], NT)
            slope[rows, cols] = (grad * slope[rows, cols].astype(jnp.float32)).astype(LOW)

        def into_width(t):
            cols = part(t * 512, 512)
            terms[rows, cols] = dot(slope[rows, :], wu[cols, :], NT).astype(LOW)

        tiles(2, into_hidden)
        tiles(4, into_width)
        back.give(dz)

    def down_tile(r, t):
        return dot(act[:, part(t * 512, 512)], dy[:, part(r * 256, 256)], TN)

    def up_tile(r, t):
        return dot(n2[:, part(r * 256, 256)], slope[:, part(t * 512, 512)], TN)

    def down_give(step):
        r = side_down.other(step)

        def tile(t):
            wq[step // 2, part(step % 2 * 1024 + t * 512, 512), :] = down_tile(r, t).astype(LOW)

        tiles(2, tile)
        side_down.give(step)

    def down_add(step):
        side_down.take(step)
        r = side_down.mine(step)

        def tile(t):
            units = part(t * 512, 512)
            down_side[step, units, :] = (down_tile(r, t) + down_side[step, units, :].astype(jnp.float32)).astype(LOW)

        tiles(2, tile)

    def up_give(step):
        r = side_up.other(step)

        def tile(t):
            up[step, :, part(t * 512, 512)] = up_tile(r, t).astype(LOW)

        tiles(2, tile)
        side_up.give(step)

    def up_add(step):
        side_up.take(step)
        r = side_up.mine(step)

        def tile(t):
            units = part(t * 512, 512)
            up_side[step, :, units] = (up_tile(r, t) + up_side[step, :, units].astype(jnp.float32)).astype(LOW)

        tiles(2, tile)

    def low_rank(dz):
        all_db.pair(dz)
        rows = pair(dz)
        datt[rows, :] = dot(db[rows, :], wo[...], NT).astype(LOW)

    branch.flush()
    down_give(0)
    down_give(1)
    descend(2)
    descend(1)
    back.far()
    down_give(2)
    descend(3)
    back.own(1)
    back.own(3)
    descend(0)
    down_give(3)
    back.forward(1)
    back.forward(3)
    for step in (1, 2):
        down_add(step)
        line_down.give(step)
    for step in range(4):
        up_give(step)
    back.finish()
    totals = [jnp.zeros((1, D), jnp.float32)] * 4
    for piece in range(4):
        rows = pl.ds(piece * 32, 32)
        own = part(net.col * OWN + piece * 32, 32)
        grad = back.result(piece * 32, 32)
        centred, inverse = norm_parts(mid[rows, :])
        upstream = dy[own, :].astype(jnp.float32)
        value = upstream + norm_back(grad, centred, inverse, wide[3:4, :])
        dmid[rows, :] = value
        low = value.astype(LOW)
        db[own, :] = low
        terms_of = (low.astype(jnp.float32), grad * centred, grad, upstream)
        totals = [a + column_sums(b) for a, b in zip(totals, terms_of)]
    all_db.begin()
    zero = jnp.zeros((2, D), jnp.float32)
    sums[...] = jnp.concatenate([zero, *totals, zero], 0)
    net.store(dmid, dmid_out)
    down_add(3)
    line_down.give(3)
    back.flush()

    def mix(t):
        cols = part(t * 512, 512)
        for i in range(2):
            rows = pl.ds(i * 512, 512)
            terms[rows, cols] = dot(act[rows, :], wd[:, cols], NN).astype(LOW)

    tiles(4, mix)
    all_db.pass_on()
    all_db.take_rest()
    down_add(0)
    low_rank(0)
    for dz in (2, 1, 3, 0):
        ffn.give(dz)
    ffn.far()
    all_db.far()
    for dz in (3, 1, 2):
        low_rank(dz)
    ffn.own(1)
    ffn.own(3)
    def of_keys(which, slots, head):
        return kv[which, slots, pl.ds(head * HEAD, HEAD)]

    def of_queries(rows, head):
        return q[rows, pl.ds(head * HEAD, HEAD)]

    gather_wu.flush()
    gather_wd.flush()
    def keep(which, slots, head, values):
        wu[slots, pl.ds(512 + which * 256 + head * HEAD, HEAD)] = values

    def attend_back(chunk):
        attend_back_chunk(chunk, of_queries, of_keys, datt, att, lse, dq, keep, net.half, length)
        for block in (chunk * 2, chunk * 2 + 1):
            theirs = part(block * 256 + (1 - net.half) * OWN, OWN)
            net.push(
                key_grads + block,
                wu.at[theirs, pl.ds(512, 512)],
                dkv_inbox.at[pl.ds(block * OWN, OWN)],
                net.partner(),
            )

    attend_back(3)
    line_down.settle()
    net.store(down_side.at[0], down_out)
    up_add(1)
    line_up.give(1)
    attend_back(2)
    ffn.forward(1)
    ffn.forward(3)
    attend_back(1)
    up_add(3)
    line_up.give(3)
    attend_back(0)
    up_add(2)
    line_up.give(2)

    def out_block(which):
        for dy in range(4):
            r = side_down.other(dy) if which else side_down.mine(dy)
            place = (1 - which) * 4 + dy
            wq[2, pl.ds(place * 256, 256), :] = dot(att[...], db[:, part(r * 256, 256)], TN).astype(LOW)

    out_block(0)
    out_block(1)
    net.store(wq.at[2], gout_out)
    up_add(0)
    lone[:, pl.ds(0, 1024)] = dot(jnp.ones((8, 1024), LOW), slope[...], NN)
    for piece in range(4):
        rows = pl.ds(piece * 256, 256)
        wd[rows, pl.ds(256, 256)] = (dq[rows, :] * SCALE).astype(LOW)
    ffn.finish()
    for piece in range(4):
        rows = pl.ds(piece * 32, 32)
        x[rows, :] = (mid[rows, :] + ffn.result(piece * 32, 32) + wide[5:6, :]).astype(LOW)
    net.store(x, mixed_out)
    line_up.settle()
    net.store(up_side.at[0], up_out)
    for chunk in (3, 2, 1, 0):
        for block in (chunk * 2, chunk * 2 + 1):
            place = pl.ds(block * OWN, OWN)
            net.got(key_grads + block, dkv_inbox.at[place])
            mine = part(block * 256 + net.half * OWN, OWN)
            total = wu[mine, pl.ds(512, 512)].astype(jnp.float32) + dkv_inbox[place, :].astype(jnp.float32)
            wd[place, pl.ds(512, 512)] = total.astype(LOW)
    dqkv = wd.at[:, pl.ds(256, 768)]
    net.store(dqkv, dqkv_out)
    lone[:, pl.ds(1024, 768)] = dot(jnp.ones((8, 1024), LOW), wd[:, pl.ds(256, 768)], NN)
    net.drain()


def ahead(lengths, inputs, cotangent, small, w_qkv, w_out, w_up, w_down, qv_bias, up_bias):
    return pl.pallas_call(
        ahead_kernel,
        out_shape=(
            low_shape(OWN, D),
            low_shape(1024, D),
            low_shape(3, D, 256),
            full_shape(8, D),
            low_shape(1024, 768),
            full_shape(OWN, D),
            low_shape(2048, 256),
            low_shape(OWN, D),
            low_shape(256, 1024),
            low_shape(1024, 256),
            full_shape(8, D),
            full_shape(8, 1792),
        ),
        in_specs=[SM, HBM, HBM, *[VM] * 6, HBM, HBM, HBM, HBM, VM, VM],
        out_specs=(HBM,) * 10 + (VM, VM),
        scratch_shapes=[
            pltpu.VMEM((OWN, D), LOW),
            pltpu.VMEM((1024, D), LOW),
            pltpu.VMEM((1024, D), LOW),
            pltpu.VMEM((1024, 256), LOW),
            pltpu.VMEM((2, 2048, 256), LOW),
            pltpu.VMEM((1024, 256), LOW),
            pltpu.VMEM((3, D, 256), LOW),
            pltpu.VMEM((256, D), LOW),
            pltpu.VMEM((8, D), jnp.float32),
            *reduce_scratch(),
            pltpu.VMEM((OWN, D), jnp.float32),
            pltpu.VMEM((1024, D), LOW),
            pltpu.VMEM((1024, 1024), LOW),
            pltpu.VMEM((1024, 1024), LOW),
            pltpu.VMEM((D, 1024), LOW),
            pltpu.VMEM((1024, D), LOW),
            pltpu.VMEM((8, 256), jnp.float32),
            pltpu.VMEM((1024, 2), jnp.float32),
            pltpu.VMEM((1024, 256), LOW),
            pltpu.VMEM((1024, 256), jnp.float32),
            pltpu.VMEM((1024, 512), LOW),
            pltpu.VMEM((OWN, D), jnp.float32),
            pltpu.VMEM((4, 1024, 256), LOW),
            pltpu.VMEM((3, 1024, 256), LOW),
            pltpu.VMEM((1024, 256), LOW),
            pltpu.VMEM((4, 256, 1024), LOW),
            pltpu.VMEM((4, 256, 1024), LOW),
            pltpu.VMEM((3, 256, 1024), LOW),
            pltpu.VMEM((256, 1024), LOW),
            *sems(224, 32),
        ],
        compiler_params=pltpu.CompilerParams(
            collective_id=1, has_side_effects=True, vmem_limit_bytes=64 * 2**20 - 2**16
        ),
        cost_estimate=pl.CostEstimate(flops=40 * 10**9, bytes_accessed=30 * 10**6, transcendentals=2 * 10**6),
    )(lengths, inputs, cotangent, *small, w_qkv, w_out, w_up, w_down, qv_bias, up_bias)


def in_rows(ref, body):
    rows, width = ref.shape[-2:]
    step = min(rows, 2 ** ((32768 // width).bit_length() - 1))
    tiles(rows // step, lambda t: body(part(t * step, step)))


class SideReduce:
    def __init__(self, net, block, inbox, first):
        self.net, self.block, self.inbox, self.slot = net, block, inbox, net.slots(8)
        self.windows = (pl.ds(0, first), pl.ds(first, inbox.shape[1] - first))

    def other(self, dy):
        return (1 - self.net.half) * 4 + (self.net.y + dy) % 4

    def mine(self, dy):
        return self.net.half * 4 + (self.net.y + dy) % 4

    def give(self, dy):
        for side, device in enumerate((self.net.partner(), self.net.cousin())):
            rows = self.windows[side]
            self.net.push(
                self.slot + dy * 2 + side, self.block(dy).at[rows], self.inbox.at[dy, rows], device
            )

    def take(self, dy):
        for side in range(2):
            self.net.got(self.slot + dy * 2 + side, self.inbox.at[dy, self.windows[side]])


class LineReduce:
    def __init__(self, net, blocks, inbox, last):
        self.net, self.blocks, self.inbox, self.last = net, blocks, inbox, last
        self.slot = net.slots(4)

    def give(self, dy):
        self.net.push(self.slot + dy - 1, self.blocks.at[dy], self.inbox.at[dy - 1], self.net.at(dy=dy))

    def settle(self):
        for dy in (1, 2, 3):
            self.net.got(self.slot + dy - 1, self.inbox.at[dy - 1])

        def add(rows):
            total = self.blocks[0, rows, :].astype(jnp.float32)
            for i in range(3):
                total += self.inbox[i, rows, :].astype(jnp.float32)
            self.blocks[0, rows, :] = total.astype(LOW)

        in_rows(self.last, add)

    def close(self):
        self.settle()
        self.net.push(self.slot + 3, self.blocks.at[0], self.last, self.net.at(dx=2))

    def finish(self, emit):
        self.net.got(self.slot + 3, self.last)
        in_rows(
            self.last,
            lambda rows: emit(rows, self.blocks[0, rows, :].astype(jnp.float32) + self.last[rows, :].astype(jnp.float32)),
        )


class LineFirst:
    def __init__(self, net, blocks, inbox, total, side, last, first):
        self.net, self.blocks, self.inbox, self.total, self.side, self.last = net, blocks, inbox, total, side, last
        self.slot = net.slots(9)
        self.windows = (pl.ds(0, first), pl.ds(first, side.shape[0] - first))

    def owner(self, which, dy):
        half = 1 - self.net.half if which else self.net.half
        return half * 4 + (self.net.y + dy) % 4

    def give(self, which, dy):
        place = which * 3 + dy - 1
        self.net.push(self.slot + place, self.blocks.at[place], self.inbox.at[place], self.net.at(dy=dy))

    def take(self, which):
        for dy in (1, 2, 3):
            self.net.got(self.slot + which * 3 + dy - 1, self.inbox.at[which * 3 + dy - 1])

    def arrived(self, which, rows):
        return sum(self.inbox[which * 3 + i, rows, :].astype(jnp.float32) for i in range(3))

    def sideways(self):
        for i, device in enumerate((self.net.partner(), self.net.cousin())):
            rows = self.windows[i]
            self.net.push(self.slot + 6 + i, self.total.at[1, rows], self.side.at[rows], device)

    def close(self):
        for i in range(2):
            self.net.got(self.slot + 6 + i, self.side.at[self.windows[i]])

        def add(rows):
            total = self.total[0, rows, :].astype(jnp.float32) + self.side[rows, :].astype(jnp.float32)
            self.total[0, rows, :] = total.astype(LOW)

        in_rows(self.side, add)
        self.net.push(self.slot + 8, self.total.at[0], self.last, self.net.at(dx=2))

    def finish(self, emit):
        self.net.got(self.slot + 8, self.last)
        in_rows(
            self.last,
            lambda rows: emit(
                rows, self.total[0, rows, :].astype(jnp.float32) + self.last[rows, :].astype(jnp.float32)
            ),
        )


def emit_to(ref):
    def emit(rows, values):
        ref[rows, :] = values

    return emit


def norm_back(grad, centred, inverse, gain):
    scaled = grad * gain
    return inverse * (
        scaled - jnp.mean(scaled, -1, keepdims=True) - centred * jnp.mean(scaled * centred, -1, keepdims=True)
    )


def norm_parts(values):
    middle = jnp.mean(values, -1, keepdims=True)
    spread = jnp.mean(values * values, -1, keepdims=True) - middle * middle
    inverse = lax.rsqrt(spread + EPSILON)
    return (values - middle) * inverse, inverse


def column_sums(values):
    return jnp.sum(values, 0, keepdims=True)


def attend_back_chunk(chunk, q, kv, grad, att, lse, dq, dkv, half, length):
    slots = pl.ds(chunk * 512, 512)
    for head in range(2):
        at = pl.ds(head * HEAD, HEAD)
        key, value = kv(0, slots, head), kv(1, slots, head)
        dkey, dvalue = jnp.zeros((512, HEAD), jnp.float32), jnp.zeros((512, HEAD), jnp.float32)
        for group in range(chunk, 4):
            rows = pl.ds(group * 256, 256)
            query, upstream = q(rows, head), grad[rows, at]
            delta = jnp.sum(upstream.astype(jnp.float32) * att[rows, at].astype(jnp.float32), -1, keepdims=True)
            scores = dot(query, key, NT) * SCALE
            slot = chunk * 512 + lax.broadcasted_iota(jnp.int32, (1, 512), 1)
            allowed = slot < length
            if group == chunk:
                allowed = allowed & (slot <= place_rows(group, half))
            probs = jnp.exp(jnp.where(allowed, scores - lse[rows, pl.ds(head, 1)], -HUGE))
            dscores = (probs * (dot(upstream, value, NT) - delta)).astype(LOW)
            share = dot(dscores, key, NN)
            if group == chunk:
                dq[rows, at] = share
            else:
                dq[rows, at] += share
            dkey += dot(dscores, query, TN)
            dvalue += dot(probs.astype(LOW), upstream, TN)
        dkv(0, slots, head, (dkey * SCALE).astype(LOW))
        dkv(1, slots, head, dvalue.astype(LOW))


class Everyone:
    def __init__(self, net, axis, inbox):
        self.net, self.axis, self.inbox, self.slot = net, axis, inbox, net.slots(7)
        self.index = net.row if axis == "row" else net.col

    def device(self, shift):
        net, index = self.net, (self.index + shift) % 8
        row, col = (index, net.col) if self.axis == "row" else (net.row, index)
        return {"dp": net.dp, "row": row, "col": col}

    def begin(self, src_of):
        for shift in range(1, 8):
            to = (self.index + shift) % 8
            self.net.push(self.slot + shift - 1, src_of(to), self.inbox.at[self.index], self.device(shift))
        self.copy = self.net.move(src_of(self.index), self.inbox.at[self.index])

    def total(self):
        self.copy.wait()
        for shift in range(1, 8):
            self.net.got(self.slot + shift - 1, self.inbox.at[(self.index + 8 - shift) % 8])
        total = self.inbox[0]
        for i in range(1, 8):
            total += self.inbox[i]
        return total


class Blocks:
    def __init__(self, net, src, inbox):
        self.net, self.src, self.inbox, self.slot = net, src, inbox, net.slots(15)

    def begin(self):
        net = self.net
        place = self.inbox.at[net.dp * 8 + net.row]
        for shift in range(16):
            row = (net.row + shift) % 8
            block = self.src.at[:, part(row * 256, 256)]
            if shift == 0:
                self.copy = net.move(block, place)
            else:
                dp = net.dp if shift < 8 else 1 - net.dp
                net.push(self.slot + shift - 1, block, place, {"dp": dp, "row": row, "col": net.col})

    def total(self):
        net = self.net
        self.copy.wait()
        for shift in range(1, 16):
            dp = net.dp if shift < 8 else 1 - net.dp
            net.got(self.slot + shift - 1, self.inbox.at[dp * 8 + (net.row + 16 - shift) % 8])
        total = self.inbox[0]
        for i in range(1, 16):
            total += self.inbox[i]
        return total


def fourth_kernel(
    dqkv_in, n1_in, wq_in, x_in, dmid_in, wide, gout_in, mixed_in, up_in, down_in, sums, single,
    grad_low, mixed_out, qkv_grad, out_out, up_out, down_out, wide_grad, lone_grad,
    dqkv, n1, wq, x, dmid, grad_own, mixed_own, mixed, out_grad, up, up_last, up_grad, down, down_last, down_grad, terms, near, left, right, ends,
    gout, gout_side, gout_line, gout_last, gqkv, gqkv_line, gqkv_total, gqkv_side, gqkv_last,
    vector, wide_cols, wide_part, wide_rows, packed, single_rows, single_part, single_last,
    send, recv, local,
):
    net = Net(send, recv, local)
    load = {}
    for name, a, b in (
        ("dqkv", dqkv_in, dqkv), ("wq", wq_in, wq), ("n1", n1_in, n1), ("gout", gout_in, gout), ("down", down_in, down), ("up", up_in, up),
        ("mixed", mixed_in, mixed_own), ("x", x_in, x), ("dmid", dmid_in, dmid),
    ):
        load[name] = net.move(a, b)
    cols = [{"dp": net.dp, "row": net.row, "col": (net.col + d) % 8} for d in range(1, 8)]
    across = [{"dp": 1 - net.dp, "row": (net.row + d) % 8, "col": net.col} for d in (0, 1, 2, 3, 5, 6, 7)]
    net.greet(across, cols)
    back = ColReduce(net, terms, near, left, right, ends)
    sum_qkv = LineFirst(net, gqkv, gqkv_line, gqkv_total, gqkv_side, gqkv_last, 128)
    side_out = SideReduce(net, lambda dy: gout.at[pl.ds(dy * 256, 256)], gout_side, 128)
    line_out = LineReduce(net, gout_side, gout_line, gout_last)
    wide_a, wide_b = Everyone(net, "col", wide_cols), Blocks(net, wide_part, wide_rows)
    single_a = Everyone(net, "row", single_rows)
    crossing = net.slots(3)

    def feature_block(ref):
        return lambda r: ref.at[:, part(r * 256, 256)]

    def token_block(ref):
        return lambda r: ref.at[(r // 2) % 2, r % 2, part(r // 4 * OWN, OWN)]

    mixed_swap = Swap(net, feature_block(mixed_own), token_block(mixed))
    grad_swap = Swap(net, feature_block(grad_own), token_block(grad_low))

    def descend(dz):
        rows = part((net.z + dz) % 4 * 256, 256)

        def tile(t):
            at = part(t * 512, 512)
            total = dot(dqkv[rows, pl.ds(0, 256)], wq[0, at, :], NT)
            for i in (1, 2):
                total += dot(dqkv[rows, pl.ds(i * 256, 256)], wq[i, at, :], NT)
            terms[rows, at] = total.astype(LOW)

        tiles(4, tile)
        back.give(dz)

    def qkv_tile(r):
        return dot(n1[:, part(r * 256, 256)], dqkv[...], TN)

    def qkv_give(which, dy):
        gqkv[which * 3 + dy - 1] = qkv_tile(sum_qkv.owner(which, dy)).astype(LOW)
        sum_qkv.give(which, dy)

    def qkv_add(which):
        sum_qkv.take(which)
        total = qkv_tile(sum_qkv.owner(which, 0)) + sum_qkv.arrived(which, pl.ds(0, 256))
        gqkv_total[which] = total.astype(LOW)

    for name in ("dqkv", "wq", "n1"):
        load[name].wait()
    qkv_give(1, 1)
    qkv_give(1, 3)
    descend(2)
    for i, (name, ref, last) in enumerate((("down", down, down_last), ("up", up, up_last))):
        load[name].wait()
        net.push(crossing + 1 + i, ref, last, net.at(dx=2))
    load["gout"].wait()
    for dy in range(4):
        side_out.give(dy)
    descend(1)
    back.far()
    qkv_give(1, 2)
    descend(3)
    back.own(1)
    back.own(3)
    qkv_give(0, 1)
    descend(0)
    qkv_give(0, 3)
    back.forward(1)
    back.forward(3)
    qkv_give(0, 2)
    load["mixed"].wait()
    mixed_swap.begin()
    for i in range(7):
        packed[i : i + 1, :] = single[0:1, i * 256 : (i + 1) * 256]
    packed[7:8, :] = jnp.zeros((1, 256), jnp.float32)
    single_a.begin(lambda r: packed)
    load["x"].wait()
    load["dmid"].wait()
    back.finish()
    totals = [jnp.zeros((1, D), jnp.float32)] * 2
    for piece in range(4):
        rows = pl.ds(piece * 32, 32)
        grad = back.result(piece * 32, 32)
        centred, inverse = norm_parts(x[rows, :].astype(jnp.float32))
        value = dmid[rows, :] + norm_back(grad, centred, inverse, wide[0:1, :])
        grad_own[rows, :] = value.astype(LOW)
        totals = [a + column_sums(b) for a, b in zip(totals, (grad * centred, grad))]
    vector[...] = sums[...] + jnp.concatenate([*totals, jnp.zeros((6, D), jnp.float32)], 0)
    wide_a.begin(lambda r: vector)
    grad_swap.begin()
    for dy in (1, 2, 3, 0):
        side_out.take(dy)
        gout_side[dy] = (gout[pl.ds((4 + dy) * 256, 256), :].astype(jnp.float32) + gout_side[dy].astype(jnp.float32)).astype(LOW)
        if dy:
            line_out.give(dy)
    wide_part[...] = wide_a.total()
    wide_b.begin()
    qkv_add(1)
    sum_qkv.sideways()
    qkv_add(0)
    single_part[...] = single_a.total()
    net.push(crossing, single_part, single_last, net.at(dx=2))
    sum_qkv.close()
    line_out.close()
    for i, (ref, last, grad, out) in enumerate(((down, down_last, down_grad, down_out), (up, up_last, up_grad, up_out))):
        net.got(crossing + 1 + i, last)

        def add(rows):
            grad[rows, :] = ref[rows, :].astype(jnp.float32) + last[rows, :].astype(jnp.float32)

        in_rows(last, add)
        net.store(grad, out)
    mixed_swap.finish()
    net.store(mixed, mixed_out)
    grad_swap.finish()
    wide_grad[...] = wide_b.total()
    net.got(crossing, single_last)
    lone_grad[...] = single_part[...] + single_last[...]

    def emit_qkv(rows, values):
        for i in range(3):
            qkv_grad[i, rows, :] = values[:, i * 256 : (i + 1) * 256]

    sum_qkv.finish(emit_qkv)
    line_out.finish(emit_to(out_grad))
    net.store(out_grad, out_out)
    net.drain()


def fourth(dqkv, n1, wq, x, dmid, wide, gout, mixed, up, down, sums, lone):
    return pl.pallas_call(
        fourth_kernel,
        out_shape=(
            low_shape(2, 2, 256, 256),
            low_shape(2, 2, 256, 256),
            full_shape(3, 256, 256),
            full_shape(256, 256),
            full_shape(256, 1024),
            full_shape(1024, 256),
            full_shape(8, 256),
            full_shape(8, 256),
        ),
        in_specs=[HBM, HBM, HBM, HBM, HBM, VM, HBM, HBM, HBM, HBM, VM, VM],
        out_specs=(VM, HBM, VM, HBM, HBM, HBM, VM, VM),
        scratch_shapes=[
            pltpu.VMEM((1024, 768), LOW),
            pltpu.VMEM((1024, D), LOW),
            pltpu.VMEM((3, D, 256), LOW),
            pltpu.VMEM((OWN, D), LOW),
            pltpu.VMEM((OWN, D), jnp.float32),
            pltpu.VMEM((OWN, D), LOW),
            pltpu.VMEM((OWN, D), LOW),
            pltpu.VMEM((2, 2, 256, 256), LOW),
            pltpu.VMEM((256, 256), jnp.float32),
            pltpu.VMEM((256, 1024), LOW),
            pltpu.VMEM((256, 1024), LOW),
            pltpu.VMEM((256, 1024), jnp.float32),
            pltpu.VMEM((1024, 256), LOW),
            pltpu.VMEM((1024, 256), LOW),
            pltpu.VMEM((1024, 256), jnp.float32),
            *reduce_scratch(),
            pltpu.VMEM((2048, 256), LOW),
            pltpu.VMEM((4, 256, 256), LOW),
            pltpu.VMEM((3, 256, 256), LOW),
            pltpu.VMEM((256, 256), LOW),
            pltpu.VMEM((6, 256, 768), LOW),
            pltpu.VMEM((6, 256, 768), LOW),
            pltpu.VMEM((2, 256, 768), LOW),
            pltpu.VMEM((256, 768), LOW),
            pltpu.VMEM((256, 768), LOW),
            pltpu.VMEM((8, D), jnp.float32),
            pltpu.VMEM((8, 8, D), jnp.float32),
            pltpu.VMEM((8, D), jnp.float32),
            pltpu.VMEM((16, 8, 256), jnp.float32),
            pltpu.VMEM((8, 256), jnp.float32),
            pltpu.VMEM((8, 8, 256), jnp.float32),
            pltpu.VMEM((8, 256), jnp.float32),
            pltpu.VMEM((8, 256), jnp.float32),
            *sems(112, 24),
        ],
        compiler_params=pltpu.CompilerParams(
            collective_id=4, has_side_effects=True, vmem_limit_bytes=60 * 2**20
        ),
        cost_estimate=pl.CostEstimate(flops=40 * 10**9, bytes_accessed=30 * 10**6, transcendentals=2 * 10**6),
    )(dqkv, n1, wq, x, dmid, wide, gout, mixed, up, down, sums, lone)


def hand_over_kernel(
    mixed_in, grad_in, qkv_in, out_in, up_in, down_in, wide, lone,
    mixed, input_grad, gain1, bias1, qkv, qv, out, out_bias, gain2, bias2, up, up_bias, down, down_bias,
    *rest,
):
    between, done = rest[:-1], rest[-1]
    pairs = ((down_in, down), (up_in, up), (qkv_in, qkv), (mixed_in, mixed), (out_in, out))
    fetches = [pltpu.make_async_copy(a, m, done.at[i]) for i, ((a, b), m) in enumerate(zip(pairs, between))]
    copies = [pltpu.make_async_copy(m, b, done.at[5 + i]) for i, ((a, b), m) in enumerate(zip(pairs, between))]
    for fetch in fetches:
        fetch.start()
    for fetch, copy in zip(fetches, copies):
        fetch.wait()
        copy.start()
    for i, ref in enumerate((gain1, bias1, out_bias, gain2, bias2, down_bias)):
        ref[...] = wide[i : i + 1, :]
    for i in range(4):
        up_bias[:, i * 256 : (i + 1) * 256] = lone[i : i + 1, :]
    qv[0:1, :] = lone[4:5, :]
    qv[1:2, :] = lone[6:7, :]
    for i in range(2):
        for j in range(2):
            input_grad[i, j] = grad_in[i, j].astype(jnp.float32)
    for copy in copies:
        copy.wait()


def hand_over(mixed, grad, qkv, out, up, down, wide, lone):
    vector = full_shape(1, 256)
    return pl.pallas_call(
        hand_over_kernel,
        out_shape=(
            low_shape(2, 2, 256, 256),
            full_shape(2, 2, 256, 256),
            vector,
            vector,
            full_shape(3, 256, 256),
            full_shape(2, 256),
            full_shape(256, 256),
            vector,
            vector,
            vector,
            full_shape(256, 1024),
            full_shape(1, 1024),
            full_shape(1024, 256),
            vector,
        ),
        in_specs=[HBM, VM, HBM, HBM, HBM, HBM, VM, VM],
        out_specs=(HBM, VM, VM, VM, HBM, VM, HBM, VM, VM, VM, HBM, VM, HBM, VM),
        scratch_shapes=[
            pltpu.VMEM((1024, 256), jnp.float32),
            pltpu.VMEM((256, 1024), jnp.float32),
            pltpu.VMEM((3, 256, 256), jnp.float32),
            pltpu.VMEM((2, 2, 256, 256), LOW),
            pltpu.VMEM((256, 256), jnp.float32),
            pltpu.SemaphoreType.DMA((10,)),
        ],
        compiler_params=pltpu.CompilerParams(vmem_limit_bytes=63 * 2**20),
    )(mixed, grad, qkv, out, up, down, wide, lone)


def shards(
    inputs,
    lengths,
    ln1_gain,
    ln1_bias,
    w_qkv,
    qv_bias,
    w_out,
    out_bias,
    ln2_gain,
    ln2_bias,
    w_up,
    up_bias,
    w_down,
    down_bias,
    cotangent,
):
    small = [a.reshape(1, 256) for a in (ln1_gain, ln1_bias, out_bias, ln2_gain, ln2_bias, down_bias)]
    x, all1, wq, wide, dqkv, dmid, gout, mixed, up, down, sums, lone = ahead(
        lengths, inputs, cotangent, small, w_qkv, w_out, w_up, w_down, qv_bias, up_bias.reshape(1, 1024)
    )
    grad, mixed, g_qkv, g_out, g_up, g_down, wide_grad, lone_grad = fourth(
        dqkv, all1, wq, x, dmid, wide, gout, mixed, up, down, sums, lone
    )
    outs = hand_over(mixed, grad, g_qkv, g_out, g_up, g_down, wide_grad, lone_grad)
    return tuple(a.reshape(-1) if a.shape[0] == 1 else a for a in outs)


def solution(mesh):
    tokens = P(None, "dp", "col", "row")
    in_specs = (
        tokens,
        P(None, "dp"),
        P("row"),
        P("row"),
        P(None, "row", "col"),
        P(None, "col"),
        P("col", "row"),
        P("row"),
        P("row"),
        P("row"),
        P("row", "col"),
        P("col"),
        P("col", "row"),
        P("row"),
        tokens,
    )
    out_specs = (
        tokens,
        tokens,
        P("row"),
        P("row"),
        P(None, "row", "col"),
        P(None, "col"),
        P("col", "row"),
        P("row"),
        P("row"),
        P("row"),
        P("row", "col"),
        P("col"),
        P("col", "row"),
        P("row"),
    )
    return jax.shard_map(shards, mesh=mesh, in_specs=in_specs, out_specs=out_specs, check_vma=False)
```

```python
import functools

import jax
import jax.numpy as jnp
from jax import lax
from jax.experimental import pallas as pl
from jax.experimental.pallas import tpu as pltpu
from jax.sharding import PartitionSpec as P

D = 2048
HEAD = 128
SCALE = HEAD**-0.5
EPSILON = 1e-05
HUGE = 1e30
LOW = jnp.bfloat16
OWN = 128
VMEM_LIMIT = 56 * 2**20


def dot(a, b, contract):
    return lax.dot_general(a, b, ((contract[0], contract[1]), ((), ())), preferred_element_type=jnp.float32)


NN = ((1,), (0,))
NT = ((1,), (1,))
TN = ((0,), (0,))


def place_rows(group, half):
    row = lax.broadcasted_iota(jnp.int32, (256, 1), 0)
    return (2 * group + row // OWN) * 256 + half * OWN + row % OWN


def allowed_keys(group, extent, half, length):
    slot = lax.broadcasted_iota(jnp.int32, (256, extent), 1)
    return (slot <= place_rows(group, half)) & (slot < length)


MESH = pl.DeviceIdType.MESH
HBM = pl.BlockSpec(memory_space=pl.ANY)
VM = pl.BlockSpec(memory_space=pltpu.VMEM)
SM = pl.BlockSpec(memory_space=pltpu.SMEM)


def part(start, size):
    return pl.ds(pl.multiple_of(start, size), size)


class Net:
    def __init__(self, send, recv, local):
        self.send, self.recv, self.local = send, recv, local
        self.used, self.local_used, self.live, self.own = 0, 0, [], []
        self.dp, self.row, self.col = (lax.axis_index(a) for a in ("dp", "row", "col"))
        self.half, self.y = self.row // 4, self.row % 4
        self.x = self.dp * 2 + self.half
        self.z, self.core = self.col // 2, self.col % 2

    def at(self, dx=0, dy=0, dz=0, other_core=False):
        x, y, z = (self.x + dx) % 4, (self.y + dy) % 4, (self.z + dz) % 4
        core = 1 - self.core if other_core else self.core
        return {"dp": x // 2, "row": (x % 2) * 4 + y, "col": z * 2 + core}

    def mate(self, shift):
        return {"dp": self.dp, "row": (self.row + shift) % 8, "col": self.col}

    def partner(self):
        return self.mate(4)

    def cousin(self):
        return {"dp": 1 - self.dp, "row": (self.row + 4) % 8, "col": self.col}

    def greet(self, more=(), cols=()):
        devices = [self.mate(d) for d in range(1, 8)]
        devices += [self.cousin()]
        devices += cols or [self.at(dz=1), self.at(dz=3), self.at(other_core=True)]
        devices += more
        barrier = pltpu.get_barrier_semaphore()
        for device in devices:
            pl.semaphore_signal(barrier, inc=1, device_id=device, device_id_type=MESH)
        pl.semaphore_wait(barrier, len(devices))

    def slots(self, count):
        self.used += count
        return self.used - count

    def _copy(self, slot, src, dst, device):
        return pltpu.make_async_remote_copy(
            src_ref=src,
            dst_ref=dst,
            send_sem=self.send.at[slot],
            recv_sem=self.recv.at[slot],
            device_id=device,
            device_id_type=MESH,
        )

    def push(self, slot, src, dst, device):
        copy = self._copy(slot, src, dst, device)
        copy.start()
        self.live.append(copy)

    def got(self, slot, ref):
        self._copy(slot, ref, ref, self.at(other_core=True)).wait_recv()

    def flush(self, copies):
        for copy in copies:
            copy.wait_send()
        self.live = [copy for copy in self.live if not any(copy is other for other in copies)]

    def move(self, src, dst):
        copy = pltpu.make_async_copy(src, dst, self.local.at[self.local_used])
        self.local_used += 1
        copy.start()
        return copy

    def store(self, src, dst):
        self.own.append(self.move(src, dst))

    def drain(self):
        for copy in self.live:
            copy.wait_send()
        for copy in self.own:
            copy.wait()


class ColGather:
    def __init__(self, net, buf):
        self.net, self.buf, self.slot = net, buf, net.slots(14)
        self.sent = []

    def rows(self, dz, other_core, piece):
        net = self.net
        core = 1 - net.core if other_core else net.core
        return self.buf.at[part(((net.z + dz) % 4 * 2 + core) * OWN + 64 * piece, 64)]

    def move(self, slot, where, piece, **to):
        ref = self.rows(where, False, piece)
        self.net.push(self.slot + slot, ref, ref, self.net.at(**to))
        self.sent.append(self.net.live[-1])

    def flush(self):
        self.net.flush(self.sent)

    def got(self, slot, dz, piece, other_core=False):
        self.net.got(self.slot + slot, self.rows(dz, other_core, piece))

    def begin(self):
        self.move(0, 0, 0, dz=1)
        self.move(3, 0, 1, dz=3)
        self.move(1, 0, 1, dz=1)
        self.move(2, 0, 0, dz=3)
        self.move(6, 0, 0, other_core=True)
        self.move(7, 0, 1, other_core=True)

    def hop(self):
        self.pass_on()
        self.take_rest()

    def pass_on(self):
        self.got(0, 3, 0)
        self.move(4, 3, 0, dz=1)
        self.got(3, 1, 1)
        self.move(5, 1, 1, dz=3)
        self.move(8, 3, 0, other_core=True)
        self.move(11, 1, 1, other_core=True)

    def take_rest(self):
        self.got(1, 3, 1)
        self.move(9, 3, 1, other_core=True)
        self.got(2, 1, 0)
        self.move(10, 1, 0, other_core=True)

    def far(self):
        self.got(4, 2, 0)
        self.move(12, 2, 0, other_core=True)
        self.got(5, 2, 1)
        self.move(13, 2, 1, other_core=True)

    def pair(self, dz):
        slot = {0: 6, 3: 8, 1: 10, 2: 12}[dz]
        self.got(slot, dz, 0, True)
        self.got(slot + 1, dz, 1, True)


class RowGather:
    def __init__(self, net, src, buf, whole, parts):
        self.net, self.src, self.buf, self.whole, self.parts = net, src, buf, whole, parts
        self.slot, self.sent = net.slots(11), []

    def place(self, dy, other=False):
        net = self.net
        half = 1 - net.half if other else net.half
        return self.whole(self.buf, half * 4 + (net.y + dy) % 4)

    def sideways(self, dy, src, sides=(0, 1)):
        net, there = self.net, self.place(dy)
        devices = (net.partner(), net.cousin())
        for side in sides:
            net.push(
                self.slot + 3 + dy * 2 + side, self.parts(src, side), self.parts(there, side), devices[side]
            )
            self.sent.append(net.live[-1])

    def flush(self):
        self.net.flush(self.sent)

    def begin(self):
        net, mine = self.net, self.place(0)
        for dy in (1, 3, 2):
            net.push(self.slot + dy - 1, self.src, mine, net.at(dy=dy))
            self.sent.append(net.live[-1])
        self.copy = net.move(self.src, mine)

    def begin_sideways(self, sides=(0, 1)):
        self.sideways(0, self.src, sides)

    def step(self, dy, sides=(0, 1)):
        ref = self.place(4 - dy)
        self.net.got(self.slot + dy - 1, ref)
        self.sideways(4 - dy, ref, sides)

    def follow(self, dy, sides):
        self.sideways(4 - dy, self.place(4 - dy), sides)

    def steps(self):
        for dy in (1, 3, 2):
            self.step(dy)

    def finish(self):
        self.copy.wait()
        for dy in range(4):
            for side in range(2):
                self.net.got(self.slot + 3 + dy * 2 + side, self.parts(self.place(dy, True), side))


def cut(rows):
    def parts(ref, side):
        total = ref.shape[-2]
        window = pl.ds(0, rows) if side == 0 else pl.ds(rows, total - rows)
        return ref.at[:, window] if len(ref.shape) == 3 else ref.at[window]

    return parts


class Swap:
    def __init__(self, net, src_of, dst_of):
        self.net, self.src_of, self.dst_of, self.slot = net, src_of, dst_of, net.slots(7)

    def begin(self):
        net = self.net
        for shift in range(1, 8):
            net.push(self.slot + shift - 1, self.src_of((net.row + shift) % 8), self.dst_of(net.row), net.mate(shift))
        self.copy = net.move(self.src_of(net.row), self.dst_of(net.row))

    def finish(self):
        net = self.net
        self.copy.wait()
        for shift in range(1, 8):
            net.got(self.slot + shift - 1, self.dst_of((net.row + 8 - shift) % 8))


def norm_rows(values, gain, bias):
    middle = jnp.mean(values, -1, keepdims=True)
    spread = jnp.mean(values * values, -1, keepdims=True) - middle * middle
    inverse = lax.rsqrt(spread + EPSILON)
    centred = (values - middle) * inverse
    return centred * gain + bias


def attend_group(q, kv, head, group, half, length):
    cols, rows, extent = pl.ds(head * HEAD, HEAD), pl.ds(group * 256, 256), 512 * (group + 1)
    scores = dot(q[rows, cols], kv[0, :extent, cols], NT) * SCALE
    scores = jnp.where(allowed_keys(group, extent, half, length), scores, -HUGE)
    highest = jnp.max(scores, -1, keepdims=True)
    weights = jnp.exp(scores - highest)
    total = jnp.sum(weights, -1, keepdims=True)
    out = dot(weights.astype(LOW), kv[1, :extent, cols], NN) / total
    return out, highest + jnp.log(total)


def low_shape(*shape):
    return jax.ShapeDtypeStruct(shape, LOW)


def full_shape(*shape):
    return jax.ShapeDtypeStruct(shape, jnp.float32)


def sems(remote, local):
    return [
        pltpu.SemaphoreType.DMA((remote,)),
        pltpu.SemaphoreType.DMA((remote,)),
        pltpu.SemaphoreType.DMA((local,)),
    ]


class ColReduce:
    def __init__(self, net, terms, near, left, right, ends):
        self.net, self.terms, self.near, self.left, self.right, self.ends = net, terms, near, left, right, ends
        self.slot = net.slots(10)
        self.sent = []

    def push(self, *copy):
        self.net.push(*copy)
        self.sent.append(self.net.live[-1])

    def flush(self):
        self.net.flush(self.sent)

    def block(self, dz, other_core=False):
        net = self.net
        core = 1 - net.core if other_core else net.core
        return part(((net.z + dz) % 4 * 2 + core) * OWN, OWN)

    def rows(self, dz, piece):
        net = self.net
        return part(((net.z + dz) % 4 * 2 + net.core) * OWN + 64 * piece, 64)

    def give(self, dz):
        self.push(
            self.slot + dz, self.terms.at[self.block(dz, True)], self.near.at[pl.ds(dz * OWN, OWN)], self.net.at(other_core=True)
        )

    def fold(self, dz):
        near = self.near.at[pl.ds(dz * OWN, OWN)]
        self.net.got(self.slot + dz, near)
        block = self.block(dz)
        self.terms[block, :] = (self.terms[block, :].astype(jnp.float32) + near[...].astype(jnp.float32)).astype(LOW)

    def send(self, slot, dz, piece, dst, side):
        self.push(self.slot + slot, self.terms.at[self.rows(dz, piece)], dst, self.net.at(dz=side))

    def far(self):
        self.fold(2)
        self.send(4, 2, 0, self.left, 1)
        self.send(5, 2, 1, self.right, 3)

    def own(self, dz):
        self.fold(dz)
        side = 0 if dz == 1 else 1
        self.send(6 + side * 2 + 1 - side, dz, 1 - side, self.ends.at[side, pl.ds((1 - side) * 64, 64)], dz)

    def forward(self, dz):
        side = 0 if dz == 1 else 1
        inbox = self.left if dz == 1 else self.right
        self.net.got(self.slot + 4 + side, inbox)
        rows = self.rows(dz, side)
        self.terms[rows, :] = (self.terms[rows, :].astype(jnp.float32) + inbox[...].astype(jnp.float32)).astype(LOW)
        self.send(6 + side * 2 + side, dz, side, self.ends.at[side, pl.ds(side * 64, 64)], dz)

    def finish(self):
        self.net.got(self.slot, self.near.at[pl.ds(0, OWN)])
        for side in range(2):
            for piece in range(2):
                self.net.got(self.slot + 6 + side * 2 + piece, self.ends.at[side, pl.ds(piece * 64, 64)])

    def result(self, start, size):
        block = part(self.net.col * OWN + start, size)
        total = self.terms[block, :].astype(jnp.float32) + self.near[pl.ds(start, size), :].astype(jnp.float32)
        for side in range(2):
            total += self.ends[side, pl.ds(start, size), :].astype(jnp.float32)
        return total


def reduce_scratch():
    return [
        pltpu.VMEM((1024, D), LOW),
        pltpu.VMEM((4 * OWN, D), LOW),
        pltpu.VMEM((64, D), LOW),
        pltpu.VMEM((64, D), LOW),
        pltpu.VMEM((2, OWN, D), LOW),
    ]


def tiles(count, body):
    lax.fori_loop(0, count, lambda t, c: (body(t), c)[1], 0)


def ahead_kernel(
    lengths, inputs, cotangent, gain1, bias1, bias_out, gain2, bias2, bias_down, w_qkv, w_out, w_up, w_down, qv_bias, up_bias,
    x_out, n1_out, wq_out, small_out, dqkv_out, dmid_out, gout_out, mixed_out, up_a, up_b, down_a, down_b, sums, lone,
    x, dy, n1, q, kv, att, wq, wo, wide,
    terms, near, left, right, ends, mid, n2, act, slope, wu, wd, small, lse,
    datt, dq, dkv_inbox, down_side, down_line, down_last, up, up_side, up_line, up_last, gout_line,
    send, recv, local,
):
    net = Net(send, recv, local)
    for i, ref in enumerate((gain1, bias1, bias_out, gain2, bias2, bias_down)):
        small[i : i + 1, :] = ref[...]
    small[6:8, :] = jnp.zeros((2, 256), jnp.float32)
    length = lengths[(net.row // 2) % 2, net.row % 2]
    net.greet([net.at(dx=2)])
    mine = part(net.col * OWN, OWN)

    def token_block(ref):
        return lambda r: ref.at[(r // 2) % 2, r % 2, part(r // 4 * OWN, OWN)]

    def feature_block(ref):
        return lambda r: ref.at[:, part(r * 256, 256)]

    def by_columns(ref, r):
        return ref.at[:, part(r * 256, 256)]

    def by_rows(ref, r):
        return ref.at[part(r * 256, 256)]

    params = Swap(net, lambda r: small, feature_block(wide))
    tokens = Swap(net, token_block(inputs), feature_block(x))
    upstream = Swap(net, token_block(cotangent), lambda r: dy.at[mine, part(r * 256, 256)])
    gather_kv = RowGather(net, w_qkv.at[pl.ds(1, 2)], wq.at[pl.ds(1, 2)], by_columns, cut(128))
    gather_q = RowGather(net, w_qkv.at[pl.ds(0, 1)], wq.at[pl.ds(0, 1)], by_columns, cut(32))
    gather_wo = RowGather(net, w_out, wo, by_columns, cut(16))
    gather_wu = RowGather(net, w_up, wu, by_rows, cut(128))
    gather_wd = RowGather(net, w_down, wd, by_columns, cut(512))
    all_n1, all_dy, all_n2 = ColGather(net, n1), ColGather(net, dy), ColGather(net, n2)
    branch = ColReduce(net, terms, near, left, right, ends)
    keys = net.slots(16)

    def pair(dz):
        return part((net.z + dz) % 4 * 256, 256)

    def project_keys(dz):
        all_n1.pair(dz)
        block = (net.z + dz) % 4
        values = n1[pair(dz), :]
        k = dot(values, wq[1], NN).astype(LOW)
        v = (dot(values, wq[2], NN) + qv_bias[1:2, :]).astype(LOW)
        for i in range(2):
            there = part((block * 2 + i) * 256 + net.half * OWN, OWN)
            kv[0, there, :] = k[i * OWN : (i + 1) * OWN]
            kv[1, there, :] = v[i * OWN : (i + 1) * OWN]

    def key_block(dz, i, half, head):
        there = part(((net.z + dz) % 4 * 2 + i) * 256 + half * OWN, OWN)
        return kv.at[:, there, pl.ds(head * HEAD, HEAD)]

    def swap_keys(dz, head):
        for i in range(2):
            ref = key_block(dz, i, net.half, head)
            net.push(keys + head * 8 + dz * 2 + i, ref, ref, net.partner())

    def take_keys(dz, head):
        for i in range(2):
            net.got(keys + head * 8 + dz * 2 + i, key_block(dz, i, 1 - net.half, head))

    def second_head(group, half, act_on):
        for i in range(2):
            place = part((group * 2 + i) * 256 + half * OWN, OWN)
            ref = kv.at[:, place, pl.ds(HEAD, HEAD)]
            act_on(keys + 8 + group * 2 + i, ref)

    params.begin()
    tokens.begin()
    gather_kv.begin()
    gather_kv.begin_sideways()
    params.finish()
    tokens.finish()
    for piece in range(4):
        rows = pl.ds(piece * 32, 32)
        low = norm_rows(x[rows, :].astype(jnp.float32), wide[0:1, :], wide[1:2, :]).astype(LOW)
        n1[part(net.col * OWN + piece * 32, 32), :] = low
    all_n1.begin()
    keep_x = net.move(x, x_out)
    net.store(wide, small_out)
    all_n1.pass_on()
    gather_kv.steps()
    upstream.begin()
    gather_q.begin()
    gather_q.begin_sideways()
    all_n1.take_rest()
    gather_kv.finish()
    for dz in (0, 3, 1):
        project_keys(dz)
        swap_keys(dz, 0)
    all_n1.far()
    project_keys(2)
    swap_keys(2, 0)
    gather_wo.begin()
    gather_wo.begin_sideways()
    gather_wu.begin()
    gather_wd.begin()
    upstream.finish()
    all_dy.begin()
    gather_q.steps()
    gather_wu.begin_sideways((1,))
    all_dy.pass_on()
    take_keys(0, 0)
    take_keys(3, 0)
    for group in range(4):
        second_head(group, net.half, lambda slot, ref: net.push(slot, ref, ref, net.partner()))
    gather_q.finish()

    def project_queries(t):
        rows = part(t * 256, 256)
        q[rows, :] = (dot(n1[rows, :], wq[0], NN) + qv_bias[0:1, :]).astype(LOW)

    tiles(4, project_queries)
    def attend(head):
        if head == 0:
            take_keys(1, 0)
            take_keys(2, 0)
        for group in range(4):
            if head:
                second_head(group, 1 - net.half, net.got)
            out, logsum = attend_group(q, kv, head, group, net.half, length)
            rows = pl.ds(group * 256, 256)
            att[rows, pl.ds(head * HEAD, HEAD)] = out.astype(LOW)
            lse[rows, pl.ds(head, 1)] = logsum

    gather_wo.steps()
    attend(0)
    all_dy.take_rest()
    all_dy.far()
    attend(1)
    gather_wu.begin_sideways((0,))
    gather_wo.finish()

    def project(dz):
        rows = pair(dz)

        def tile(t):
            cols = part(t * 512, 512)
            terms[rows, cols] = dot(att[rows, :], wo[:, cols], NN).astype(LOW)

        tiles(4, tile)
        branch.give(dz)

    project(2)
    project(1)
    branch.far()
    project(3)
    branch.own(1)
    branch.own(3)
    project(0)
    gather_wu.step(1)
    gather_wu.step(3)
    branch.forward(1)
    branch.forward(3)
    gather_wu.step(2)
    keep_n1 = net.move(n1, n1_out)
    keep_wq = net.move(wq, wq_out)
    branch.finish()
    for piece in range(4):
        rows = pl.ds(piece * 32, 32)
        total = x[rows, :].astype(jnp.float32) + branch.result(piece * 32, 32) + wide[2:3, :]
        mid[rows, :] = total
        low = norm_rows(total, wide[3:4, :], wide[4:5, :]).astype(LOW)
        n2[part(net.col * OWN + piece * 32, 32), :] = low
    for copy in (keep_x, keep_n1, keep_wq):
        copy.wait()
    gather_kv.flush()
    gather_q.flush()
    all_n1.flush()
    all_n2.begin()
    gather_wd.begin_sideways()
    gather_wd.step(1)
    gather_wd.step(3)
    gather_wu.finish()

    def ascend(dz):
        all_n2.pair(dz)
        rows = pair(dz)

        def tile(t):
            cols = part(t * 256, 256)
            hidden = dot(n2[rows, :], wu[:, cols], NN) + up_bias[:, cols]
            share = 0.5 + 0.5 * lax.erf(hidden * 0.5**0.5)
            act[rows, cols] = (hidden * share).astype(LOW)
            density = jnp.exp(-0.5 * hidden * hidden) * (0.5 / jnp.pi) ** 0.5
            slope[rows, cols] = (share + hidden * density).astype(LOW)

        tiles(4, tile)

    ascend(0)
    all_n2.pass_on()
    gather_wd.step(2)
    all_n2.take_rest()
    ascend(3)
    for dz in range(4):
        all_dy.pair(dz)
    all_n2.far()
    ascend(1)
    ascend(2)
    gather_wd.finish()
    back = ColReduce(net, terms, near, left, right, ends)
    all_db, db = ColGather(net, n1), n1
    ffn = ColReduce(net, terms, near, left, right, ends)
    side_down = SideReduce(net, lambda dy: wq.at[dy // 2, pl.ds(dy % 2 * 1024, 1024)], down_side, 384)
    line_down = LineReduce(net, down_side, down_line, down_last)
    side_up = SideReduce(net, lambda dy: up.at[dy], up_side, 96)
    line_up = LineReduce(net, up_side, up_line, up_last)
    sum_out = LineFirst(net, lambda i: wq.at[2, pl.ds(i * 256, 256)], gout_line, None, None, None, 128)
    key_grads = net.slots(8)

    def descend(dz):
        rows = pair(dz)

        def into_hidden(t):
            cols = part(t * 512, 512)
            grad = dot(dy[rows, :], wd[cols, :], NT)
            slope[rows, cols] = (grad * slope[rows, cols].astype(jnp.float32)).astype(LOW)

        def into_width(t):
            cols = part(t * 512, 512)
            terms[rows, cols] = dot(slope[rows, :], wu[cols, :], NT).astype(LOW)

        tiles(2, into_hidden)
        tiles(4, into_width)
        back.give(dz)

    def down_tile(r, t):
        return dot(act[:, part(t * 512, 512)], dy[:, part(r * 256, 256)], TN)

    def up_tile(r, t):
        return dot(n2[:, part(r * 256, 256)], slope[:, part(t * 512, 512)], TN)

    def down_give(step):
        r = side_down.other(step)

        def tile(t):
            wq[step // 2, part(step % 2 * 1024 + t * 512, 512), :] = down_tile(r, t).astype(LOW)

        tiles(2, tile)
        side_down.give(step)

    def down_add(step):
        side_down.take(step)
        r = side_down.mine(step)

        def tile(t):
            units = part(t * 512, 512)
            down_side[step, units, :] = (down_tile(r, t) + down_side[step, units, :].astype(jnp.float32)).astype(LOW)

        tiles(2, tile)

    def up_give(step):
        r = side_up.other(step)

        def tile(t):
            up[step, :, part(t * 512, 512)] = up_tile(r, t).astype(LOW)

        tiles(2, tile)
        side_up.give(step)

    def up_add(step):
        side_up.take(step)
        r = side_up.mine(step)

        def tile(t):
            units = part(t * 512, 512)
            up_side[step, :, units] = (up_tile(r, t) + up_side[step, :, units].astype(jnp.float32)).astype(LOW)

        tiles(2, tile)

    def low_rank(dz):
        all_db.pair(dz)
        rows = pair(dz)
        datt[rows, :] = dot(db[rows, :], wo[...], NT).astype(LOW)

    branch.flush()
    down_give(2)
    down_give(1)
    descend(2)
    descend(1)
    back.far()
    down_give(3)
    descend(3)
    back.own(1)
    back.own(3)
    down_add(2)
    line_down.give(2)
    descend(0)
    down_give(0)
    back.forward(1)
    back.forward(3)
    for step in (1, 3):
        down_add(step)
        line_down.give(step)
    for step in (2, 1, 3, 0):
        up_give(step)
    back.finish()
    totals = [jnp.zeros((1, D), jnp.float32)] * 4
    for piece in range(4):
        rows = pl.ds(piece * 32, 32)
        own = part(net.col * OWN + piece * 32, 32)
        grad = back.result(piece * 32, 32)
        centred, inverse = norm_parts(mid[rows, :])
        upstream = dy[own, :].astype(jnp.float32)
        value = upstream + norm_back(grad, centred, inverse, wide[3:4, :])
        x[rows, :] = (mid[rows, :] + wide[5:6, :]).astype(LOW)
        mid[rows, :] = value
        low = value.astype(LOW)
        db[own, :] = low
        terms_of = (low.astype(jnp.float32), grad * centred, grad, upstream)
        totals = [a + column_sums(b) for a, b in zip(totals, terms_of)]
    all_db.begin()
    zero = jnp.zeros((2, D), jnp.float32)
    sums[...] = jnp.concatenate([zero, *totals, zero], 0)
    net.store(mid, dmid_out)
    back.flush()

    def mix(t):
        cols = part(t * 512, 512)
        for i in range(2):
            rows = pl.ds(i * 512, 512)
            terms[rows, cols] = dot(act[rows, :], wd[:, cols], NN).astype(LOW)

    tiles(4, mix)
    all_db.pass_on()
    down_add(0)
    line_down.close()
    net.store(down_side.at[0], down_a)
    all_db.take_rest()
    low_rank(0)
    for dz in (2, 1, 3, 0):
        ffn.give(dz)
    ffn.far()
    up_add(2)
    line_up.give(2)
    all_db.far()
    for dz in (3, 1, 2):
        low_rank(dz)
    ffn.own(1)
    ffn.own(3)
    def of_keys(which, slots, head):
        return kv[which, slots, pl.ds(head * HEAD, HEAD)]

    def of_queries(rows, head):
        return q[rows, pl.ds(head * HEAD, HEAD)]

    gather_wu.flush()
    gather_wd.flush()
    def keep(which, slots, head, values):
        wu[slots, pl.ds(512 + which * 256 + head * HEAD, HEAD)] = values

    def attend_back(chunk):
        attend_back_chunk(chunk, of_queries, of_keys, datt, att, lse, dq, keep, net.half, length)
        for block in (chunk * 2, chunk * 2 + 1):
            theirs = part(block * 256 + (1 - net.half) * OWN, OWN)
            net.push(
                key_grads + block,
                wu.at[theirs, pl.ds(512, 512)],
                dkv_inbox.at[pl.ds(block * OWN, OWN)],
                net.partner(),
            )

    attend_back(3)
    up_add(1)
    line_up.give(1)
    attend_back(2)
    ffn.forward(1)
    ffn.forward(3)
    up_add(3)
    line_up.give(3)
    attend_back(1)
    attend_back(0)

    def out_block(which, dy):
        r = sum_out.owner(which, dy)
        place = which * 3 + dy - 1 if dy else 6 + which
        wq[2, pl.ds(place * 256, 256), :] = dot(att[...], n1[:, part(r * 256, 256)], TN).astype(LOW)

    for which in (1, 0):
        for dy in (2, 1, 3):
            out_block(which, dy)
            sum_out.give(which, dy)
        out_block(which, 0)
    up_add(0)
    lone[:, pl.ds(0, 1024)] = dot(jnp.ones((8, 1024), LOW), slope[...], NN)
    for piece in range(4):
        rows = pl.ds(piece * 256, 256)
        wd[rows, pl.ds(256, 256)] = (dq[rows, :] * SCALE).astype(LOW)
    ffn.finish()
    for piece in range(4):
        rows = pl.ds(piece * 32, 32)
        x[rows, :] = (x[rows, :].astype(jnp.float32) + ffn.result(piece * 32, 32)).astype(LOW)
    net.store(x, mixed_out)
    line_up.close()
    net.store(up_side.at[0], up_a)
    for which in (1, 0):
        sum_out.take(which)
        own = wq[2, pl.ds((6 + which) * 256, 256), :].astype(jnp.float32)
        datt[pl.ds(which * 256, 256), :] = (own + sum_out.arrived(which, pl.ds(0, 256))).astype(LOW)
        net.store(datt.at[pl.ds(which * 256, 256)], gout_out.at[which])
    for chunk in (3, 2, 1, 0):
        for block in (chunk * 2, chunk * 2 + 1):
            place = pl.ds(block * OWN, OWN)
            net.got(key_grads + block, dkv_inbox.at[place])
            mine = part(block * 256 + net.half * OWN, OWN)
            total = wu[mine, pl.ds(512, 512)].astype(jnp.float32) + dkv_inbox[place, :].astype(jnp.float32)
            wd[place, pl.ds(512, 512)] = total.astype(LOW)
    dqkv = wd.at[:, pl.ds(256, 768)]
    net.store(dqkv, dqkv_out)
    lone[:, pl.ds(1024, 768)] = dot(jnp.ones((8, 1024), LOW), wd[:, pl.ds(256, 768)], NN)
    line_down.take()
    net.store(down_last, down_b)
    line_up.take()
    net.store(up_last, up_b)
    net.drain()


def ahead(lengths, inputs, cotangent, small, w_qkv, w_out, w_up, w_down, qv_bias, up_bias):
    return pl.pallas_call(
        ahead_kernel,
        out_shape=(
            low_shape(OWN, D),
            low_shape(1024, D),
            low_shape(3, D, 256),
            full_shape(8, D),
            low_shape(1024, 768),
            full_shape(OWN, D),
            low_shape(2, 256, 256),
            low_shape(OWN, D),
            low_shape(256, 1024),
            low_shape(256, 1024),
            low_shape(1024, 256),
            low_shape(1024, 256),
            full_shape(8, D),
            full_shape(8, 1792),
        ),
        in_specs=[SM, HBM, HBM, *[VM] * 6, HBM, HBM, HBM, HBM, VM, VM],
        out_specs=(HBM,) * 12 + (VM, VM),
        scratch_shapes=[
            pltpu.VMEM((OWN, D), LOW),
            pltpu.VMEM((1024, D), LOW),
            pltpu.VMEM((1024, D), LOW),
            pltpu.VMEM((1024, 256), LOW),
            pltpu.VMEM((2, 2048, 256), LOW),
            pltpu.VMEM((1024, 256), LOW),
            pltpu.VMEM((3, D, 256), LOW),
            pltpu.VMEM((256, D), LOW),
            pltpu.VMEM((8, D), jnp.float32),
            *reduce_scratch(),
            pltpu.VMEM((OWN, D), jnp.float32),
            pltpu.VMEM((1024, D), LOW),
            pltpu.VMEM((1024, 1024), LOW),
            pltpu.VMEM((1024, 1024), LOW),
            pltpu.VMEM((D, 1024), LOW),
            pltpu.VMEM((1024, D), LOW),
            pltpu.VMEM((8, 256), jnp.float32),
            pltpu.VMEM((1024, 2), jnp.float32),
            pltpu.VMEM((1024, 256), LOW),
            pltpu.VMEM((1024, 256), jnp.float32),
            pltpu.VMEM((1024, 512), LOW),
            pltpu.VMEM((4, 1024, 256), LOW),
            pltpu.VMEM((3, 1024, 256), LOW),
            pltpu.VMEM((1024, 256), LOW),
            pltpu.VMEM((4, 256, 1024), LOW),
            pltpu.VMEM((4, 256, 1024), LOW),
            pltpu.VMEM((3, 256, 1024), LOW),
            pltpu.VMEM((256, 1024), LOW),
            pltpu.VMEM((6, 256, 256), LOW),
            *sems(232, 32),
        ],
        compiler_params=pltpu.CompilerParams(
            collective_id=1, has_side_effects=True, vmem_limit_bytes=64 * 2**20 - 2**16
        ),
        cost_estimate=pl.CostEstimate(flops=40 * 10**9, bytes_accessed=30 * 10**6, transcendentals=2 * 10**6),
    )(lengths, inputs, cotangent, *small, w_qkv, w_out, w_up, w_down, qv_bias, up_bias)


def in_rows(ref, body):
    rows, width = ref.shape[-2:]
    step = min(rows, 2 ** ((32768 // width).bit_length() - 1))
    tiles(rows // step, lambda t: body(part(t * step, step)))


class SideReduce:
    def __init__(self, net, block, inbox, first):
        self.net, self.block, self.inbox, self.slot = net, block, inbox, net.slots(8)
        self.windows = (pl.ds(0, first), pl.ds(first, inbox.shape[1] - first))

    def other(self, dy):
        return (1 - self.net.half) * 4 + (self.net.y + dy) % 4

    def mine(self, dy):
        return self.net.half * 4 + (self.net.y + dy) % 4

    def give(self, dy):
        for side, device in enumerate((self.net.partner(), self.net.cousin())):
            rows = self.windows[side]
            self.net.push(
                self.slot + dy * 2 + side, self.block(dy).at[rows], self.inbox.at[dy, rows], device
            )

    def take(self, dy):
        for side in range(2):
            self.net.got(self.slot + dy * 2 + side, self.inbox.at[dy, self.windows[side]])


class LineReduce:
    def __init__(self, net, blocks, inbox, last):
        self.net, self.blocks, self.inbox, self.last = net, blocks, inbox, last
        self.slot = net.slots(4)

    def give(self, dy):
        self.net.push(self.slot + dy - 1, self.blocks.at[dy], self.inbox.at[dy - 1], self.net.at(dy=dy))

    def settle(self):
        for dy in (1, 2, 3):
            self.net.got(self.slot + dy - 1, self.inbox.at[dy - 1])

        def add(rows):
            total = self.blocks[0, rows, :].astype(jnp.float32)
            for i in range(3):
                total += self.inbox[i, rows, :].astype(jnp.float32)
            self.blocks[0, rows, :] = total.astype(LOW)

        in_rows(self.last, add)

    def close(self):
        self.settle()
        self.net.push(self.slot + 3, self.blocks.at[0], self.last, self.net.at(dx=2))

    def take(self):
        self.net.got(self.slot + 3, self.last)

    def finish(self, emit):
        self.take()
        in_rows(
            self.last,
            lambda rows: emit(rows, self.blocks[0, rows, :].astype(jnp.float32) + self.last[rows, :].astype(jnp.float32)),
        )


class LineFirst:
    def __init__(self, net, block, inbox, total, side, last, first):
        self.net, self.block, self.inbox, self.total, self.side, self.last = net, block, inbox, total, side, last
        self.slot = net.slots(9)
        self.windows = (pl.ds(0, first), pl.ds(first, inbox.shape[1] - first))

    def owner(self, which, dy):
        half = 1 - self.net.half if which else self.net.half
        return half * 4 + (self.net.y + dy) % 4

    def give(self, which, dy):
        place = which * 3 + dy - 1
        self.net.push(self.slot + place, self.block(place), self.inbox.at[place], self.net.at(dy=dy))

    def take(self, which):
        for dy in (1, 2, 3):
            self.net.got(self.slot + which * 3 + dy - 1, self.inbox.at[which * 3 + dy - 1])

    def arrived(self, which, rows):
        return sum(self.inbox[which * 3 + i, rows, :].astype(jnp.float32) for i in range(3))

    def sideways(self):
        for i, device in enumerate((self.net.partner(), self.net.cousin())):
            rows = self.windows[i]
            self.net.push(self.slot + 6 + i, self.total.at[1, rows], self.side.at[rows], device)

    def close(self):
        for i in range(2):
            self.net.got(self.slot + 6 + i, self.side.at[self.windows[i]])

        def add(rows):
            total = self.total[0, rows, :].astype(jnp.float32) + self.side[rows, :].astype(jnp.float32)
            self.total[0, rows, :] = total.astype(LOW)

        in_rows(self.side, add)
        self.net.push(self.slot + 8, self.total.at[0], self.last, self.net.at(dx=2))

    def finish(self, emit):
        self.net.got(self.slot + 8, self.last)
        in_rows(
            self.last,
            lambda rows: emit(
                rows, self.total[0, rows, :].astype(jnp.float32) + self.last[rows, :].astype(jnp.float32)
            ),
        )


def emit_to(ref):
    def emit(rows, values):
        ref[rows, :] = values

    return emit


def norm_back(grad, centred, inverse, gain):
    scaled = grad * gain
    return inverse * (
        scaled - jnp.mean(scaled, -1, keepdims=True) - centred * jnp.mean(scaled * centred, -1, keepdims=True)
    )


def norm_parts(values):
    middle = jnp.mean(values, -1, keepdims=True)
    spread = jnp.mean(values * values, -1, keepdims=True) - middle * middle
    inverse = lax.rsqrt(spread + EPSILON)
    return (values - middle) * inverse, inverse


def column_sums(values):
    return jnp.sum(values, 0, keepdims=True)


def attend_back_chunk(chunk, q, kv, grad, att, lse, dq, dkv, half, length):
    slots = pl.ds(chunk * 512, 512)
    for head in range(2):
        at = pl.ds(head * HEAD, HEAD)
        key, value = kv(0, slots, head), kv(1, slots, head)
        dkey, dvalue = jnp.zeros((512, HEAD), jnp.float32), jnp.zeros((512, HEAD), jnp.float32)
        for group in range(chunk, 4):
            rows = pl.ds(group * 256, 256)
            query, upstream = q(rows, head), grad[rows, at]
            delta = jnp.sum(upstream.astype(jnp.float32) * att[rows, at].astype(jnp.float32), -1, keepdims=True)
            scores = dot(query, key, NT) * SCALE
            slot = chunk * 512 + lax.broadcasted_iota(jnp.int32, (1, 512), 1)
            allowed = slot < length
            if group == chunk:
                allowed = allowed & (slot <= place_rows(group, half))
            probs = jnp.exp(jnp.where(allowed, scores - lse[rows, pl.ds(head, 1)], -HUGE))
            dscores = (probs * (dot(upstream, value, NT) - delta)).astype(LOW)
            share = dot(dscores, key, NN)
            if group == chunk:
                dq[rows, at] = share
            else:
                dq[rows, at] += share
            dkey += dot(dscores, query, TN)
            dvalue += dot(probs.astype(LOW), upstream, TN)
        dkv(0, slots, head, (dkey * SCALE).astype(LOW))
        dkv(1, slots, head, dvalue.astype(LOW))


class Everyone:
    def __init__(self, net, axis, inbox):
        self.net, self.axis, self.inbox, self.slot = net, axis, inbox, net.slots(7)
        self.index = net.row if axis == "row" else net.col

    def device(self, shift):
        net, index = self.net, (self.index + shift) % 8
        row, col = (index, net.col) if self.axis == "row" else (net.row, index)
        return {"dp": net.dp, "row": row, "col": col}

    def begin(self, src_of):
        for shift in range(1, 8):
            to = (self.index + shift) % 8
            self.net.push(self.slot + shift - 1, src_of(to), self.inbox.at[self.index], self.device(shift))
        self.copy = self.net.move(src_of(self.index), self.inbox.at[self.index])

    def total(self):
        self.copy.wait()
        for shift in range(1, 8):
            self.net.got(self.slot + shift - 1, self.inbox.at[(self.index + 8 - shift) % 8])
        total = self.inbox[0]
        for i in range(1, 8):
            total += self.inbox[i]
        return total


class Blocks:
    def __init__(self, net, src, inbox):
        self.net, self.src, self.inbox, self.slot = net, src, inbox, net.slots(15)

    def begin(self):
        net = self.net
        place = self.inbox.at[net.dp * 8 + net.row]
        for shift in range(16):
            row = (net.row + shift) % 8
            block = self.src.at[:, part(row * 256, 256)]
            if shift == 0:
                self.copy = net.move(block, place)
            else:
                dp = net.dp if shift < 8 else 1 - net.dp
                net.push(self.slot + shift - 1, block, place, {"dp": dp, "row": row, "col": net.col})

    def total(self):
        net = self.net
        self.copy.wait()
        for shift in range(1, 16):
            dp = net.dp if shift < 8 else 1 - net.dp
            net.got(self.slot + shift - 1, self.inbox.at[dp * 8 + (net.row + 16 - shift) % 8])
        total = self.inbox[0]
        for i in range(1, 16):
            total += self.inbox[i]
        return total


def fourth_kernel(
    dqkv_in, n1_in, wq_in, x_in, dmid_in, wide, gout_in, mixed_in, sums, single,
    grad_low, mixed_out, qkv_grad, out_out, wide_grad, lone_grad,
    dqkv, n1, wq, x, dmid, grad_own, mixed_own, mixed, out_grad, terms, near, left, right, ends,
    gout, gout_side, gout_last, gq, gq_side, gq_line, gq_last, gkv, gkv_line, gkv_total, gkv_side, gkv_last,
    vector, wide_cols, wide_part, wide_rows, packed, single_rows, single_part, single_last,
    send, recv, local,
):
    net = Net(send, recv, local)
    load = {}
    for name, a, b in (
        ("dqkv", dqkv_in, dqkv), ("wq", wq_in, wq), ("n1", n1_in, n1), ("gout", gout_in, gout),
        ("mixed", mixed_in, mixed_own), ("x", x_in, x), ("dmid", dmid_in, dmid),
    ):
        load[name] = net.move(a, b)
    cols = [{"dp": net.dp, "row": net.row, "col": (net.col + d) % 8} for d in range(1, 8)]
    across = [{"dp": 1 - net.dp, "row": (net.row + d) % 8, "col": net.col} for d in (0, 1, 2, 3, 5, 6, 7)]
    net.greet(across, cols)
    back = ColReduce(net, terms, near, left, right, ends)
    side_q = SideReduce(net, lambda dy: gq.at[dy], gq_side, 128)
    line_q = LineReduce(net, gq_side, gq_line, gq_last)
    sum_kv = LineFirst(net, lambda i: gkv.at[i], gkv_line, gkv_total, gkv_side, gkv_last, 128)
    sum_out = LineFirst(net, None, gout_side, gout, gout_side, gout_last, 128)
    wide_a, wide_b = Everyone(net, "col", wide_cols), Blocks(net, wide_part, wide_rows)
    single_a = Everyone(net, "row", single_rows)
    crossing = net.slots(1)

    def feature_block(ref):
        return lambda r: ref.at[:, part(r * 256, 256)]

    def token_block(ref):
        return lambda r: ref.at[(r // 2) % 2, r % 2, part(r // 4 * OWN, OWN)]

    mixed_swap = Swap(net, feature_block(mixed_own), token_block(mixed))
    grad_swap = Swap(net, feature_block(grad_own), token_block(grad_low))

    def descend(dz):
        rows = part((net.z + dz) % 4 * 256, 256)

        def tile(t):
            at = part(t * 512, 512)
            total = dot(dqkv[rows, pl.ds(0, 256)], wq[0, at, :], NT)
            for i in (1, 2):
                total += dot(dqkv[rows, pl.ds(i * 256, 256)], wq[i, at, :], NT)
            terms[rows, at] = total.astype(LOW)

        tiles(4, tile)
        back.give(dz)

    def q_tile(r):
        return dot(n1[:, part(r * 256, 256)], dqkv[:, pl.ds(0, 256)], TN)

    def kv_tile(r):
        return dot(n1[:, part(r * 256, 256)], dqkv[:, pl.ds(256, 512)], TN)

    def q_give(dy):
        gq[dy] = q_tile(side_q.other(dy)).astype(LOW)
        side_q.give(dy)

    def q_add(dy):
        side_q.take(dy)
        gq_side[dy] = (q_tile(side_q.mine(dy)) + gq_side[dy].astype(jnp.float32)).astype(LOW)
        if dy:
            line_q.give(dy)

    def kv_give(which, dy):
        gkv[which * 3 + dy - 1] = kv_tile(sum_kv.owner(which, dy)).astype(LOW)
        sum_kv.give(which, dy)

    def kv_add(which):
        sum_kv.take(which)
        total = kv_tile(sum_kv.owner(which, 0)) + sum_kv.arrived(which, pl.ds(0, 256))
        gkv_total[which] = total.astype(LOW)

    for i in range(7):
        packed[i : i + 1, :] = single[0:1, i * 256 : (i + 1) * 256]
    packed[7:8, :] = jnp.zeros((1, 256), jnp.float32)
    single_a.begin(lambda r: packed)
    for name in ("dqkv", "wq", "n1"):
        load[name].wait()
    for dy in (2, 1, 3):
        kv_give(1, dy)
    descend(2)
    kv_give(0, 2)
    descend(1)
    back.far()
    kv_give(0, 1)
    kv_give(0, 3)
    descend(3)
    back.own(1)
    back.own(3)
    for dy in (2, 1, 3, 0):
        q_give(dy)
    descend(0)
    load["gout"].wait()
    sum_out.sideways()
    back.forward(1)
    back.forward(3)
    load["mixed"].wait()
    mixed_swap.begin()
    for dy in (2, 1, 3, 0):
        q_add(dy)
    load["x"].wait()
    load["dmid"].wait()
    back.finish()
    totals = [jnp.zeros((1, D), jnp.float32)] * 2
    for piece in range(4):
        rows = pl.ds(piece * 32, 32)
        grad = back.result(piece * 32, 32)
        centred, inverse = norm_parts(x[rows, :].astype(jnp.float32))
        value = dmid[rows, :] + norm_back(grad, centred, inverse, wide[0:1, :])
        grad_own[rows, :] = value.astype(LOW)
        totals = [a + column_sums(b) for a, b in zip(totals, (grad * centred, grad))]
    vector[...] = sums[...] + jnp.concatenate([*totals, jnp.zeros((6, D), jnp.float32)], 0)
    wide_a.begin(lambda r: vector)
    grad_swap.begin()
    kv_add(1)
    sum_kv.sideways()
    single_part[...] = single_a.total()
    net.push(crossing, single_part, single_last, net.at(dx=2))
    kv_add(0)
    wide_part[...] = wide_a.total()
    wide_b.begin()
    sum_kv.close()
    sum_out.close()
    line_q.close()
    mixed_swap.finish()
    net.store(mixed, mixed_out)
    grad_swap.finish()
    wide_grad[...] = wide_b.total()
    net.got(crossing, single_last)
    lone_grad[...] = single_part[...] + single_last[...]

    def emit_q(rows, values):
        qkv_grad[0, rows, :] = values

    def emit_kv(rows, values):
        for i in range(2):
            qkv_grad[1 + i, rows, :] = values[:, i * 256 : (i + 1) * 256]

    sum_out.finish(emit_to(out_grad))
    line_q.finish(emit_q)
    sum_kv.finish(emit_kv)
    net.store(out_grad, out_out)
    net.drain()


def fourth(dqkv, n1, wq, x, dmid, wide, gout, mixed, sums, lone):
    return pl.pallas_call(
        fourth_kernel,
        out_shape=(
            low_shape(2, 2, 256, 256),
            low_shape(2, 2, 256, 256),
            full_shape(3, 256, 256),
            full_shape(256, 256),
            full_shape(8, 256),
            full_shape(8, 256),
        ),
        in_specs=[HBM, HBM, HBM, HBM, HBM, VM, HBM, HBM, VM, VM],
        out_specs=(VM, HBM, VM, HBM, VM, VM),
        scratch_shapes=[
            pltpu.VMEM((1024, 768), LOW),
            pltpu.VMEM((1024, D), LOW),
            pltpu.VMEM((3, D, 256), LOW),
            pltpu.VMEM((OWN, D), LOW),
            pltpu.VMEM((OWN, D), jnp.float32),
            pltpu.VMEM((OWN, D), LOW),
            pltpu.VMEM((OWN, D), LOW),
            pltpu.VMEM((2, 2, 256, 256), LOW),
            pltpu.VMEM((256, 256), jnp.float32),
            *reduce_scratch(),
            pltpu.VMEM((2, 256, 256), LOW),
            pltpu.VMEM((256, 256), LOW),
            pltpu.VMEM((256, 256), LOW),
            pltpu.VMEM((4, 256, 256), LOW),
            pltpu.VMEM((4, 256, 256), LOW),
            pltpu.VMEM((3, 256, 256), LOW),
            pltpu.VMEM((256, 256), LOW),
            pltpu.VMEM((6, 256, 512), LOW),
            pltpu.VMEM((6, 256, 512), LOW),
            pltpu.VMEM((2, 256, 512), LOW),
            pltpu.VMEM((256, 512), LOW),
            pltpu.VMEM((256, 512), LOW),
            pltpu.VMEM((8, D), jnp.float32),
            pltpu.VMEM((8, 8, D), jnp.float32),
            pltpu.VMEM((8, D), jnp.float32),
            pltpu.VMEM((16, 8, 256), jnp.float32),
            pltpu.VMEM((8, 256), jnp.float32),
            pltpu.VMEM((8, 8, 256), jnp.float32),
            pltpu.VMEM((8, 256), jnp.float32),
            pltpu.VMEM((8, 256), jnp.float32),
            *sems(112, 24),
        ],
        compiler_params=pltpu.CompilerParams(
            collective_id=4, has_side_effects=True, vmem_limit_bytes=60 * 2**20
        ),
        cost_estimate=pl.CostEstimate(flops=40 * 10**9, bytes_accessed=30 * 10**6, transcendentals=2 * 10**6),
    )(dqkv, n1, wq, x, dmid, wide, gout, mixed, sums, lone)


def hand_over_kernel(
    mixed_in, grad_in, qkv_in, out_in, up_a, up_b, down_a, down_b, wide, lone,
    mixed, input_grad, gain1, bias1, qkv, qv, out, out_bias, gain2, bias2, up, up_bias, down, down_bias,
    *rest,
):
    between, done = rest[:-1], rest[-1]
    pairs = ((qkv_in, qkv), (mixed_in, mixed), (out_in, out))
    fetches = [pltpu.make_async_copy(a, m, done.at[i]) for i, ((a, b), m) in enumerate(zip(pairs, between))]
    copies = [pltpu.make_async_copy(m, b, done.at[3 + i]) for i, ((a, b), m) in enumerate(zip(pairs, between))]
    for fetch in fetches:
        fetch.start()
    for ref, a, b in ((down, down_a, down_b), (up, up_a, up_b)):

        def add(rows):
            ref[rows, :] = a[rows, :].astype(jnp.float32) + b[rows, :].astype(jnp.float32)

        in_rows(ref, add)
    for fetch, copy in zip(fetches, copies):
        fetch.wait()
        copy.start()
    for i, ref in enumerate((gain1, bias1, out_bias, gain2, bias2, down_bias)):
        ref[...] = wide[i : i + 1, :]
    for i in range(4):
        up_bias[:, i * 256 : (i + 1) * 256] = lone[i : i + 1, :]
    qv[0:1, :] = lone[4:5, :]
    qv[1:2, :] = lone[6:7, :]
    for i in range(2):
        for j in range(2):
            input_grad[i, j] = grad_in[i, j].astype(jnp.float32)
    for copy in copies:
        copy.wait()


def hand_over(mixed, grad, qkv, out, up_a, up_b, down_a, down_b, wide, lone):
    vector = full_shape(1, 256)
    return pl.pallas_call(
        hand_over_kernel,
        out_shape=(
            low_shape(2, 2, 256, 256),
            full_shape(2, 2, 256, 256),
            vector,
            vector,
            full_shape(3, 256, 256),
            full_shape(2, 256),
            full_shape(256, 256),
            vector,
            vector,
            vector,
            full_shape(256, 1024),
            full_shape(1, 1024),
            full_shape(1024, 256),
            vector,
        ),
        in_specs=[HBM, VM, HBM, HBM, VM, VM, VM, VM, VM, VM],
        out_specs=(HBM, VM, VM, VM, HBM, VM, HBM, VM, VM, VM, VM, VM, VM, VM),
        scratch_shapes=[
            pltpu.VMEM((3, 256, 256), jnp.float32),
            pltpu.VMEM((2, 2, 256, 256), LOW),
            pltpu.VMEM((256, 256), jnp.float32),
            pltpu.SemaphoreType.DMA((6,)),
        ],
        compiler_params=pltpu.CompilerParams(vmem_limit_bytes=63 * 2**20),
    )(mixed, grad, qkv, out, up_a, up_b, down_a, down_b, wide, lone)


def shards(
    inputs,
    lengths,
    ln1_gain,
    ln1_bias,
    w_qkv,
    qv_bias,
    w_out,
    out_bias,
    ln2_gain,
    ln2_bias,
    w_up,
    up_bias,
    w_down,
    down_bias,
    cotangent,
):
    small = [a.reshape(1, 256) for a in (ln1_gain, ln1_bias, out_bias, ln2_gain, ln2_bias, down_bias)]
    x, all1, wq, wide, dqkv, dmid, gout, mixed, up_a, up_b, down_a, down_b, sums, lone = ahead(
        lengths, inputs, cotangent, small, w_qkv, w_out, w_up, w_down, qv_bias, up_bias.reshape(1, 1024)
    )
    grad, mixed, g_qkv, g_out, wide_grad, lone_grad = fourth(dqkv, all1, wq, x, dmid, wide, gout, mixed, sums, lone)
    outs = hand_over(mixed, grad, g_qkv, g_out, up_a, up_b, down_a, down_b, wide_grad, lone_grad)
    return tuple(a.reshape(-1) if a.shape[0] == 1 else a for a in outs)


def solution(mesh):
    tokens = P(None, "dp", "col", "row")
    in_specs = (
        tokens,
        P(None, "dp"),
        P("row"),
        P("row"),
        P(None, "row", "col"),
        P(None, "col"),
        P("col", "row"),
        P("row"),
        P("row"),
        P("row"),
        P("row", "col"),
        P("col"),
        P("col", "row"),
        P("row"),
        tokens,
    )
    out_specs = (
        tokens,
        tokens,
        P("row"),
        P("row"),
        P(None, "row", "col"),
        P(None, "col"),
        P("col", "row"),
        P("row"),
        P("row"),
        P("row"),
        P("row", "col"),
        P("col"),
        P("col", "row"),
        P("row"),
    )
    return jax.shard_map(shards, mesh=mesh, in_specs=in_specs, out_specs=out_specs, check_vma=False)
```

```python
import functools

import jax
import jax.numpy as jnp
from jax import lax
from jax.experimental import pallas as pl
from jax.experimental.pallas import tpu as pltpu
from jax.sharding import PartitionSpec as P

D = 2048
HEAD = 128
SCALE = HEAD**-0.5
EPSILON = 1e-05
HUGE = 1e30
LOW = jnp.bfloat16
OWN = 128
VMEM_LIMIT = 56 * 2**20


def dot(a, b, contract):
    return lax.dot_general(a, b, ((contract[0], contract[1]), ((), ())), preferred_element_type=jnp.float32)


NN = ((1,), (0,))
NT = ((1,), (1,))
TN = ((0,), (0,))


def place_rows(group, half):
    row = lax.broadcasted_iota(jnp.int32, (256, 1), 0)
    return (2 * group + row // OWN) * 256 + half * OWN + row % OWN


def allowed_keys(group, extent, half, length):
    slot = lax.broadcasted_iota(jnp.int32, (256, extent), 1)
    return (slot <= place_rows(group, half)) & (slot < length)


MESH = pl.DeviceIdType.MESH
HBM = pl.BlockSpec(memory_space=pl.ANY)
VM = pl.BlockSpec(memory_space=pltpu.VMEM)
SM = pl.BlockSpec(memory_space=pltpu.SMEM)


def part(start, size):
    return pl.ds(pl.multiple_of(start, size), size)


class Net:
    def __init__(self, send, recv, local):
        self.send, self.recv, self.local = send, recv, local
        self.used, self.local_used, self.live, self.own = 0, 0, [], []
        self.dp, self.row, self.col = (lax.axis_index(a) for a in ("dp", "row", "col"))
        self.half, self.y = self.row // 4, self.row % 4
        self.x = self.dp * 2 + self.half
        self.z, self.core = self.col // 2, self.col % 2

    def at(self, dx=0, dy=0, dz=0, other_core=False):
        x, y, z = (self.x + dx) % 4, (self.y + dy) % 4, (self.z + dz) % 4
        core = 1 - self.core if other_core else self.core
        return {"dp": x // 2, "row": (x % 2) * 4 + y, "col": z * 2 + core}

    def mate(self, shift):
        return {"dp": self.dp, "row": (self.row + shift) % 8, "col": self.col}

    def partner(self):
        return self.mate(4)

    def cousin(self):
        return {"dp": 1 - self.dp, "row": (self.row + 4) % 8, "col": self.col}

    def greet(self, more=(), cols=()):
        devices = [self.mate(d) for d in range(1, 8)]
        devices += [self.cousin()]
        devices += cols or [self.at(dz=1), self.at(dz=3), self.at(other_core=True)]
        devices += more
        self.expected = len(devices)
        for device in devices:
            pl.semaphore_signal(pltpu.get_barrier_semaphore(), inc=1, device_id=device, device_id_type=MESH)

    def meet(self):
        pl.semaphore_wait(pltpu.get_barrier_semaphore(), self.expected)

    def slots(self, count):
        self.used += count
        return self.used - count

    def _copy(self, slot, src, dst, device):
        return pltpu.make_async_remote_copy(
            src_ref=src,
            dst_ref=dst,
            send_sem=self.send.at[slot],
            recv_sem=self.recv.at[slot],
            device_id=device,
            device_id_type=MESH,
        )

    def push(self, slot, src, dst, device):
        copy = self._copy(slot, src, dst, device)
        copy.start()
        self.live.append(copy)

    def got(self, slot, ref):
        self._copy(slot, ref, ref, self.at(other_core=True)).wait_recv()

    def flush(self, copies):
        for copy in copies:
            copy.wait_send()
        self.live = [copy for copy in self.live if not any(copy is other for other in copies)]

    def move(self, src, dst):
        copy = pltpu.make_async_copy(src, dst, self.local.at[self.local_used])
        self.local_used += 1
        copy.start()
        return copy

    def store(self, src, dst):
        self.own.append(self.move(src, dst))

    def drain(self):
        for copy in self.live:
            copy.wait_send()
        for copy in self.own:
            copy.wait()


class ColGather:
    def __init__(self, net, buf):
        self.net, self.buf, self.slot = net, buf, net.slots(14)
        self.sent = []

    def rows(self, dz, other_core, piece):
        net = self.net
        core = 1 - net.core if other_core else net.core
        return self.buf.at[part(((net.z + dz) % 4 * 2 + core) * OWN + 64 * piece, 64)]

    def move(self, slot, where, piece, **to):
        ref = self.rows(where, False, piece)
        self.net.push(self.slot + slot, ref, ref, self.net.at(**to))
        self.sent.append(self.net.live[-1])

    def flush(self):
        self.net.flush(self.sent)

    def got(self, slot, dz, piece, other_core=False):
        self.net.got(self.slot + slot, self.rows(dz, other_core, piece))

    def begin(self):
        self.move(0, 0, 0, dz=1)
        self.move(3, 0, 1, dz=3)
        self.move(1, 0, 1, dz=1)
        self.move(2, 0, 0, dz=3)
        self.move(6, 0, 0, other_core=True)
        self.move(7, 0, 1, other_core=True)

    def hop(self):
        self.pass_on()
        self.take_rest()

    def pass_on(self):
        self.got(0, 3, 0)
        self.move(4, 3, 0, dz=1)
        self.got(3, 1, 1)
        self.move(5, 1, 1, dz=3)
        self.move(8, 3, 0, other_core=True)
        self.move(11, 1, 1, other_core=True)

    def take_rest(self):
        self.got(1, 3, 1)
        self.move(9, 3, 1, other_core=True)
        self.got(2, 1, 0)
        self.move(10, 1, 0, other_core=True)

    def far(self):
        self.got(4, 2, 0)
        self.move(12, 2, 0, other_core=True)
        self.got(5, 2, 1)
        self.move(13, 2, 1, other_core=True)

    def pair(self, dz):
        slot = {0: 6, 3: 8, 1: 10, 2: 12}[dz]
        self.got(slot, dz, 0, True)
        self.got(slot + 1, dz, 1, True)


class RowGather:
    def __init__(self, net, src, buf, whole, parts):
        self.net, self.src, self.buf, self.whole, self.parts = net, src, buf, whole, parts
        self.slot, self.sent = net.slots(11), []

    def place(self, dy, other=False):
        net = self.net
        half = 1 - net.half if other else net.half
        return self.whole(self.buf, half * 4 + (net.y + dy) % 4)

    def sideways(self, dy, src, sides=(0, 1)):
        net, there = self.net, self.place(dy)
        devices = (net.partner(), net.cousin())
        for side in sides:
            net.push(
                self.slot + 3 + dy * 2 + side, self.parts(src, side), self.parts(there, side), devices[side]
            )
            self.sent.append(net.live[-1])

    def flush(self):
        self.net.flush(self.sent)

    def begin(self):
        net, mine = self.net, self.place(0)
        for dy in (1, 3, 2):
            net.push(self.slot + dy - 1, self.src, mine, net.at(dy=dy))
            self.sent.append(net.live[-1])
        self.copy = net.move(self.src, mine)

    def begin_sideways(self, sides=(0, 1)):
        self.sideways(0, self.src, sides)

    def step(self, dy, sides=(0, 1)):
        ref = self.place(4 - dy)
        self.net.got(self.slot + dy - 1, ref)
        self.sideways(4 - dy, ref, sides)

    def follow(self, dy, sides):
        self.sideways(4 - dy, self.place(4 - dy), sides)

    def steps(self):
        for dy in (1, 3, 2):
            self.step(dy)

    def finish(self):
        self.copy.wait()
        for dy in range(4):
            for side in range(2):
                self.net.got(self.slot + 3 + dy * 2 + side, self.parts(self.place(dy, True), side))


def cut(rows):
    def parts(ref, side):
        total = ref.shape[-2]
        window = pl.ds(0, rows) if side == 0 else pl.ds(rows, total - rows)
        return ref.at[:, window] if len(ref.shape) == 3 else ref.at[window]

    return parts


class Swap:
    def __init__(self, net, src_of, dst_of):
        self.net, self.src_of, self.dst_of, self.slot = net, src_of, dst_of, net.slots(7)

    def begin(self):
        net = self.net
        for shift in range(1, 8):
            net.push(self.slot + shift - 1, self.src_of((net.row + shift) % 8), self.dst_of(net.row), net.mate(shift))
        self.copy = net.move(self.src_of(net.row), self.dst_of(net.row))

    def finish(self):
        net = self.net
        self.copy.wait()
        for shift in range(1, 8):
            net.got(self.slot + shift - 1, self.dst_of((net.row + 8 - shift) % 8))


def norm_rows(values, gain, bias):
    middle = jnp.mean(values, -1, keepdims=True)
    spread = jnp.mean(values * values, -1, keepdims=True) - middle * middle
    inverse = lax.rsqrt(spread + EPSILON)
    centred = (values - middle) * inverse
    return centred * gain + bias


def attend_group(q, kv, head, group, half, length):
    cols, rows, extent = pl.ds(head * HEAD, HEAD), pl.ds(group * 256, 256), 512 * (group + 1)
    scores = dot(q[rows, cols], kv[0, :extent, cols], NT) * SCALE
    scores = jnp.where(allowed_keys(group, extent, half, length), scores, -HUGE)
    highest = jnp.max(scores, -1, keepdims=True)
    weights = jnp.exp(scores - highest)
    total = jnp.sum(weights, -1, keepdims=True)
    out = dot(weights.astype(LOW), kv[1, :extent, cols], NN) / total
    return out, highest + jnp.log(total)


def low_shape(*shape):
    return jax.ShapeDtypeStruct(shape, LOW)


def full_shape(*shape):
    return jax.ShapeDtypeStruct(shape, jnp.float32)


def sems(remote, local):
    return [
        pltpu.SemaphoreType.DMA((remote,)),
        pltpu.SemaphoreType.DMA((remote,)),
        pltpu.SemaphoreType.DMA((local,)),
    ]


class ColReduce:
    def __init__(self, net, terms, near, left, right, ends):
        self.net, self.terms, self.near, self.left, self.right, self.ends = net, terms, near, left, right, ends
        self.slot = net.slots(10)
        self.sent = []

    def push(self, *copy):
        self.net.push(*copy)
        self.sent.append(self.net.live[-1])

    def flush(self):
        self.net.flush(self.sent)

    def block(self, dz, other_core=False):
        net = self.net
        core = 1 - net.core if other_core else net.core
        return part(((net.z + dz) % 4 * 2 + core) * OWN, OWN)

    def rows(self, dz, piece):
        net = self.net
        return part(((net.z + dz) % 4 * 2 + net.core) * OWN + 64 * piece, 64)

    def give(self, dz):
        self.push(
            self.slot + dz, self.terms.at[self.block(dz, True)], self.near.at[pl.ds(dz * OWN, OWN)], self.net.at(other_core=True)
        )

    def fold(self, dz):
        near = self.near.at[pl.ds(dz * OWN, OWN)]
        self.net.got(self.slot + dz, near)
        block = self.block(dz)
        self.terms[block, :] = (self.terms[block, :].astype(jnp.float32) + near[...].astype(jnp.float32)).astype(LOW)

    def send(self, slot, dz, piece, dst, side):
        self.push(self.slot + slot, self.terms.at[self.rows(dz, piece)], dst, self.net.at(dz=side))

    def far(self):
        self.fold(2)
        self.send(4, 2, 0, self.left, 1)
        self.send(5, 2, 1, self.right, 3)

    def own(self, dz):
        self.fold(dz)
        side = 0 if dz == 1 else 1
        self.send(6 + side * 2 + 1 - side, dz, 1 - side, self.ends.at[side, pl.ds((1 - side) * 64, 64)], dz)

    def forward(self, dz):
        side = 0 if dz == 1 else 1
        inbox = self.left if dz == 1 else self.right
        self.net.got(self.slot + 4 + side, inbox)
        rows = self.rows(dz, side)
        self.terms[rows, :] = (self.terms[rows, :].astype(jnp.float32) + inbox[...].astype(jnp.float32)).astype(LOW)
        self.send(6 + side * 2 + side, dz, side, self.ends.at[side, pl.ds(side * 64, 64)], dz)

    def finish(self):
        self.net.got(self.slot, self.near.at[pl.ds(0, OWN)])
        for side in range(2):
            for piece in range(2):
                self.net.got(self.slot + 6 + side * 2 + piece, self.ends.at[side, pl.ds(piece * 64, 64)])

    def result(self, start, size):
        block = part(self.net.col * OWN + start, size)
        total = self.terms[block, :].astype(jnp.float32) + self.near[pl.ds(start, size), :].astype(jnp.float32)
        for side in range(2):
            total += self.ends[side, pl.ds(start, size), :].astype(jnp.float32)
        return total


def reduce_scratch():
    return [
        pltpu.VMEM((1024, D), LOW),
        pltpu.VMEM((4 * OWN, D), LOW),
        pltpu.VMEM((64, D), LOW),
        pltpu.VMEM((64, D), LOW),
        pltpu.VMEM((2, OWN, D), LOW),
    ]


def tiles(count, body):
    lax.fori_loop(0, count, lambda t, c: (body(t), c)[1], 0)


def ahead_kernel(
    lengths, inputs, cotangent, gain1, bias1, bias_out, gain2, bias2, bias_down, w_qkv, w_out, w_up, w_down, qv_bias, up_bias,
    x_out, n1_out, wq_out, small_out, dqkv_out, dmid_out, gout_out, mixed_out, up_a, up_b, down_a, down_b, sums, lone,
    x, dy, n1, q, kv, att, wq, wo, wide,
    terms, near, left, right, ends, mid, n2, act, slope, wu, wd, small, lse,
    datt, dq, dkv_inbox, down_side, down_line, down_last, up, up_side, up_line, up_last, gout_line,
    send, recv, local,
):
    net = Net(send, recv, local)
    for i, ref in enumerate((gain1, bias1, bias_out, gain2, bias2, bias_down)):
        small[i : i + 1, :] = ref[...]
    small[6:8, :] = jnp.zeros((2, 256), jnp.float32)
    length = lengths[(net.row // 2) % 2, net.row % 2]
    net.greet([net.at(dx=2)])
    net.meet()
    mine = part(net.col * OWN, OWN)

    def token_block(ref):
        return lambda r: ref.at[(r // 2) % 2, r % 2, part(r // 4 * OWN, OWN)]

    def feature_block(ref):
        return lambda r: ref.at[:, part(r * 256, 256)]

    def by_columns(ref, r):
        return ref.at[:, part(r * 256, 256)]

    def by_rows(ref, r):
        return ref.at[part(r * 256, 256)]

    params = Swap(net, lambda r: small, feature_block(wide))
    tokens = Swap(net, token_block(inputs), feature_block(x))
    upstream = Swap(net, token_block(cotangent), lambda r: dy.at[mine, part(r * 256, 256)])
    gather_kv = RowGather(net, w_qkv.at[pl.ds(1, 2)], wq.at[pl.ds(1, 2)], by_columns, cut(128))
    gather_q = RowGather(net, w_qkv.at[pl.ds(0, 1)], wq.at[pl.ds(0, 1)], by_columns, cut(32))
    gather_wo = RowGather(net, w_out, wo, by_columns, cut(16))
    gather_wu = RowGather(net, w_up, wu, by_rows, cut(128))
    gather_wd = RowGather(net, w_down, wd, by_columns, cut(512))
    all_n1, all_dy, all_n2 = ColGather(net, n1), ColGather(net, dy), ColGather(net, n2)
    branch = ColReduce(net, terms, near, left, right, ends)
    keys = net.slots(16)

    def pair(dz):
        return part((net.z + dz) % 4 * 256, 256)

    def project_keys(dz):
        all_n1.pair(dz)
        block = (net.z + dz) % 4
        values = n1[pair(dz), :]
        k = dot(values, wq[1], NN).astype(LOW)
        v = (dot(values, wq[2], NN) + qv_bias[1:2, :]).astype(LOW)
        for i in range(2):
            there = part((block * 2 + i) * 256 + net.half * OWN, OWN)
            kv[0, there, :] = k[i * OWN : (i + 1) * OWN]
            kv[1, there, :] = v[i * OWN : (i + 1) * OWN]

    def key_block(dz, i, half, head):
        there = part(((net.z + dz) % 4 * 2 + i) * 256 + half * OWN, OWN)
        return kv.at[:, there, pl.ds(head * HEAD, HEAD)]

    def swap_keys(dz, head):
        for i in range(2):
            ref = key_block(dz, i, net.half, head)
            net.push(keys + head * 8 + dz * 2 + i, ref, ref, net.partner())

    def take_keys(dz, head):
        for i in range(2):
            net.got(keys + head * 8 + dz * 2 + i, key_block(dz, i, 1 - net.half, head))

    def second_head(group, half, act_on):
        for i in range(2):
            place = part((group * 2 + i) * 256 + half * OWN, OWN)
            ref = kv.at[:, place, pl.ds(HEAD, HEAD)]
            act_on(keys + 8 + group * 2 + i, ref)

    params.begin()
    tokens.begin()
    gather_kv.begin()
    gather_kv.begin_sideways()
    params.finish()
    tokens.finish()
    for piece in range(4):
        rows = pl.ds(piece * 32, 32)
        low = norm_rows(x[rows, :].astype(jnp.float32), wide[0:1, :], wide[1:2, :]).astype(LOW)
        n1[part(net.col * OWN + piece * 32, 32), :] = low
    all_n1.begin()
    keep_x = net.move(x, x_out)
    net.store(wide, small_out)
    all_n1.pass_on()
    gather_kv.steps()
    upstream.begin()
    gather_q.begin()
    gather_q.begin_sideways()
    all_n1.take_rest()
    gather_kv.finish()
    for dz in (0, 3, 1):
        project_keys(dz)
        swap_keys(dz, 0)
    all_n1.far()
    project_keys(2)
    swap_keys(2, 0)
    gather_wo.begin()
    gather_wo.begin_sideways()
    gather_wu.begin()
    gather_wd.begin()
    upstream.finish()
    all_dy.begin()
    gather_q.steps()
    gather_wu.begin_sideways((1,))
    all_dy.pass_on()
    take_keys(0, 0)
    take_keys(3, 0)
    for group in range(4):
        second_head(group, net.half, lambda slot, ref: net.push(slot, ref, ref, net.partner()))
    gather_q.finish()

    def project_queries(t):
        rows = part(t * 256, 256)
        q[rows, :] = (dot(n1[rows, :], wq[0], NN) + qv_bias[0:1, :]).astype(LOW)

    tiles(4, project_queries)
    def attend(head):
        if head == 0:
            take_keys(1, 0)
            take_keys(2, 0)
        for group in range(4):
            if head:
                second_head(group, 1 - net.half, net.got)
            out, logsum = attend_group(q, kv, head, group, net.half, length)
            rows = pl.ds(group * 256, 256)
            att[rows, pl.ds(head * HEAD, HEAD)] = out.astype(LOW)
            lse[rows, pl.ds(head, 1)] = logsum

    gather_wo.steps()
    attend(0)
    all_dy.take_rest()
    all_dy.far()
    attend(1)
    gather_wu.begin_sideways((0,))
    gather_wo.finish()

    def project(dz):
        rows = pair(dz)

        def tile(t):
            cols = part(t * 512, 512)
            terms[rows, cols] = dot(att[rows, :], wo[:, cols], NN).astype(LOW)

        tiles(4, tile)
        branch.give(dz)

    project(2)
    project(1)
    branch.far()
    project(3)
    branch.own(1)
    branch.own(3)
    project(0)
    gather_wu.step(1)
    gather_wu.step(3)
    branch.forward(1)
    branch.forward(3)
    gather_wu.step(2)
    gather_wd.begin_sideways()
    keep_n1 = net.move(n1, n1_out)
    keep_wq = net.move(wq, wq_out)
    branch.finish()
    for piece in range(4):
        rows = pl.ds(piece * 32, 32)
        total = x[rows, :].astype(jnp.float32) + branch.result(piece * 32, 32) + wide[2:3, :]
        mid[rows, :] = total
        low = norm_rows(total, wide[3:4, :], wide[4:5, :]).astype(LOW)
        n2[part(net.col * OWN + piece * 32, 32), :] = low
    for copy in (keep_x, keep_n1, keep_wq):
        copy.wait()
    gather_kv.flush()
    gather_q.flush()
    all_n1.flush()
    all_n2.begin()
    gather_wd.step(1)
    gather_wd.step(3)
    gather_wu.finish()

    def ascend(dz):
        all_n2.pair(dz)
        rows = pair(dz)

        def tile(t):
            cols = part(t * 256, 256)
            hidden = dot(n2[rows, :], wu[:, cols], NN) + up_bias[:, cols]
            share = 0.5 + 0.5 * lax.erf(hidden * 0.5**0.5)
            act[rows, cols] = (hidden * share).astype(LOW)
            density = jnp.exp(-0.5 * hidden * hidden) * (0.5 / jnp.pi) ** 0.5
            slope[rows, cols] = (share + hidden * density).astype(LOW)

        tiles(4, tile)

    ascend(0)
    all_n2.pass_on()
    gather_wd.step(2)
    all_n2.take_rest()
    ascend(3)
    for dz in range(4):
        all_dy.pair(dz)
    all_n2.far()
    ascend(1)
    ascend(2)
    gather_wd.finish()
    back = ColReduce(net, terms, near, left, right, ends)
    all_db, db = ColGather(net, n1), n1
    ffn = ColReduce(net, terms, near, left, right, ends)
    side_down = SideReduce(net, lambda dy: wq.at[dy // 2, pl.ds(dy % 2 * 1024, 1024)], down_side, 384)
    line_down = LineReduce(net, down_side, down_line, down_last)
    side_up = SideReduce(net, lambda dy: up.at[dy], up_side, 96)
    line_up = LineReduce(net, up_side, up_line, up_last)
    sum_out = LineFirst(net, lambda i: wq.at[2, pl.ds(i * 256, 256)], gout_line, None, None, None, 128)
    key_grads = net.slots(8)

    def descend(dz):
        rows = pair(dz)

        def into_hidden(t):
            cols = part(t * 512, 512)
            grad = dot(dy[rows, :], wd[cols, :], NT)
            slope[rows, cols] = (grad * slope[rows, cols].astype(jnp.float32)).astype(LOW)

        def into_width(t):
            cols = part(t * 512, 512)
            terms[rows, cols] = dot(slope[rows, :], wu[cols, :], NT).astype(LOW)

        tiles(2, into_hidden)
        tiles(4, into_width)
        back.give(dz)

    def down_tile(r, t):
        return dot(act[:, part(t * 512, 512)], dy[:, part(r * 256, 256)], TN)

    def up_tile(r, t):
        return dot(n2[:, part(r * 256, 256)], slope[:, part(t * 512, 512)], TN)

    def down_give(step):
        r = side_down.other(step)

        def tile(t):
            wq[step // 2, part(step % 2 * 1024 + t * 512, 512), :] = down_tile(r, t).astype(LOW)

        tiles(2, tile)
        side_down.give(step)

    def down_add(step):
        side_down.take(step)
        r = side_down.mine(step)

        def tile(t):
            units = part(t * 512, 512)
            down_side[step, units, :] = (down_tile(r, t) + down_side[step, units, :].astype(jnp.float32)).astype(LOW)

        tiles(2, tile)

    def up_give(step):
        r = side_up.other(step)

        def tile(t):
            up[step, :, part(t * 512, 512)] = up_tile(r, t).astype(LOW)

        tiles(2, tile)
        side_up.give(step)

    def up_add(step):
        side_up.take(step)
        r = side_up.mine(step)

        def tile(t):
            units = part(t * 512, 512)
            up_side[step, :, units] = (up_tile(r, t) + up_side[step, :, units].astype(jnp.float32)).astype(LOW)

        tiles(2, tile)

    def low_rank(dz):
        all_db.pair(dz)
        rows = pair(dz)
        datt[rows, :] = dot(db[rows, :], wo[...], NT).astype(LOW)

    branch.flush()
    down_give(2)
    down_give(1)
    descend(2)
    descend(1)
    back.far()
    down_give(3)
    descend(3)
    back.own(1)
    back.own(3)
    down_add(2)
    line_down.give(2)
    descend(0)
    down_give(0)
    back.forward(1)
    back.forward(3)
    for step in (1, 3):
        down_add(step)
        line_down.give(step)
    for step in (2, 1, 3, 0):
        up_give(step)
    back.finish()
    totals = [jnp.zeros((1, D), jnp.float32)] * 4
    for piece in range(4):
        rows = pl.ds(piece * 32, 32)
        own = part(net.col * OWN + piece * 32, 32)
        grad = back.result(piece * 32, 32)
        centred, inverse = norm_parts(mid[rows, :])
        upstream = dy[own, :].astype(jnp.float32)
        value = upstream + norm_back(grad, centred, inverse, wide[3:4, :])
        x[rows, :] = (mid[rows, :] + wide[5:6, :]).astype(LOW)
        mid[rows, :] = value
        low = value.astype(LOW)
        db[own, :] = low
        terms_of = (low.astype(jnp.float32), grad * centred, grad, upstream)
        totals = [a + column_sums(b) for a, b in zip(totals, terms_of)]
    all_db.begin()
    zero = jnp.zeros((2, D), jnp.float32)
    sums[...] = jnp.concatenate([zero, *totals, zero], 0)
    net.store(mid, dmid_out)
    back.flush()

    def mix(t):
        cols = part(t * 512, 512)
        for i in range(2):
            rows = pl.ds(i * 512, 512)
            terms[rows, cols] = dot(act[rows, :], wd[:, cols], NN).astype(LOW)

    tiles(4, mix)
    all_db.pass_on()
    down_add(0)
    line_down.close()
    net.store(down_side.at[0], down_a)
    all_db.take_rest()
    low_rank(0)
    for dz in (2, 1, 3, 0):
        ffn.give(dz)
    ffn.far()
    up_add(2)
    line_up.give(2)
    all_db.far()
    for dz in (3, 1, 2):
        low_rank(dz)
    ffn.own(1)
    ffn.own(3)
    def of_keys(which, slots, head):
        return kv[which, slots, pl.ds(head * HEAD, HEAD)]

    def of_queries(rows, head):
        return q[rows, pl.ds(head * HEAD, HEAD)]

    gather_wu.flush()
    gather_wd.flush()
    def keep(which, slots, head, values):
        wu[slots, pl.ds(512 + which * 256 + head * HEAD, HEAD)] = values

    def attend_back(chunk):
        attend_back_chunk(chunk, of_queries, of_keys, datt, att, lse, dq, keep, net.half, length)
        for block in (chunk * 2, chunk * 2 + 1):
            theirs = part(block * 256 + (1 - net.half) * OWN, OWN)
            net.push(
                key_grads + block,
                wu.at[theirs, pl.ds(512, 512)],
                dkv_inbox.at[pl.ds(block * OWN, OWN)],
                net.partner(),
            )

    attend_back(3)
    up_add(1)
    line_up.give(1)
    attend_back(2)
    ffn.forward(1)
    ffn.forward(3)
    up_add(3)
    line_up.give(3)
    attend_back(1)
    attend_back(0)

    def out_block(which, dy):
        r = sum_out.owner(which, dy)
        place = which * 3 + dy - 1 if dy else 6 + which
        wq[2, pl.ds(place * 256, 256), :] = dot(att[...], n1[:, part(r * 256, 256)], TN).astype(LOW)

    for which in (1, 0):
        for dy in (2, 1, 3):
            out_block(which, dy)
            sum_out.give(which, dy)
        out_block(which, 0)
    up_add(0)
    lone[:, pl.ds(0, 1024)] = dot(jnp.ones((8, 1024), LOW), slope[...], NN)
    for piece in range(4):
        rows = pl.ds(piece * 256, 256)
        wd[rows, pl.ds(256, 256)] = (dq[rows, :] * SCALE).astype(LOW)
    ffn.finish()
    for piece in range(4):
        rows = pl.ds(piece * 32, 32)
        x[rows, :] = (x[rows, :].astype(jnp.float32) + ffn.result(piece * 32, 32)).astype(LOW)
    net.store(x, mixed_out)
    line_up.close()
    net.store(up_side.at[0], up_a)
    for which in (1, 0):
        sum_out.take(which)
        own = wq[2, pl.ds((6 + which) * 256, 256), :].astype(jnp.float32)
        datt[pl.ds(which * 256, 256), :] = (own + sum_out.arrived(which, pl.ds(0, 256))).astype(LOW)
        net.store(datt.at[pl.ds(which * 256, 256)], gout_out.at[which])
    for chunk in (3, 2, 1, 0):
        for block in (chunk * 2, chunk * 2 + 1):
            place = pl.ds(block * OWN, OWN)
            net.got(key_grads + block, dkv_inbox.at[place])
            mine = part(block * 256 + net.half * OWN, OWN)
            total = wu[mine, pl.ds(512, 512)].astype(jnp.float32) + dkv_inbox[place, :].astype(jnp.float32)
            wd[place, pl.ds(512, 512)] = total.astype(LOW)
    dqkv = wd.at[:, pl.ds(256, 768)]
    net.store(dqkv, dqkv_out)
    lone[:, pl.ds(1024, 768)] = dot(jnp.ones((8, 1024), LOW), wd[:, pl.ds(256, 768)], NN)
    line_down.take()
    net.store(down_last, down_b)
    line_up.take()
    net.store(up_last, up_b)
    net.drain()


def ahead(lengths, inputs, cotangent, small, w_qkv, w_out, w_up, w_down, qv_bias, up_bias):
    return pl.pallas_call(
        ahead_kernel,
        out_shape=(
            low_shape(OWN, D),
            low_shape(1024, D),
            low_shape(3, D, 256),
            full_shape(8, D),
            low_shape(1024, 768),
            full_shape(OWN, D),
            low_shape(2, 256, 256),
            low_shape(OWN, D),
            low_shape(256, 1024),
            low_shape(256, 1024),
            low_shape(1024, 256),
            low_shape(1024, 256),
            full_shape(8, D),
            full_shape(8, 1792),
        ),
        in_specs=[SM, HBM, HBM, *[VM] * 6, HBM, HBM, HBM, HBM, VM, VM],
        out_specs=(HBM,) * 12 + (VM, VM),
        scratch_shapes=[
            pltpu.VMEM((OWN, D), LOW),
            pltpu.VMEM((1024, D), LOW),
            pltpu.VMEM((1024, D), LOW),
            pltpu.VMEM((1024, 256), LOW),
            pltpu.VMEM((2, 2048, 256), LOW),
            pltpu.VMEM((1024, 256), LOW),
            pltpu.VMEM((3, D, 256), LOW),
            pltpu.VMEM((256, D), LOW),
            pltpu.VMEM((8, D), jnp.float32),
            *reduce_scratch(),
            pltpu.VMEM((OWN, D), jnp.float32),
            pltpu.VMEM((1024, D), LOW),
            pltpu.VMEM((1024, 1024), LOW),
            pltpu.VMEM((1024, 1024), LOW),
            pltpu.VMEM((D, 1024), LOW),
            pltpu.VMEM((1024, D), LOW),
            pltpu.VMEM((8, 256), jnp.float32),
            pltpu.VMEM((1024, 2), jnp.float32),
            pltpu.VMEM((1024, 256), LOW),
            pltpu.VMEM((1024, 256), jnp.float32),
            pltpu.VMEM((1024, 512), LOW),
            pltpu.VMEM((4, 1024, 256), LOW),
            pltpu.VMEM((3, 1024, 256), LOW),
            pltpu.VMEM((1024, 256), LOW),
            pltpu.VMEM((4, 256, 1024), LOW),
            pltpu.VMEM((4, 256, 1024), LOW),
            pltpu.VMEM((3, 256, 1024), LOW),
            pltpu.VMEM((256, 1024), LOW),
            pltpu.VMEM((6, 256, 256), LOW),
            *sems(232, 32),
        ],
        compiler_params=pltpu.CompilerParams(
            collective_id=1, has_side_effects=True, vmem_limit_bytes=64 * 2**20 - 2**16
        ),
        cost_estimate=pl.CostEstimate(flops=40 * 10**9, bytes_accessed=30 * 10**6, transcendentals=2 * 10**6),
    )(lengths, inputs, cotangent, *small, w_qkv, w_out, w_up, w_down, qv_bias, up_bias)


def in_rows(ref, body):
    rows, width = ref.shape[-2:]
    step = min(rows, 2 ** ((32768 // width).bit_length() - 1))
    tiles(rows // step, lambda t: body(part(t * step, step)))


class SideReduce:
    def __init__(self, net, block, inbox, first):
        self.net, self.block, self.inbox, self.slot = net, block, inbox, net.slots(8)
        self.windows = (pl.ds(0, first), pl.ds(first, inbox.shape[1] - first))

    def other(self, dy):
        return (1 - self.net.half) * 4 + (self.net.y + dy) % 4

    def mine(self, dy):
        return self.net.half * 4 + (self.net.y + dy) % 4

    def give(self, dy):
        for side, device in enumerate((self.net.partner(), self.net.cousin())):
            rows = self.windows[side]
            self.net.push(
                self.slot + dy * 2 + side, self.block(dy).at[rows], self.inbox.at[dy, rows], device
            )

    def take(self, dy):
        for side in range(2):
            self.net.got(self.slot + dy * 2 + side, self.inbox.at[dy, self.windows[side]])


class LineReduce:
    def __init__(self, net, blocks, inbox, last):
        self.net, self.blocks, self.inbox, self.last = net, blocks, inbox, last
        self.slot = net.slots(4)

    def give(self, dy):
        self.net.push(self.slot + dy - 1, self.blocks.at[dy], self.inbox.at[dy - 1], self.net.at(dy=dy))

    def settle(self):
        for dy in (1, 2, 3):
            self.net.got(self.slot + dy - 1, self.inbox.at[dy - 1])

        def add(rows):
            total = self.blocks[0, rows, :].astype(jnp.float32)
            for i in range(3):
                total += self.inbox[i, rows, :].astype(jnp.float32)
            self.blocks[0, rows, :] = total.astype(LOW)

        in_rows(self.last, add)

    def close(self):
        self.settle()
        self.net.push(self.slot + 3, self.blocks.at[0], self.last, self.net.at(dx=2))

    def take(self):
        self.net.got(self.slot + 3, self.last)

    def finish(self, emit):
        self.take()
        in_rows(
            self.last,
            lambda rows: emit(rows, self.blocks[0, rows, :].astype(jnp.float32) + self.last[rows, :].astype(jnp.float32)),
        )


class LineFirst:
    def __init__(self, net, block, inbox, total, side, last, first):
        self.net, self.block, self.inbox, self.total, self.side, self.last = net, block, inbox, total, side, last
        self.slot = net.slots(9)
        self.windows = (pl.ds(0, first), pl.ds(first, inbox.shape[1] - first))

    def owner(self, which, dy):
        half = 1 - self.net.half if which else self.net.half
        return half * 4 + (self.net.y + dy) % 4

    def give(self, which, dy):
        place = which * 3 + dy - 1
        self.net.push(self.slot + place, self.block(place), self.inbox.at[place], self.net.at(dy=dy))

    def take(self, which):
        for dy in (1, 2, 3):
            self.net.got(self.slot + which * 3 + dy - 1, self.inbox.at[which * 3 + dy - 1])

    def arrived(self, which, rows):
        return sum(self.inbox[which * 3 + i, rows, :].astype(jnp.float32) for i in range(3))

    def sideways(self):
        for i, device in enumerate((self.net.partner(), self.net.cousin())):
            rows = self.windows[i]
            self.net.push(self.slot + 6 + i, self.total.at[1, rows], self.side.at[rows], device)

    def close(self):
        for i in range(2):
            self.net.got(self.slot + 6 + i, self.side.at[self.windows[i]])

        def add(rows):
            total = self.total[0, rows, :].astype(jnp.float32) + self.side[rows, :].astype(jnp.float32)
            self.total[0, rows, :] = total.astype(LOW)

        in_rows(self.side, add)
        self.net.push(self.slot + 8, self.total.at[0], self.last, self.net.at(dx=2))

    def finish(self, emit):
        self.net.got(self.slot + 8, self.last)
        in_rows(
            self.last,
            lambda rows: emit(
                rows, self.total[0, rows, :].astype(jnp.float32) + self.last[rows, :].astype(jnp.float32)
            ),
        )


def emit_to(ref):
    def emit(rows, values):
        ref[rows, :] = values

    return emit


def norm_back(grad, centred, inverse, gain):
    scaled = grad * gain
    return inverse * (
        scaled - jnp.mean(scaled, -1, keepdims=True) - centred * jnp.mean(scaled * centred, -1, keepdims=True)
    )


def norm_parts(values):
    middle = jnp.mean(values, -1, keepdims=True)
    spread = jnp.mean(values * values, -1, keepdims=True) - middle * middle
    inverse = lax.rsqrt(spread + EPSILON)
    return (values - middle) * inverse, inverse


def column_sums(values):
    return jnp.sum(values, 0, keepdims=True)


def attend_back_chunk(chunk, q, kv, grad, att, lse, dq, dkv, half, length):
    slots = pl.ds(chunk * 512, 512)
    for head in range(2):
        at = pl.ds(head * HEAD, HEAD)
        key, value = kv(0, slots, head), kv(1, slots, head)
        dkey, dvalue = jnp.zeros((512, HEAD), jnp.float32), jnp.zeros((512, HEAD), jnp.float32)
        for group in range(chunk, 4):
            rows = pl.ds(group * 256, 256)
            query, upstream = q(rows, head), grad[rows, at]
            delta = jnp.sum(upstream.astype(jnp.float32) * att[rows, at].astype(jnp.float32), -1, keepdims=True)
            scores = dot(query, key, NT) * SCALE
            slot = chunk * 512 + lax.broadcasted_iota(jnp.int32, (1, 512), 1)
            allowed = slot < length
            if group == chunk:
                allowed = allowed & (slot <= place_rows(group, half))
            probs = jnp.exp(jnp.where(allowed, scores - lse[rows, pl.ds(head, 1)], -HUGE))
            dscores = (probs * (dot(upstream, value, NT) - delta)).astype(LOW)
            share = dot(dscores, key, NN)
            if group == chunk:
                dq[rows, at] = share
            else:
                dq[rows, at] += share
            dkey += dot(dscores, query, TN)
            dvalue += dot(probs.astype(LOW), upstream, TN)
        dkv(0, slots, head, (dkey * SCALE).astype(LOW))
        dkv(1, slots, head, dvalue.astype(LOW))


class Everyone:
    def __init__(self, net, axis, inbox):
        self.net, self.axis, self.inbox, self.slot = net, axis, inbox, net.slots(7)
        self.index = net.row if axis == "row" else net.col

    def device(self, shift):
        net, index = self.net, (self.index + shift) % 8
        row, col = (index, net.col) if self.axis == "row" else (net.row, index)
        return {"dp": net.dp, "row": row, "col": col}

    def begin(self, src_of):
        for shift in range(1, 8):
            to = (self.index + shift) % 8
            self.net.push(self.slot + shift - 1, src_of(to), self.inbox.at[self.index], self.device(shift))
        self.copy = self.net.move(src_of(self.index), self.inbox.at[self.index])

    def total(self):
        self.copy.wait()
        for shift in range(1, 8):
            self.net.got(self.slot + shift - 1, self.inbox.at[(self.index + 8 - shift) % 8])
        total = self.inbox[0]
        for i in range(1, 8):
            total += self.inbox[i]
        return total


class Blocks:
    def __init__(self, net, src, inbox):
        self.net, self.src, self.inbox, self.slot = net, src, inbox, net.slots(15)

    def begin(self):
        net = self.net
        place = self.inbox.at[net.dp * 8 + net.row]
        for shift in range(16):
            row = (net.row + shift) % 8
            block = self.src.at[:, part(row * 256, 256)]
            if shift == 0:
                self.copy = net.move(block, place)
            else:
                dp = net.dp if shift < 8 else 1 - net.dp
                net.push(self.slot + shift - 1, block, place, {"dp": dp, "row": row, "col": net.col})

    def total(self):
        net = self.net
        self.copy.wait()
        for shift in range(1, 16):
            dp = net.dp if shift < 8 else 1 - net.dp
            net.got(self.slot + shift - 1, self.inbox.at[dp * 8 + (net.row + 16 - shift) % 8])
        total = self.inbox[0]
        for i in range(1, 16):
            total += self.inbox[i]
        return total


def fourth_kernel(
    dqkv_in, n1_in, wq_in, x_in, dmid_in, wide, gout_in, mixed_in, sums, single,
    grad_low, mixed_out, qkv_grad, out_out, wide_grad, lone_grad,
    dqkv, n1, wq, x, dmid, grad_own, mixed_own, mixed, out_grad, terms, near, left, right, ends,
    gout, gout_side, gout_last, gqk, gqk_side, gqk_line, gqk_last, gv, gv_line, gv_total, gv_side, gv_last,
    early, early_cols, late, late_cols, wide_part, wide_rows, packed, single_rows, single_part, single_last,
    send, recv, local,
):
    net = Net(send, recv, local)
    load = {}
    for name, a, b in (
        ("dqkv", dqkv_in, dqkv), ("wq", wq_in, wq), ("n1", n1_in, n1), ("gout", gout_in, gout),
        ("mixed", mixed_in, mixed_own), ("x", x_in, x), ("dmid", dmid_in, dmid),
    ):
        load[name] = net.move(a, b)
    cols = [{"dp": net.dp, "row": net.row, "col": (net.col + d) % 8} for d in range(1, 8)]
    across = [{"dp": 1 - net.dp, "row": (net.row + d) % 8, "col": net.col} for d in (0, 1, 2, 3, 5, 6, 7)]
    net.greet(across, cols)
    back = ColReduce(net, terms, near, left, right, ends)
    side_qk = SideReduce(net, lambda dy: gqk.at[dy], gqk_side, 128)
    line_qk = LineReduce(net, gqk_side, gqk_line, gqk_last)
    sum_v = LineFirst(net, lambda i: gv.at[i], gv_line, gv_total, gv_side, gv_last, 128)
    sum_out = LineFirst(net, None, gout_side, gout, gout_side, gout_last, 128)
    wide_early, wide_late = Everyone(net, "col", early_cols), Everyone(net, "col", late_cols)
    wide_b = Blocks(net, wide_part, wide_rows)
    single_a = Everyone(net, "row", single_rows)
    crossing = net.slots(1)

    def feature_block(ref):
        return lambda r: ref.at[:, part(r * 256, 256)]

    def token_block(ref):
        return lambda r: ref.at[(r // 2) % 2, r % 2, part(r // 4 * OWN, OWN)]

    mixed_swap = Swap(net, feature_block(mixed_own), token_block(mixed))
    grad_swap = Swap(net, feature_block(grad_own), token_block(grad_low))

    def spread(dz):
        rows = part((net.z + dz) % 4 * 256, 256)

        def tile(t):
            at = part(t * 512, 512)
            total = dot(dqkv[rows, pl.ds(0, 256)], wq[0, at, :], NT)
            for i in (1, 2):
                total += dot(dqkv[rows, pl.ds(i * 256, 256)], wq[i, at, :], NT)
            terms[rows, at] = total.astype(LOW)

        tiles(4, tile)

    def descend(dz):
        spread(dz)
        back.give(dz)

    def qk_tile(r):
        return dot(n1[:, part(r * 256, 256)], dqkv[:, pl.ds(0, 512)], TN)

    def v_tile(r):
        return dot(n1[:, part(r * 256, 256)], dqkv[:, pl.ds(512, 256)], TN)

    def qk_make(dy):
        gqk[dy] = qk_tile(side_qk.other(dy)).astype(LOW)

    def qk_give(dy):
        qk_make(dy)
        side_qk.give(dy)

    def qk_add(dy):
        side_qk.take(dy)
        gqk_side[dy] = (qk_tile(side_qk.mine(dy)) + gqk_side[dy].astype(jnp.float32)).astype(LOW)
        if dy:
            line_qk.give(dy)

    def v_give(which, dy):
        gv[which * 3 + dy - 1] = v_tile(sum_v.owner(which, dy)).astype(LOW)
        sum_v.give(which, dy)

    def v_add(which):
        sum_v.take(which)
        total = v_tile(sum_v.owner(which, 0)) + sum_v.arrived(which, pl.ds(0, 256))
        gv_total[which] = total.astype(LOW)

    for i in range(7):
        packed[i : i + 1, :] = single[0:1, i * 256 : (i + 1) * 256]
    packed[7:8, :] = jnp.zeros((1, 256), jnp.float32)
    for i in range(4):
        for j in range(4):
            early[i * 4 + j : i * 4 + j + 1, :] = sums[2 + i : 3 + i, j * 512 : (j + 1) * 512]
    for name in ("dqkv", "n1", "wq"):
        load[name].wait()
    for dy in (2, 1):
        qk_make(dy)
    spread(2)
    net.meet()
    for dy in (2, 1):
        side_qk.give(dy)
    back.give(2)
    single_a.begin(lambda r: packed)
    wide_early.begin(lambda r: early)
    load["gout"].wait()
    sum_out.sideways()
    for dy in (2, 1, 3):
        v_give(1, dy)
    descend(1)
    back.far()
    for dy in (3, 0):
        qk_give(dy)
    descend(3)
    back.own(1)
    back.own(3)
    for dy in (2, 1, 3):
        v_give(0, dy)
    descend(0)
    back.forward(1)
    back.forward(3)
    sum_out.close()
    load["mixed"].wait()
    mixed_swap.begin()
    for dy in (2, 1, 3, 0):
        qk_add(dy)
    load["x"].wait()
    load["dmid"].wait()
    back.finish()
    totals = [jnp.zeros((1, D), jnp.float32)] * 2
    for piece in range(4):
        rows = pl.ds(piece * 32, 32)
        grad = back.result(piece * 32, 32)
        centred, inverse = norm_parts(x[rows, :].astype(jnp.float32))
        value = dmid[rows, :] + norm_back(grad, centred, inverse, wide[0:1, :])
        grad_own[rows, :] = value.astype(LOW)
        totals = [a + column_sums(b) for a, b in zip(totals, (grad * centred, grad))]
    for i in range(2):
        for j in range(4):
            late[i * 4 + j : i * 4 + j + 1, :] = totals[i][:, j * 512 : (j + 1) * 512]
    wide_late.begin(lambda r: late)
    wide_part[6:8, :] = jnp.zeros((2, D), jnp.float32)
    total = wide_early.total()
    for i in range(4):
        for j in range(4):
            wide_part[2 + i : 3 + i, j * 512 : (j + 1) * 512] = total[i * 4 + j : i * 4 + j + 1, :]
    v_add(1)
    sum_v.sideways()
    total = wide_late.total()
    for i in range(2):
        for j in range(4):
            wide_part[i : i + 1, j * 512 : (j + 1) * 512] = total[i * 4 + j : i * 4 + j + 1, :]
    wide_b.begin()
    grad_swap.begin()
    single_part[...] = single_a.total()
    net.push(crossing, single_part, single_last, net.at(dx=2))
    v_add(0)
    sum_v.close()
    line_qk.close()
    mixed_swap.finish()
    net.store(mixed, mixed_out)
    grad_swap.finish()
    wide_grad[...] = wide_b.total()
    net.got(crossing, single_last)
    lone_grad[...] = single_part[...] + single_last[...]

    def emit_qk(rows, values):
        for i in range(2):
            qkv_grad[i, rows, :] = values[:, i * 256 : (i + 1) * 256]

    def emit_v(rows, values):
        qkv_grad[2, rows, :] = values

    sum_out.finish(emit_to(out_grad))
    line_qk.finish(emit_qk)
    sum_v.finish(emit_v)
    net.store(out_grad, out_out)
    net.drain()


def fourth(dqkv, n1, wq, x, dmid, wide, gout, mixed, sums, lone):
    return pl.pallas_call(
        fourth_kernel,
        out_shape=(
            low_shape(2, 2, 256, 256),
            low_shape(2, 2, 256, 256),
            full_shape(3, 256, 256),
            full_shape(256, 256),
            full_shape(8, 256),
            full_shape(8, 256),
        ),
        in_specs=[HBM, HBM, HBM, HBM, HBM, VM, HBM, HBM, VM, VM],
        out_specs=(VM, HBM, VM, HBM, VM, VM),
        scratch_shapes=[
            pltpu.VMEM((1024, 768), LOW),
            pltpu.VMEM((1024, D), LOW),
            pltpu.VMEM((3, D, 256), LOW),
            pltpu.VMEM((OWN, D), LOW),
            pltpu.VMEM((OWN, D), jnp.float32),
            pltpu.VMEM((OWN, D), LOW),
            pltpu.VMEM((OWN, D), LOW),
            pltpu.VMEM((2, 2, 256, 256), LOW),
            pltpu.VMEM((256, 256), jnp.float32),
            *reduce_scratch(),
            pltpu.VMEM((2, 256, 256), LOW),
            pltpu.VMEM((256, 256), LOW),
            pltpu.VMEM((256, 256), LOW),
            pltpu.VMEM((4, 256, 512), LOW),
            pltpu.VMEM((4, 256, 512), LOW),
            pltpu.VMEM((3, 256, 512), LOW),
            pltpu.VMEM((256, 512), LOW),
            pltpu.VMEM((6, 256, 256), LOW),
            pltpu.VMEM((6, 256, 256), LOW),
            pltpu.VMEM((2, 256, 256), LOW),
            pltpu.VMEM((256, 256), LOW),
            pltpu.VMEM((256, 256), LOW),
            pltpu.VMEM((16, 512), jnp.float32),
            pltpu.VMEM((8, 16, 512), jnp.float32),
            pltpu.VMEM((8, 512), jnp.float32),
            pltpu.VMEM((8, 8, 512), jnp.float32),
            pltpu.VMEM((8, D), jnp.float32),
            pltpu.VMEM((16, 8, 256), jnp.float32),
            pltpu.VMEM((8, 256), jnp.float32),
            pltpu.VMEM((8, 8, 256), jnp.float32),
            pltpu.VMEM((8, 256), jnp.float32),
            pltpu.VMEM((8, 256), jnp.float32),
            *sems(120, 24),
        ],
        compiler_params=pltpu.CompilerParams(
            collective_id=4, has_side_effects=True, vmem_limit_bytes=60 * 2**20
        ),
        cost_estimate=pl.CostEstimate(flops=40 * 10**9, bytes_accessed=30 * 10**6, transcendentals=2 * 10**6),
    )(dqkv, n1, wq, x, dmid, wide, gout, mixed, sums, lone)


def hand_over_kernel(
    mixed_in, grad_in, qkv_in, out_in, up_a, up_b, down_a, down_b, wide, lone,
    mixed, input_grad, gain1, bias1, qkv, qv, out, out_bias, gain2, bias2, up, up_bias, down, down_bias,
    a_down, b_down, a_up, b_up, low_grad, qkv_part, mixed_part, out_part, full_down, full_up, full_grad, done,
):
    def move(i, src, dst):
        copy = pltpu.make_async_copy(src, dst, done.at[i])
        copy.start()
        return copy

    sources = (
        (down_a, a_down), (down_b, b_down), (up_a, a_up), (up_b, b_up), (grad_in, low_grad), (qkv_in, qkv_part), (mixed_in, mixed_part),
        (out_in, out_part),
    )
    fetches = [move(i, a, b) for i, (a, b) in enumerate(sources)]
    for i, ref in enumerate((gain1, bias1, out_bias, gain2, bias2, down_bias)):
        ref[...] = wide[i : i + 1, :]
    for i in range(4):
        up_bias[:, i * 256 : (i + 1) * 256] = lone[i : i + 1, :]
    qv[0:1, :] = lone[4:5, :]
    qv[1:2, :] = lone[6:7, :]
    stores = []
    for i, (full, a, b, ref) in enumerate(((full_down, a_down, b_down, down), (full_up, a_up, b_up, up))):
        fetches[2 * i].wait()
        fetches[2 * i + 1].wait()

        def add(rows):
            full[rows, :] = a[rows, :].astype(jnp.float32) + b[rows, :].astype(jnp.float32)

        in_rows(full, add)
        stores.append(move(8 + i, full, ref))
    fetches[4].wait()
    for i in range(2):
        for j in range(2):
            full_grad[i, j] = low_grad[i, j].astype(jnp.float32)
    stores.append(move(10, full_grad, input_grad))
    for i, (src, ref) in enumerate(((qkv_part, qkv), (mixed_part, mixed), (out_part, out))):
        fetches[5 + i].wait()
        stores.append(move(11 + i, src, ref))
    for store in stores:
        store.wait()


def hand_over(mixed, grad, qkv, out, up_a, up_b, down_a, down_b, wide, lone):
    vector = full_shape(1, 256)
    return pl.pallas_call(
        hand_over_kernel,
        out_shape=(
            low_shape(2, 2, 256, 256),
            full_shape(2, 2, 256, 256),
            vector,
            vector,
            full_shape(3, 256, 256),
            full_shape(2, 256),
            full_shape(256, 256),
            vector,
            vector,
            vector,
            full_shape(256, 1024),
            full_shape(1, 1024),
            full_shape(1024, 256),
            vector,
        ),
        in_specs=[HBM] * 8 + [VM, VM],
        out_specs=(HBM, HBM, VM, VM, HBM, VM, HBM, VM, VM, VM, HBM, VM, HBM, VM),
        scratch_shapes=[
            pltpu.VMEM((1024, 256), LOW),
            pltpu.VMEM((1024, 256), LOW),
            pltpu.VMEM((256, 1024), LOW),
            pltpu.VMEM((256, 1024), LOW),
            pltpu.VMEM((2, 2, 256, 256), LOW),
            pltpu.VMEM((3, 256, 256), jnp.float32),
            pltpu.VMEM((2, 2, 256, 256), LOW),
            pltpu.VMEM((256, 256), jnp.float32),
            pltpu.VMEM((1024, 256), jnp.float32),
            pltpu.VMEM((256, 1024), jnp.float32),
            pltpu.VMEM((2, 2, 256, 256), jnp.float32),
            pltpu.SemaphoreType.DMA((14,)),
        ],
        compiler_params=pltpu.CompilerParams(vmem_limit_bytes=63 * 2**20),
    )(mixed, grad, qkv, out, up_a, up_b, down_a, down_b, wide, lone)


def shards(
    inputs,
    lengths,
    ln1_gain,
    ln1_bias,
    w_qkv,
    qv_bias,
    w_out,
    out_bias,
    ln2_gain,
    ln2_bias,
    w_up,
    up_bias,
    w_down,
    down_bias,
    cotangent,
):
    small = [a.reshape(1, 256) for a in (ln1_gain, ln1_bias, out_bias, ln2_gain, ln2_bias, down_bias)]
    x, all1, wq, wide, dqkv, dmid, gout, mixed, up_a, up_b, down_a, down_b, sums, lone = ahead(
        lengths, inputs, cotangent, small, w_qkv, w_out, w_up, w_down, qv_bias, up_bias.reshape(1, 1024)
    )
    grad, mixed, g_qkv, g_out, wide_grad, lone_grad = fourth(dqkv, all1, wq, x, dmid, wide, gout, mixed, sums, lone)
    outs = hand_over(mixed, grad, g_qkv, g_out, up_a, up_b, down_a, down_b, wide_grad, lone_grad)
    return tuple(a.reshape(-1) if a.shape[0] == 1 else a for a in outs)


def solution(mesh):
    tokens = P(None, "dp", "col", "row")
    in_specs = (
        tokens,
        P(None, "dp"),
        P("row"),
        P("row"),
        P(None, "row", "col"),
        P(None, "col"),
        P("col", "row"),
        P("row"),
        P("row"),
        P("row"),
        P("row", "col"),
        P("col"),
        P("col", "row"),
        P("row"),
        tokens,
    )
    out_specs = (
        tokens,
        tokens,
        P("row"),
        P("row"),
        P(None, "row", "col"),
        P(None, "col"),
        P("col", "row"),
        P("row"),
        P("row"),
        P("row"),
        P("row", "col"),
        P("col"),
        P("col", "row"),
        P("row"),
    )
    return jax.shard_map(shards, mesh=mesh, in_specs=in_specs, out_specs=out_specs, check_vma=False)
```

```python
import functools

import jax
import jax.numpy as jnp
from jax import lax
from jax.experimental import pallas as pl
from jax.experimental.pallas import tpu as pltpu
from jax.sharding import PartitionSpec as P

D = 2048
HEAD = 128
SCALE = HEAD**-0.5
EPSILON = 1e-05
HUGE = 1e30
LOW = jnp.bfloat16
OWN = 128
VMEM_LIMIT = 56 * 2**20


def dot(a, b, contract):
    return lax.dot_general(a, b, ((contract[0], contract[1]), ((), ())), preferred_element_type=jnp.float32)


NN = ((1,), (0,))
NT = ((1,), (1,))
TN = ((0,), (0,))


def place_rows(group, half):
    row = lax.broadcasted_iota(jnp.int32, (256, 1), 0)
    return (2 * group + row // OWN) * 256 + half * OWN + row % OWN


def allowed_keys(group, extent, half, length):
    slot = lax.broadcasted_iota(jnp.int32, (256, extent), 1)
    return (slot <= place_rows(group, half)) & (slot < length)


MESH = pl.DeviceIdType.MESH
HBM = pl.BlockSpec(memory_space=pl.ANY)
VM = pl.BlockSpec(memory_space=pltpu.VMEM)
SM = pl.BlockSpec(memory_space=pltpu.SMEM)


def part(start, size):
    return pl.ds(pl.multiple_of(start, size), size)


class Net:
    def __init__(self, send, recv, local):
        self.send, self.recv, self.local = send, recv, local
        self.used, self.local_used, self.live, self.own = 0, 0, [], []
        self.dp, self.row, self.col = (lax.axis_index(a) for a in ("dp", "row", "col"))
        self.half, self.y = self.row // 4, self.row % 4
        self.x = self.dp * 2 + self.half
        self.z, self.core = self.col // 2, self.col % 2

    def at(self, dx=0, dy=0, dz=0, other_core=False):
        x, y, z = (self.x + dx) % 4, (self.y + dy) % 4, (self.z + dz) % 4
        core = 1 - self.core if other_core else self.core
        return {"dp": x // 2, "row": (x % 2) * 4 + y, "col": z * 2 + core}

    def mate(self, shift):
        return {"dp": self.dp, "row": (self.row + shift) % 8, "col": self.col}

    def partner(self):
        return self.mate(4)

    def cousin(self):
        return {"dp": 1 - self.dp, "row": (self.row + 4) % 8, "col": self.col}

    def greet(self, more=(), cols=()):
        devices = [self.mate(d) for d in range(1, 8)]
        devices += [self.cousin()]
        devices += cols or [self.at(dz=1), self.at(dz=3), self.at(other_core=True)]
        devices += more
        self.expected = len(devices)
        for device in devices:
            pl.semaphore_signal(pltpu.get_barrier_semaphore(), inc=1, device_id=device, device_id_type=MESH)

    def meet(self):
        pl.semaphore_wait(pltpu.get_barrier_semaphore(), self.expected)

    def slots(self, count):
        self.used += count
        return self.used - count

    def _copy(self, slot, src, dst, device):
        return pltpu.make_async_remote_copy(
            src_ref=src,
            dst_ref=dst,
            send_sem=self.send.at[slot],
            recv_sem=self.recv.at[slot],
            device_id=device,
            device_id_type=MESH,
        )

    def push(self, slot, src, dst, device):
        copy = self._copy(slot, src, dst, device)
        copy.start()
        self.live.append(copy)

    def got(self, slot, ref):
        self._copy(slot, ref, ref, self.at(other_core=True)).wait_recv()

    def flush(self, copies):
        for copy in copies:
            copy.wait_send()
        self.live = [copy for copy in self.live if not any(copy is other for other in copies)]

    def move(self, src, dst):
        copy = pltpu.make_async_copy(src, dst, self.local.at[self.local_used])
        self.local_used += 1
        copy.start()
        return copy

    def store(self, src, dst):
        self.own.append(self.move(src, dst))

    def drain(self):
        for copy in self.live:
            copy.wait_send()
        for copy in self.own:
            copy.wait()


class ColGather:
    def __init__(self, net, buf):
        self.net, self.buf, self.slot = net, buf, net.slots(14)
        self.sent = []

    def rows(self, dz, other_core, piece):
        net = self.net
        core = 1 - net.core if other_core else net.core
        return self.buf.at[part(((net.z + dz) % 4 * 2 + core) * OWN + 64 * piece, 64)]

    def move(self, slot, where, piece, **to):
        ref = self.rows(where, False, piece)
        self.net.push(self.slot + slot, ref, ref, self.net.at(**to))
        self.sent.append(self.net.live[-1])

    def flush(self):
        self.net.flush(self.sent)

    def got(self, slot, dz, piece, other_core=False):
        self.net.got(self.slot + slot, self.rows(dz, other_core, piece))

    def begin(self):
        self.move(0, 0, 0, dz=1)
        self.move(3, 0, 1, dz=3)
        self.move(1, 0, 1, dz=1)
        self.move(2, 0, 0, dz=3)
        self.move(6, 0, 0, other_core=True)
        self.move(7, 0, 1, other_core=True)

    def hop(self):
        self.pass_on()
        self.take_rest()

    def pass_on(self):
        self.got(0, 3, 0)
        self.move(4, 3, 0, dz=1)
        self.got(3, 1, 1)
        self.move(5, 1, 1, dz=3)
        self.move(8, 3, 0, other_core=True)
        self.move(11, 1, 1, other_core=True)

    def take_rest(self):
        self.got(1, 3, 1)
        self.move(9, 3, 1, other_core=True)
        self.got(2, 1, 0)
        self.move(10, 1, 0, other_core=True)

    def far(self):
        self.got(4, 2, 0)
        self.move(12, 2, 0, other_core=True)
        self.got(5, 2, 1)
        self.move(13, 2, 1, other_core=True)

    def pair(self, dz):
        slot = {0: 6, 3: 8, 1: 10, 2: 12}[dz]
        self.got(slot, dz, 0, True)
        self.got(slot + 1, dz, 1, True)


class RowGather:
    def __init__(self, net, src, buf, whole, parts):
        self.net, self.src, self.buf, self.whole, self.parts = net, src, buf, whole, parts
        self.slot, self.sent = net.slots(11), []

    def place(self, dy, other=False):
        net = self.net
        half = 1 - net.half if other else net.half
        return self.whole(self.buf, half * 4 + (net.y + dy) % 4)

    def sideways(self, dy, src, sides=(0, 1)):
        net, there = self.net, self.place(dy)
        devices = (net.partner(), net.cousin())
        for side in sides:
            net.push(
                self.slot + 3 + dy * 2 + side, self.parts(src, side), self.parts(there, side), devices[side]
            )
            self.sent.append(net.live[-1])

    def flush(self):
        self.net.flush(self.sent)

    def begin(self):
        net, mine = self.net, self.place(0)
        for dy in (1, 3, 2):
            net.push(self.slot + dy - 1, self.src, mine, net.at(dy=dy))
            self.sent.append(net.live[-1])
        self.copy = net.move(self.src, mine)

    def begin_sideways(self, sides=(0, 1)):
        self.sideways(0, self.src, sides)

    def step(self, dy, sides=(0, 1)):
        ref = self.place(4 - dy)
        self.net.got(self.slot + dy - 1, ref)
        self.sideways(4 - dy, ref, sides)

    def follow(self, dy, sides):
        self.sideways(4 - dy, self.place(4 - dy), sides)

    def steps(self):
        for dy in (1, 3, 2):
            self.step(dy)

    def finish(self):
        self.copy.wait()
        for dy in range(4):
            for side in range(2):
                self.net.got(self.slot + 3 + dy * 2 + side, self.parts(self.place(dy, True), side))


def cut(rows):
    def parts(ref, side):
        total = ref.shape[-2]
        window = pl.ds(0, rows) if side == 0 else pl.ds(rows, total - rows)
        return ref.at[:, window] if len(ref.shape) == 3 else ref.at[window]

    return parts


class Swap:
    def __init__(self, net, src_of, dst_of):
        self.net, self.src_of, self.dst_of, self.slot = net, src_of, dst_of, net.slots(7)

    def begin(self):
        net = self.net
        for shift in range(1, 8):
            net.push(self.slot + shift - 1, self.src_of((net.row + shift) % 8), self.dst_of(net.row), net.mate(shift))
        self.copy = net.move(self.src_of(net.row), self.dst_of(net.row))

    def finish(self):
        net = self.net
        self.copy.wait()
        for shift in range(1, 8):
            net.got(self.slot + shift - 1, self.dst_of((net.row + 8 - shift) % 8))


def norm_rows(values, gain, bias):
    middle = jnp.mean(values, -1, keepdims=True)
    spread = jnp.mean(values * values, -1, keepdims=True) - middle * middle
    inverse = lax.rsqrt(spread + EPSILON)
    centred = (values - middle) * inverse
    return centred * gain + bias


def attend_group(q, kv, head, group, half, length):
    cols, rows, extent = pl.ds(head * HEAD, HEAD), pl.ds(group * 256, 256), 512 * (group + 1)
    scores = dot(q[rows, cols], kv[0, :extent, cols], NT) * SCALE
    scores = jnp.where(allowed_keys(group, extent, half, length), scores, -HUGE)
    highest = jnp.max(scores, -1, keepdims=True)
    weights = jnp.exp(scores - highest)
    total = jnp.sum(weights, -1, keepdims=True)
    out = dot(weights.astype(LOW), kv[1, :extent, cols], NN) / total
    return out, highest + jnp.log(total)


def low_shape(*shape):
    return jax.ShapeDtypeStruct(shape, LOW)


def full_shape(*shape):
    return jax.ShapeDtypeStruct(shape, jnp.float32)


def sems(remote, local):
    return [
        pltpu.SemaphoreType.DMA((remote,)),
        pltpu.SemaphoreType.DMA((remote,)),
        pltpu.SemaphoreType.DMA((local,)),
    ]


class ColReduce:
    def __init__(self, net, terms, near, left, right, ends):
        self.net, self.terms, self.near, self.left, self.right, self.ends = net, terms, near, left, right, ends
        self.slot = net.slots(10)
        self.sent = []

    def push(self, *copy):
        self.net.push(*copy)
        self.sent.append(self.net.live[-1])

    def flush(self):
        self.net.flush(self.sent)

    def block(self, dz, other_core=False):
        net = self.net
        core = 1 - net.core if other_core else net.core
        return part(((net.z + dz) % 4 * 2 + core) * OWN, OWN)

    def rows(self, dz, piece):
        net = self.net
        return part(((net.z + dz) % 4 * 2 + net.core) * OWN + 64 * piece, 64)

    def give(self, dz):
        self.push(
            self.slot + dz, self.terms.at[self.block(dz, True)], self.near.at[pl.ds(dz * OWN, OWN)], self.net.at(other_core=True)
        )

    def fold(self, dz):
        near = self.near.at[pl.ds(dz * OWN, OWN)]
        self.net.got(self.slot + dz, near)
        block = self.block(dz)
        self.terms[block, :] = (self.terms[block, :].astype(jnp.float32) + near[...].astype(jnp.float32)).astype(LOW)

    def send(self, slot, dz, piece, dst, side):
        self.push(self.slot + slot, self.terms.at[self.rows(dz, piece)], dst, self.net.at(dz=side))

    def far(self):
        self.fold(2)
        self.send(4, 2, 0, self.left, 1)
        self.send(5, 2, 1, self.right, 3)

    def own(self, dz):
        self.fold(dz)
        side = 0 if dz == 1 else 1
        self.send(6 + side * 2 + 1 - side, dz, 1 - side, self.ends.at[side, pl.ds((1 - side) * 64, 64)], dz)

    def forward(self, dz):
        side = 0 if dz == 1 else 1
        inbox = self.left if dz == 1 else self.right
        self.net.got(self.slot + 4 + side, inbox)
        rows = self.rows(dz, side)
        self.terms[rows, :] = (self.terms[rows, :].astype(jnp.float32) + inbox[...].astype(jnp.float32)).astype(LOW)
        self.send(6 + side * 2 + side, dz, side, self.ends.at[side, pl.ds(side * 64, 64)], dz)

    def finish(self):
        self.net.got(self.slot, self.near.at[pl.ds(0, OWN)])
        for side in range(2):
            for piece in range(2):
                self.net.got(self.slot + 6 + side * 2 + piece, self.ends.at[side, pl.ds(piece * 64, 64)])

    def result(self, start, size):
        block = part(self.net.col * OWN + start, size)
        total = self.terms[block, :].astype(jnp.float32) + self.near[pl.ds(start, size), :].astype(jnp.float32)
        for side in range(2):
            total += self.ends[side, pl.ds(start, size), :].astype(jnp.float32)
        return total


def reduce_scratch():
    return [
        pltpu.VMEM((1024, D), LOW),
        pltpu.VMEM((4 * OWN, D), LOW),
        pltpu.VMEM((64, D), LOW),
        pltpu.VMEM((64, D), LOW),
        pltpu.VMEM((2, OWN, D), LOW),
    ]


def tiles(count, body):
    lax.fori_loop(0, count, lambda t, c: (body(t), c)[1], 0)


def ahead_kernel(
    lengths, inputs, cotangent, gain1, bias1, bias_out, gain2, bias2, bias_down, w_qkv, w_out, w_up, w_down, qv_bias, up_bias,
    x_out, n1_out, wq_out, small_out, dqkv_out, dmid_out, gout_out, mixed_out, up_a, up_b, down_a, down_b, sums, lone,
    x, dy, n1, q, kv, att, wq, wo, wide,
    terms, near, left, right, ends, mid, n2, act, slope, wu, wd, small, lse,
    datt, dq, dkv_inbox, down_side, down_line, down_last, up, up_side, up_line, up_last, gout_line,
    send, recv, local,
):
    net = Net(send, recv, local)
    for i, ref in enumerate((gain1, bias1, bias_out, gain2, bias2, bias_down)):
        small[i : i + 1, :] = ref[...]
    small[6:8, :] = jnp.zeros((2, 256), jnp.float32)
    length = lengths[(net.row // 2) % 2, net.row % 2]
    net.greet([net.at(dx=2)])
    net.meet()
    mine = part(net.col * OWN, OWN)

    def token_block(ref):
        return lambda r: ref.at[(r // 2) % 2, r % 2, part(r // 4 * OWN, OWN)]

    def feature_block(ref):
        return lambda r: ref.at[:, part(r * 256, 256)]

    def by_columns(ref, r):
        return ref.at[:, part(r * 256, 256)]

    def by_rows(ref, r):
        return ref.at[part(r * 256, 256)]

    params = Swap(net, lambda r: small, feature_block(wide))
    tokens = Swap(net, token_block(inputs), feature_block(x))
    upstream = Swap(net, token_block(cotangent), lambda r: dy.at[mine, part(r * 256, 256)])
    gather_kv = RowGather(net, w_qkv.at[pl.ds(1, 2)], wq.at[pl.ds(1, 2)], by_columns, cut(128))
    gather_q = RowGather(net, w_qkv.at[pl.ds(0, 1)], wq.at[pl.ds(0, 1)], by_columns, cut(32))
    gather_wo = RowGather(net, w_out, wo, by_columns, cut(16))
    gather_wu = RowGather(net, w_up, wu, by_rows, cut(128))
    gather_wd = RowGather(net, w_down, wd, by_columns, cut(512))
    all_n1, all_dy, all_n2 = ColGather(net, n1), ColGather(net, dy), ColGather(net, n2)
    branch = ColReduce(net, terms, near, left, right, ends)
    keys = net.slots(16)

    def pair(dz):
        return part((net.z + dz) % 4 * 256, 256)

    def project_keys(dz):
        all_n1.pair(dz)
        block = (net.z + dz) % 4
        values = n1[pair(dz), :]
        k = dot(values, wq[1], NN).astype(LOW)
        v = (dot(values, wq[2], NN) + qv_bias[1:2, :]).astype(LOW)
        for i in range(2):
            there = part((block * 2 + i) * 256 + net.half * OWN, OWN)
            kv[0, there, :] = k[i * OWN : (i + 1) * OWN]
            kv[1, there, :] = v[i * OWN : (i + 1) * OWN]

    def key_block(dz, i, half, head):
        there = part(((net.z + dz) % 4 * 2 + i) * 256 + half * OWN, OWN)
        return kv.at[:, there, pl.ds(head * HEAD, HEAD)]

    def swap_keys(dz, head):
        for i in range(2):
            ref = key_block(dz, i, net.half, head)
            net.push(keys + head * 8 + dz * 2 + i, ref, ref, net.partner())

    def take_keys(dz, head):
        for i in range(2):
            net.got(keys + head * 8 + dz * 2 + i, key_block(dz, i, 1 - net.half, head))

    def second_head(group, half, act_on):
        for i in range(2):
            place = part((group * 2 + i) * 256 + half * OWN, OWN)
            ref = kv.at[:, place, pl.ds(HEAD, HEAD)]
            act_on(keys + 8 + group * 2 + i, ref)

    params.begin()
    tokens.begin()
    gather_kv.begin()
    gather_kv.begin_sideways()
    params.finish()
    tokens.finish()
    for piece in range(4):
        rows = pl.ds(piece * 32, 32)
        low = norm_rows(x[rows, :].astype(jnp.float32), wide[0:1, :], wide[1:2, :]).astype(LOW)
        n1[part(net.col * OWN + piece * 32, 32), :] = low
    all_n1.begin()
    keep_x = net.move(x, x_out)
    net.store(wide, small_out)
    all_n1.pass_on()
    gather_kv.steps()
    upstream.begin()
    gather_q.begin()
    gather_q.begin_sideways()
    all_n1.take_rest()
    gather_kv.finish()
    for dz in (0, 3, 1):
        project_keys(dz)
        swap_keys(dz, 0)
    all_n1.far()
    project_keys(2)
    swap_keys(2, 0)
    gather_wo.begin()
    gather_wo.begin_sideways()
    gather_wu.begin()
    gather_wd.begin()
    upstream.finish()
    all_dy.begin()
    gather_q.steps()
    gather_wu.begin_sideways((1,))
    all_dy.pass_on()
    take_keys(0, 0)
    take_keys(3, 0)
    for group in range(4):
        second_head(group, net.half, lambda slot, ref: net.push(slot, ref, ref, net.partner()))
    gather_q.finish()

    def project_queries(t):
        rows = part(t * 256, 256)
        q[rows, :] = (dot(n1[rows, :], wq[0], NN) + qv_bias[0:1, :]).astype(LOW)

    tiles(4, project_queries)
    def attend(head):
        if head == 0:
            take_keys(1, 0)
            take_keys(2, 0)
        for group in range(4):
            if head:
                second_head(group, 1 - net.half, net.got)
            out, logsum = attend_group(q, kv, head, group, net.half, length)
            rows = pl.ds(group * 256, 256)
            att[rows, pl.ds(head * HEAD, HEAD)] = out.astype(LOW)
            lse[rows, pl.ds(head, 1)] = logsum

    gather_wo.steps()
    attend(0)
    all_dy.take_rest()
    all_dy.far()
    attend(1)
    gather_wu.begin_sideways((0,))
    gather_wo.finish()

    def project(dz):
        rows = pair(dz)

        def tile(t):
            cols = part(t * 512, 512)
            terms[rows, cols] = dot(att[rows, :], wo[:, cols], NN).astype(LOW)

        tiles(4, tile)
        branch.give(dz)

    project(2)
    project(1)
    branch.far()
    project(3)
    branch.own(1)
    branch.own(3)
    project(0)
    gather_wu.step(1)
    gather_wu.step(3)
    branch.forward(1)
    branch.forward(3)
    gather_wu.step(2)
    gather_wd.begin_sideways()
    keep_n1 = net.move(n1, n1_out)
    keep_wq = net.move(wq, wq_out)
    branch.finish()
    for piece in range(4):
        rows = pl.ds(piece * 32, 32)
        total = x[rows, :].astype(jnp.float32) + branch.result(piece * 32, 32) + wide[2:3, :]
        mid[rows, :] = total
        low = norm_rows(total, wide[3:4, :], wide[4:5, :]).astype(LOW)
        n2[part(net.col * OWN + piece * 32, 32), :] = low
    for copy in (keep_x, keep_n1, keep_wq):
        copy.wait()
    gather_kv.flush()
    gather_q.flush()
    all_n1.flush()
    all_n2.begin()
    gather_wd.step(1)
    gather_wd.step(3)
    gather_wu.finish()

    def ascend(dz):
        all_n2.pair(dz)
        rows = pair(dz)

        def tile(t):
            cols = part(t * 256, 256)
            hidden = dot(n2[rows, :], wu[:, cols], NN) + up_bias[:, cols]
            share = 0.5 + 0.5 * lax.erf(hidden * 0.5**0.5)
            act[rows, cols] = (hidden * share).astype(LOW)
            density = jnp.exp(-0.5 * hidden * hidden) * (0.5 / jnp.pi) ** 0.5
            slope[rows, cols] = (share + hidden * density).astype(LOW)

        tiles(4, tile)

    ascend(0)
    all_n2.pass_on()
    gather_wd.step(2)
    all_n2.take_rest()
    ascend(3)
    for dz in range(4):
        all_dy.pair(dz)
    all_n2.far()
    ascend(1)
    ascend(2)
    gather_wd.finish()
    back = ColReduce(net, terms, near, left, right, ends)
    all_db, db = ColGather(net, n1), n1
    ffn = ColReduce(net, terms, near, left, right, ends)
    side_down = SideReduce(net, lambda dy: wq.at[dy // 2, pl.ds(dy % 2 * 1024, 1024)], down_side, 384)
    line_down = LineReduce(net, down_side, down_line, down_last)
    side_up = SideReduce(net, lambda dy: up.at[dy], up_side, 96)
    line_up = LineReduce(net, up_side, up_line, up_last)
    sum_out = LineFirst(net, lambda i: wq.at[2, pl.ds(i * 256, 256)], gout_line, None, None, None, 128)
    key_grads = net.slots(8)

    def descend(dz):
        rows = pair(dz)

        def into_hidden(t):
            cols = part(t * 512, 512)
            grad = dot(dy[rows, :], wd[cols, :], NT)
            slope[rows, cols] = (grad * slope[rows, cols].astype(jnp.float32)).astype(LOW)

        def into_width(t):
            cols = part(t * 512, 512)
            terms[rows, cols] = dot(slope[rows, :], wu[cols, :], NT).astype(LOW)

        tiles(2, into_hidden)
        tiles(4, into_width)
        back.give(dz)

    def down_tile(r, t):
        return dot(act[:, part(t * 512, 512)], dy[:, part(r * 256, 256)], TN)

    def up_tile(r, t):
        return dot(n2[:, part(r * 256, 256)], slope[:, part(t * 512, 512)], TN)

    def down_give(step):
        r = side_down.other(step)

        def tile(t):
            wq[step // 2, part(step % 2 * 1024 + t * 512, 512), :] = down_tile(r, t).astype(LOW)

        tiles(2, tile)
        side_down.give(step)

    def down_add(step):
        side_down.take(step)
        r = side_down.mine(step)

        def tile(t):
            units = part(t * 512, 512)
            down_side[step, units, :] = (down_tile(r, t) + down_side[step, units, :].astype(jnp.float32)).astype(LOW)

        tiles(2, tile)

    def up_give(step):
        r = side_up.other(step)

        def tile(t):
            up[step, :, part(t * 512, 512)] = up_tile(r, t).astype(LOW)

        tiles(2, tile)
        side_up.give(step)

    def up_add(step):
        side_up.take(step)
        r = side_up.mine(step)

        def tile(t):
            units = part(t * 512, 512)
            up_side[step, :, units] = (up_tile(r, t) + up_side[step, :, units].astype(jnp.float32)).astype(LOW)

        tiles(2, tile)

    def low_rank(dz):
        all_db.pair(dz)
        rows = pair(dz)
        datt[rows, :] = dot(db[rows, :], wo[...], NT).astype(LOW)

    branch.flush()
    down_give(2)
    down_give(1)
    descend(2)
    descend(1)
    back.far()
    down_give(3)
    descend(3)
    back.own(1)
    back.own(3)
    down_add(2)
    line_down.give(2)
    descend(0)
    down_give(0)
    back.forward(1)
    back.forward(3)
    for step in (1, 3):
        down_add(step)
        line_down.give(step)
    for step in (2, 1, 3, 0):
        up_give(step)
    back.finish()
    totals = [jnp.zeros((1, D), jnp.float32)] * 4
    for piece in range(4):
        rows = pl.ds(piece * 32, 32)
        own = part(net.col * OWN + piece * 32, 32)
        grad = back.result(piece * 32, 32)
        centred, inverse = norm_parts(mid[rows, :])
        upstream = dy[own, :].astype(jnp.float32)
        value = upstream + norm_back(grad, centred, inverse, wide[3:4, :])
        x[rows, :] = (mid[rows, :] + wide[5:6, :]).astype(LOW)
        mid[rows, :] = value
        low = value.astype(LOW)
        db[own, :] = low
        terms_of = (low.astype(jnp.float32), grad * centred, grad, upstream)
        totals = [a + column_sums(b) for a, b in zip(totals, terms_of)]
    all_db.begin()
    zero = jnp.zeros((2, D), jnp.float32)
    sums[...] = jnp.concatenate([zero, *totals, zero], 0)
    net.store(mid, dmid_out)
    back.flush()

    def mix(t):
        cols = part(t * 512, 512)
        for i in range(2):
            rows = pl.ds(i * 512, 512)
            terms[rows, cols] = dot(act[rows, :], wd[:, cols], NN).astype(LOW)

    tiles(4, mix)
    all_db.pass_on()
    down_add(0)
    line_down.close()
    net.store(down_side.at[0], down_a)
    all_db.take_rest()
    low_rank(0)
    for dz in (2, 1, 3, 0):
        ffn.give(dz)
    ffn.far()
    up_add(2)
    line_up.give(2)
    all_db.far()
    for dz in (3, 1, 2):
        low_rank(dz)
    ffn.own(1)
    ffn.own(3)
    def of_keys(which, slots, head):
        return kv[which, slots, pl.ds(head * HEAD, HEAD)]

    def of_queries(rows, head):
        return q[rows, pl.ds(head * HEAD, HEAD)]

    gather_wu.flush()
    gather_wd.flush()
    def keep(which, slots, head, values):
        wu[slots, pl.ds(512 + which * 256 + head * HEAD, HEAD)] = values

    def attend_back(chunk):
        attend_back_chunk(chunk, of_queries, of_keys, datt, att, lse, dq, keep, net.half, length)
        for block in (chunk * 2, chunk * 2 + 1):
            theirs = part(block * 256 + (1 - net.half) * OWN, OWN)
            net.push(
                key_grads + block,
                wu.at[theirs, pl.ds(512, 512)],
                dkv_inbox.at[pl.ds(block * OWN, OWN)],
                net.partner(),
            )

    attend_back(3)
    up_add(1)
    line_up.give(1)
    attend_back(2)
    ffn.forward(1)
    ffn.forward(3)
    up_add(3)
    line_up.give(3)
    attend_back(1)
    attend_back(0)

    def out_block(which, dy):
        r = sum_out.owner(which, dy)
        place = which * 3 + dy - 1 if dy else 6 + which
        wq[2, pl.ds(place * 256, 256), :] = dot(att[...], n1[:, part(r * 256, 256)], TN).astype(LOW)

    for which in (1, 0):
        for dy in (2, 1, 3):
            out_block(which, dy)
            sum_out.give(which, dy)
        out_block(which, 0)
    up_add(0)
    lone[:, pl.ds(0, 1024)] = dot(jnp.ones((8, 1024), LOW), slope[...], NN)
    for piece in range(4):
        rows = pl.ds(piece * 256, 256)
        wd[rows, pl.ds(256, 256)] = (dq[rows, :] * SCALE).astype(LOW)
    ffn.finish()
    for piece in range(4):
        rows = pl.ds(piece * 32, 32)
        x[rows, :] = (x[rows, :].astype(jnp.float32) + ffn.result(piece * 32, 32)).astype(LOW)
    net.store(x, mixed_out)
    line_up.close()
    net.store(up_side.at[0], up_a)
    for which in (1, 0):
        sum_out.take(which)
        own = wq[2, pl.ds((6 + which) * 256, 256), :].astype(jnp.float32)
        datt[pl.ds(which * 256, 256), :] = (own + sum_out.arrived(which, pl.ds(0, 256))).astype(LOW)
        net.store(datt.at[pl.ds(which * 256, 256)], gout_out.at[which])
    for chunk in (3, 2, 1, 0):
        for block in (chunk * 2, chunk * 2 + 1):
            place = pl.ds(block * OWN, OWN)
            net.got(key_grads + block, dkv_inbox.at[place])
            mine = part(block * 256 + net.half * OWN, OWN)
            total = wu[mine, pl.ds(512, 512)].astype(jnp.float32) + dkv_inbox[place, :].astype(jnp.float32)
            wd[place, pl.ds(512, 512)] = total.astype(LOW)
    dqkv = wd.at[:, pl.ds(256, 768)]
    net.store(dqkv, dqkv_out)
    lone[:, pl.ds(1024, 768)] = dot(jnp.ones((8, 1024), LOW), wd[:, pl.ds(256, 768)], NN)
    line_down.take()
    net.store(down_last, down_b)
    line_up.take()
    net.store(up_last, up_b)
    net.drain()


def ahead(lengths, inputs, cotangent, small, w_qkv, w_out, w_up, w_down, qv_bias, up_bias):
    return pl.pallas_call(
        ahead_kernel,
        out_shape=(
            low_shape(OWN, D),
            low_shape(1024, D),
            low_shape(3, D, 256),
            full_shape(8, D),
            low_shape(1024, 768),
            full_shape(OWN, D),
            low_shape(2, 256, 256),
            low_shape(OWN, D),
            low_shape(256, 1024),
            low_shape(256, 1024),
            low_shape(1024, 256),
            low_shape(1024, 256),
            full_shape(8, D),
            full_shape(8, 1792),
        ),
        in_specs=[SM, HBM, HBM, *[VM] * 6, HBM, HBM, HBM, HBM, VM, VM],
        out_specs=(HBM,) * 12 + (VM, VM),
        scratch_shapes=[
            pltpu.VMEM((OWN, D), LOW),
            pltpu.VMEM((1024, D), LOW),
            pltpu.VMEM((1024, D), LOW),
            pltpu.VMEM((1024, 256), LOW),
            pltpu.VMEM((2, 2048, 256), LOW),
            pltpu.VMEM((1024, 256), LOW),
            pltpu.VMEM((3, D, 256), LOW),
            pltpu.VMEM((256, D), LOW),
            pltpu.VMEM((8, D), jnp.float32),
            *reduce_scratch(),
            pltpu.VMEM((OWN, D), jnp.float32),
            pltpu.VMEM((1024, D), LOW),
            pltpu.VMEM((1024, 1024), LOW),
            pltpu.VMEM((1024, 1024), LOW),
            pltpu.VMEM((D, 1024), LOW),
            pltpu.VMEM((1024, D), LOW),
            pltpu.VMEM((8, 256), jnp.float32),
            pltpu.VMEM((1024, 2), jnp.float32),
            pltpu.VMEM((1024, 256), LOW),
            pltpu.VMEM((1024, 256), jnp.float32),
            pltpu.VMEM((1024, 512), LOW),
            pltpu.VMEM((4, 1024, 256), LOW),
            pltpu.VMEM((3, 1024, 256), LOW),
            pltpu.VMEM((1024, 256), LOW),
            pltpu.VMEM((4, 256, 1024), LOW),
            pltpu.VMEM((4, 256, 1024), LOW),
            pltpu.VMEM((3, 256, 1024), LOW),
            pltpu.VMEM((256, 1024), LOW),
            pltpu.VMEM((6, 256, 256), LOW),
            *sems(232, 32),
        ],
        compiler_params=pltpu.CompilerParams(
            collective_id=1, has_side_effects=True, vmem_limit_bytes=64 * 2**20 - 2**16
        ),
        cost_estimate=pl.CostEstimate(flops=40 * 10**9, bytes_accessed=30 * 10**6, transcendentals=2 * 10**6),
    )(lengths, inputs, cotangent, *small, w_qkv, w_out, w_up, w_down, qv_bias, up_bias)


def in_rows(ref, body):
    rows, width = ref.shape[-2:]
    step = min(rows, 2 ** ((32768 // width).bit_length() - 1))
    tiles(rows // step, lambda t: body(part(t * step, step)))


class SideReduce:
    def __init__(self, net, block, inbox, first):
        self.net, self.block, self.inbox, self.slot = net, block, inbox, net.slots(8)
        self.windows = (pl.ds(0, first), pl.ds(first, inbox.shape[1] - first))

    def other(self, dy):
        return (1 - self.net.half) * 4 + (self.net.y + dy) % 4

    def mine(self, dy):
        return self.net.half * 4 + (self.net.y + dy) % 4

    def give(self, dy):
        for side, device in enumerate((self.net.partner(), self.net.cousin())):
            rows = self.windows[side]
            self.net.push(
                self.slot + dy * 2 + side, self.block(dy).at[rows], self.inbox.at[dy, rows], device
            )

    def take(self, dy):
        for side in range(2):
            self.net.got(self.slot + dy * 2 + side, self.inbox.at[dy, self.windows[side]])


class LineReduce:
    def __init__(self, net, blocks, inbox, last):
        self.net, self.blocks, self.inbox, self.last = net, blocks, inbox, last
        self.slot = net.slots(4)

    def give(self, dy):
        self.net.push(self.slot + dy - 1, self.blocks.at[dy], self.inbox.at[dy - 1], self.net.at(dy=dy))

    def settle(self):
        for dy in (1, 2, 3):
            self.net.got(self.slot + dy - 1, self.inbox.at[dy - 1])

        def add(rows):
            total = self.blocks[0, rows, :].astype(jnp.float32)
            for i in range(3):
                total += self.inbox[i, rows, :].astype(jnp.float32)
            self.blocks[0, rows, :] = total.astype(LOW)

        in_rows(self.last, add)

    def close(self):
        self.settle()
        self.net.push(self.slot + 3, self.blocks.at[0], self.last, self.net.at(dx=2))

    def take(self):
        self.net.got(self.slot + 3, self.last)

    def finish(self, emit):
        self.take()
        in_rows(
            self.last,
            lambda rows: emit(rows, self.blocks[0, rows, :].astype(jnp.float32) + self.last[rows, :].astype(jnp.float32)),
        )


class LineFirst:
    def __init__(self, net, block, inbox, total, side, last, first):
        self.net, self.block, self.inbox, self.total, self.side, self.last = net, block, inbox, total, side, last
        self.slot = net.slots(9)
        self.windows = (pl.ds(0, first), pl.ds(first, inbox.shape[1] - first))

    def owner(self, which, dy):
        half = 1 - self.net.half if which else self.net.half
        return half * 4 + (self.net.y + dy) % 4

    def give(self, which, dy):
        place = which * 3 + dy - 1
        self.net.push(self.slot + place, self.block(place), self.inbox.at[place], self.net.at(dy=dy))

    def take(self, which):
        for dy in (1, 2, 3):
            self.net.got(self.slot + which * 3 + dy - 1, self.inbox.at[which * 3 + dy - 1])

    def arrived(self, which, rows):
        return sum(self.inbox[which * 3 + i, rows, :].astype(jnp.float32) for i in range(3))

    def sideways(self):
        for i, device in enumerate((self.net.partner(), self.net.cousin())):
            rows = self.windows[i]
            self.net.push(self.slot + 6 + i, self.total.at[1, rows], self.side.at[rows], device)

    def close(self):
        for i in range(2):
            self.net.got(self.slot + 6 + i, self.side.at[self.windows[i]])

        def add(rows):
            total = self.total[0, rows, :].astype(jnp.float32) + self.side[rows, :].astype(jnp.float32)
            self.total[0, rows, :] = total.astype(LOW)

        in_rows(self.side, add)
        self.net.push(self.slot + 8, self.total.at[0], self.last, self.net.at(dx=2))

    def finish(self, emit):
        self.net.got(self.slot + 8, self.last)
        in_rows(
            self.last,
            lambda rows: emit(
                rows, self.total[0, rows, :].astype(jnp.float32) + self.last[rows, :].astype(jnp.float32)
            ),
        )


def emit_to(ref):
    def emit(rows, values):
        ref[rows, :] = values

    return emit


def norm_back(grad, centred, inverse, gain):
    scaled = grad * gain
    return inverse * (
        scaled - jnp.mean(scaled, -1, keepdims=True) - centred * jnp.mean(scaled * centred, -1, keepdims=True)
    )


def norm_parts(values):
    middle = jnp.mean(values, -1, keepdims=True)
    spread = jnp.mean(values * values, -1, keepdims=True) - middle * middle
    inverse = lax.rsqrt(spread + EPSILON)
    return (values - middle) * inverse, inverse


def column_sums(values):
    return jnp.sum(values, 0, keepdims=True)


def attend_back_chunk(chunk, q, kv, grad, att, lse, dq, dkv, half, length):
    slots = pl.ds(chunk * 512, 512)
    for head in range(2):
        at = pl.ds(head * HEAD, HEAD)
        key, value = kv(0, slots, head), kv(1, slots, head)
        dkey, dvalue = jnp.zeros((512, HEAD), jnp.float32), jnp.zeros((512, HEAD), jnp.float32)
        for group in range(chunk, 4):
            rows = pl.ds(group * 256, 256)
            query, upstream = q(rows, head), grad[rows, at]
            delta = jnp.sum(upstream.astype(jnp.float32) * att[rows, at].astype(jnp.float32), -1, keepdims=True)
            scores = dot(query, key, NT) * SCALE
            slot = chunk * 512 + lax.broadcasted_iota(jnp.int32, (1, 512), 1)
            allowed = slot < length
            if group == chunk:
                allowed = allowed & (slot <= place_rows(group, half))
            probs = jnp.exp(jnp.where(allowed, scores - lse[rows, pl.ds(head, 1)], -HUGE))
            dscores = (probs * (dot(upstream, value, NT) - delta)).astype(LOW)
            share = dot(dscores, key, NN)
            if group == chunk:
                dq[rows, at] = share
            else:
                dq[rows, at] += share
            dkey += dot(dscores, query, TN)
            dvalue += dot(probs.astype(LOW), upstream, TN)
        dkv(0, slots, head, (dkey * SCALE).astype(LOW))
        dkv(1, slots, head, dvalue.astype(LOW))


class Everyone:
    def __init__(self, net, axis, inbox):
        self.net, self.axis, self.inbox, self.slot = net, axis, inbox, net.slots(7)
        self.index = net.row if axis == "row" else net.col

    def device(self, shift):
        net, index = self.net, (self.index + shift) % 8
        row, col = (index, net.col) if self.axis == "row" else (net.row, index)
        return {"dp": net.dp, "row": row, "col": col}

    def begin(self, src_of):
        for shift in range(1, 8):
            to = (self.index + shift) % 8
            self.net.push(self.slot + shift - 1, src_of(to), self.inbox.at[self.index], self.device(shift))
        self.copy = self.net.move(src_of(self.index), self.inbox.at[self.index])

    def total(self):
        self.copy.wait()
        for shift in range(1, 8):
            self.net.got(self.slot + shift - 1, self.inbox.at[(self.index + 8 - shift) % 8])
        total = self.inbox[0]
        for i in range(1, 8):
            total += self.inbox[i]
        return total


class Blocks:
    def __init__(self, net, src, inbox):
        self.net, self.src, self.inbox, self.slot = net, src, inbox, net.slots(15)

    def begin(self):
        net = self.net
        place = self.inbox.at[net.dp * 8 + net.row]
        for shift in range(16):
            row = (net.row + shift) % 8
            block = self.src.at[:, part(row * 256, 256)]
            if shift == 0:
                self.copy = net.move(block, place)
            else:
                dp = net.dp if shift < 8 else 1 - net.dp
                net.push(self.slot + shift - 1, block, place, {"dp": dp, "row": row, "col": net.col})

    def total(self):
        net = self.net
        self.copy.wait()
        for shift in range(1, 16):
            dp = net.dp if shift < 8 else 1 - net.dp
            net.got(self.slot + shift - 1, self.inbox.at[dp * 8 + (net.row + 16 - shift) % 8])
        total = self.inbox[0]
        for i in range(1, 16):
            total += self.inbox[i]
        return total


def fourth_kernel(
    dqkv_in, n1_in, wq_in, x_in, dmid_in, wide, gout_in, mixed_in, sums, single,
    grad_low, mixed_out, qkv_grad, out_out, wide_grad, lone_grad,
    dqkv, n1, wq, x, dmid, grad_own, mixed_own, mixed, out_grad, terms, near, left, right, ends,
    gout, gout_side, gout_last, gqk, gqk_side, gqk_line, gqk_last, gv, gv_line, gv_total, gv_side, gv_last,
    early, early_cols, late, late_cols, wide_part, wide_rows, packed, single_rows, single_part, single_last,
    send, recv, local,
):
    net = Net(send, recv, local)
    load = {}
    for name, a, b in (
        ("dqkv", dqkv_in, dqkv), ("wq", wq_in, wq), ("n1", n1_in, n1), ("gout", gout_in, gout),
        ("mixed", mixed_in, mixed_own), ("x", x_in, x), ("dmid", dmid_in, dmid),
    ):
        load[name] = net.move(a, b)
    cols = [{"dp": net.dp, "row": net.row, "col": (net.col + d) % 8} for d in range(1, 8)]
    across = [{"dp": 1 - net.dp, "row": (net.row + d) % 8, "col": net.col} for d in (0, 1, 2, 3, 5, 6, 7)]
    net.greet(across, cols)
    back = ColReduce(net, terms, near, left, right, ends)
    side_qk = SideReduce(net, lambda dy: gqk.at[dy], gqk_side, 128)
    line_qk = LineReduce(net, gqk_side, gqk_line, gqk_last)
    sum_v = LineFirst(net, lambda i: gv.at[i], gv_line, gv_total, gv_side, gv_last, 128)
    sum_out = LineFirst(net, None, gout_side, gout, gout_side, gout_last, 128)
    wide_early, wide_late = Everyone(net, "col", early_cols), Everyone(net, "col", late_cols)
    wide_b = Blocks(net, wide_part, wide_rows)
    single_a = Everyone(net, "row", single_rows)
    crossing = net.slots(1)

    def feature_block(ref):
        return lambda r: ref.at[:, part(r * 256, 256)]

    def token_block(ref):
        return lambda r: ref.at[(r // 2) % 2, r % 2, part(r // 4 * OWN, OWN)]

    mixed_swap = Swap(net, feature_block(mixed_own), token_block(mixed))
    grad_swap = Swap(net, feature_block(grad_own), token_block(grad_low))

    def spread(dz):
        rows = part((net.z + dz) % 4 * 256, 256)

        def tile(t):
            at = part(t * 512, 512)
            total = dot(dqkv[rows, pl.ds(0, 256)], wq[0, at, :], NT)
            for i in (1, 2):
                total += dot(dqkv[rows, pl.ds(i * 256, 256)], wq[i, at, :], NT)
            terms[rows, at] = total.astype(LOW)

        tiles(4, tile)

    def descend(dz):
        spread(dz)
        back.give(dz)

    def qk_tile(r):
        return dot(n1[:, part(r * 256, 256)], dqkv[:, pl.ds(0, 512)], TN)

    def v_tile(r):
        return dot(n1[:, part(r * 256, 256)], dqkv[:, pl.ds(512, 256)], TN)

    def qk_make(dy):
        gqk[dy] = qk_tile(side_qk.other(dy)).astype(LOW)

    def qk_give(dy):
        qk_make(dy)
        side_qk.give(dy)

    def qk_add(dy):
        side_qk.take(dy)
        gqk_side[dy] = (qk_tile(side_qk.mine(dy)) + gqk_side[dy].astype(jnp.float32)).astype(LOW)
        if dy:
            line_qk.give(dy)

    def v_give(which, dy):
        gv[which * 3 + dy - 1] = v_tile(sum_v.owner(which, dy)).astype(LOW)
        sum_v.give(which, dy)

    def v_add(which):
        sum_v.take(which)
        total = v_tile(sum_v.owner(which, 0)) + sum_v.arrived(which, pl.ds(0, 256))
        gv_total[which] = total.astype(LOW)

    for i in range(7):
        packed[i : i + 1, :] = single[0:1, i * 256 : (i + 1) * 256]
    packed[7:8, :] = jnp.zeros((1, 256), jnp.float32)
    for i in range(4):
        for j in range(4):
            early[i * 4 + j : i * 4 + j + 1, :] = sums[2 + i : 3 + i, j * 512 : (j + 1) * 512]
    for name in ("dqkv", "n1", "wq"):
        load[name].wait()
    for dy in (2, 1):
        qk_make(dy)
    spread(2)
    net.meet()
    for dy in (2, 1):
        side_qk.give(dy)
    back.give(2)
    single_a.begin(lambda r: packed)
    wide_early.begin(lambda r: early)
    load["gout"].wait()
    sum_out.sideways()
    for dy in (2, 1, 3):
        v_give(1, dy)
    descend(1)
    back.far()
    for dy in (3, 0):
        qk_give(dy)
    descend(3)
    back.own(1)
    back.own(3)
    for dy in (2, 1, 3):
        v_give(0, dy)
    descend(0)
    back.forward(1)
    back.forward(3)
    sum_out.close()
    for dy in (2, 1, 3, 0):
        qk_add(dy)
    load["mixed"].wait()
    mixed_swap.begin()
    load["x"].wait()
    load["dmid"].wait()
    back.finish()
    totals = [jnp.zeros((1, D), jnp.float32)] * 2
    for piece in range(4):
        rows = pl.ds(piece * 32, 32)
        grad = back.result(piece * 32, 32)
        centred, inverse = norm_parts(x[rows, :].astype(jnp.float32))
        value = dmid[rows, :] + norm_back(grad, centred, inverse, wide[0:1, :])
        grad_own[rows, :] = value.astype(LOW)
        totals = [a + column_sums(b) for a, b in zip(totals, (grad * centred, grad))]
    for i in range(2):
        for j in range(4):
            late[i * 4 + j : i * 4 + j + 1, :] = totals[i][:, j * 512 : (j + 1) * 512]
    wide_late.begin(lambda r: late)
    wide_part[6:8, :] = jnp.zeros((2, D), jnp.float32)
    total = wide_early.total()
    for i in range(4):
        for j in range(4):
            wide_part[2 + i : 3 + i, j * 512 : (j + 1) * 512] = total[i * 4 + j : i * 4 + j + 1, :]
    v_add(1)
    sum_v.sideways()
    total = wide_late.total()
    for i in range(2):
        for j in range(4):
            wide_part[i : i + 1, j * 512 : (j + 1) * 512] = total[i * 4 + j : i * 4 + j + 1, :]
    wide_b.begin()
    grad_swap.begin()
    single_part[...] = single_a.total()
    net.push(crossing, single_part, single_last, net.at(dx=2))
    v_add(0)
    sum_v.close()
    line_qk.close()
    mixed_swap.finish()
    net.store(mixed, mixed_out)
    grad_swap.finish()
    wide_grad[...] = wide_b.total()
    net.got(crossing, single_last)
    lone_grad[...] = single_part[...] + single_last[...]

    def emit_qk(rows, values):
        for i in range(2):
            qkv_grad[i, rows, :] = values[:, i * 256 : (i + 1) * 256]

    def emit_v(rows, values):
        qkv_grad[2, rows, :] = values

    sum_out.finish(emit_to(out_grad))
    line_qk.finish(emit_qk)
    sum_v.finish(emit_v)
    net.store(out_grad, out_out)
    net.drain()


def fourth(dqkv, n1, wq, x, dmid, wide, gout, mixed, sums, lone):
    return pl.pallas_call(
        fourth_kernel,
        out_shape=(
            low_shape(2, 2, 256, 256),
            low_shape(2, 2, 256, 256),
            full_shape(3, 256, 256),
            full_shape(256, 256),
            full_shape(8, 256),
            full_shape(8, 256),
        ),
        in_specs=[HBM, HBM, HBM, HBM, HBM, VM, HBM, HBM, VM, VM],
        out_specs=(VM, HBM, VM, HBM, VM, VM),
        scratch_shapes=[
            pltpu.VMEM((1024, 768), LOW),
            pltpu.VMEM((1024, D), LOW),
            pltpu.VMEM((3, D, 256), LOW),
            pltpu.VMEM((OWN, D), LOW),
            pltpu.VMEM((OWN, D), jnp.float32),
            pltpu.VMEM((OWN, D), LOW),
            pltpu.VMEM((OWN, D), LOW),
            pltpu.VMEM((2, 2, 256, 256), LOW),
            pltpu.VMEM((256, 256), jnp.float32),
            *reduce_scratch(),
            pltpu.VMEM((2, 256, 256), LOW),
            pltpu.VMEM((256, 256), LOW),
            pltpu.VMEM((256, 256), LOW),
            pltpu.VMEM((4, 256, 512), LOW),
            pltpu.VMEM((4, 256, 512), LOW),
            pltpu.VMEM((3, 256, 512), LOW),
            pltpu.VMEM((256, 512), LOW),
            pltpu.VMEM((6, 256, 256), LOW),
            pltpu.VMEM((6, 256, 256), LOW),
            pltpu.VMEM((2, 256, 256), LOW),
            pltpu.VMEM((256, 256), LOW),
            pltpu.VMEM((256, 256), LOW),
            pltpu.VMEM((16, 512), jnp.float32),
            pltpu.VMEM((8, 16, 512), jnp.float32),
            pltpu.VMEM((8, 512), jnp.float32),
            pltpu.VMEM((8, 8, 512), jnp.float32),
            pltpu.VMEM((8, D), jnp.float32),
            pltpu.VMEM((16, 8, 256), jnp.float32),
            pltpu.VMEM((8, 256), jnp.float32),
            pltpu.VMEM((8, 8, 256), jnp.float32),
            pltpu.VMEM((8, 256), jnp.float32),
            pltpu.VMEM((8, 256), jnp.float32),
            *sems(120, 24),
        ],
        compiler_params=pltpu.CompilerParams(
            collective_id=4, has_side_effects=True, vmem_limit_bytes=60 * 2**20
        ),
        cost_estimate=pl.CostEstimate(flops=40 * 10**9, bytes_accessed=30 * 10**6, transcendentals=2 * 10**6),
    )(dqkv, n1, wq, x, dmid, wide, gout, mixed, sums, lone)


def hand_over_kernel(
    mixed_in, grad_in, qkv_in, out_in, up_a, up_b, down_a, down_b, wide, lone,
    mixed, input_grad, gain1, bias1, qkv, qv, out, out_bias, gain2, bias2, up, up_bias, down, down_bias,
    a_down, b_down, a_up, b_up, low_grad, qkv_part, mixed_part, out_part, full_down, full_up, full_grad, done,
):
    def move(i, src, dst):
        copy = pltpu.make_async_copy(src, dst, done.at[i])
        copy.start()
        return copy

    sources = (
        (down_a, a_down), (down_b, b_down), (up_a, a_up), (up_b, b_up), (grad_in, low_grad), (qkv_in, qkv_part), (mixed_in, mixed_part),
        (out_in, out_part),
    )
    fetches = [move(i, a, b) for i, (a, b) in enumerate(sources)]
    for i, ref in enumerate((gain1, bias1, out_bias, gain2, bias2, down_bias)):
        ref[...] = wide[i : i + 1, :]
    for i in range(4):
        up_bias[:, i * 256 : (i + 1) * 256] = lone[i : i + 1, :]
    qv[0:1, :] = lone[4:5, :]
    qv[1:2, :] = lone[6:7, :]
    stores = []
    for i, (full, a, b, ref) in enumerate(((full_down, a_down, b_down, down), (full_up, a_up, b_up, up))):
        fetches[2 * i].wait()
        fetches[2 * i + 1].wait()

        def add(rows):
            full[rows, :] = a[rows, :].astype(jnp.float32) + b[rows, :].astype(jnp.float32)

        in_rows(full, add)
        stores.append(move(8 + i, full, ref))
    fetches[4].wait()
    for i in range(2):
        for j in range(2):
            full_grad[i, j] = low_grad[i, j].astype(jnp.float32)
    stores.append(move(10, full_grad, input_grad))
    for i, (src, ref) in enumerate(((qkv_part, qkv), (mixed_part, mixed), (out_part, out))):
        fetches[5 + i].wait()
        stores.append(move(11 + i, src, ref))
    for store in stores:
        store.wait()


def hand_over(mixed, grad, qkv, out, up_a, up_b, down_a, down_b, wide, lone):
    vector = full_shape(1, 256)
    return pl.pallas_call(
        hand_over_kernel,
        out_shape=(
            low_shape(2, 2, 256, 256),
            full_shape(2, 2, 256, 256),
            vector,
            vector,
            full_shape(3, 256, 256),
            full_shape(2, 256),
            full_shape(256, 256),
            vector,
            vector,
            vector,
            full_shape(256, 1024),
            full_shape(1, 1024),
            full_shape(1024, 256),
            vector,
        ),
        in_specs=[HBM] * 8 + [VM, VM],
        out_specs=(HBM, HBM, VM, VM, HBM, VM, HBM, VM, VM, VM, HBM, VM, HBM, VM),
        scratch_shapes=[
            pltpu.VMEM((1024, 256), LOW),
            pltpu.VMEM((1024, 256), LOW),
            pltpu.VMEM((256, 1024), LOW),
            pltpu.VMEM((256, 1024), LOW),
            pltpu.VMEM((2, 2, 256, 256), LOW),
            pltpu.VMEM((3, 256, 256), jnp.float32),
            pltpu.VMEM((2, 2, 256, 256), LOW),
            pltpu.VMEM((256, 256), jnp.float32),
            pltpu.VMEM((1024, 256), jnp.float32),
            pltpu.VMEM((256, 1024), jnp.float32),
            pltpu.VMEM((2, 2, 256, 256), jnp.float32),
            pltpu.SemaphoreType.DMA((14,)),
        ],
        compiler_params=pltpu.CompilerParams(vmem_limit_bytes=63 * 2**20),
    )(mixed, grad, qkv, out, up_a, up_b, down_a, down_b, wide, lone)


def shards(
    inputs,
    lengths,
    ln1_gain,
    ln1_bias,
    w_qkv,
    qv_bias,
    w_out,
    out_bias,
    ln2_gain,
    ln2_bias,
    w_up,
    up_bias,
    w_down,
    down_bias,
    cotangent,
):
    small = [a.reshape(1, 256) for a in (ln1_gain, ln1_bias, out_bias, ln2_gain, ln2_bias, down_bias)]
    x, all1, wq, wide, dqkv, dmid, gout, mixed, up_a, up_b, down_a, down_b, sums, lone = ahead(
        lengths, inputs, cotangent, small, w_qkv, w_out, w_up, w_down, qv_bias, up_bias.reshape(1, 1024)
    )
    grad, mixed, g_qkv, g_out, wide_grad, lone_grad = fourth(dqkv, all1, wq, x, dmid, wide, gout, mixed, sums, lone)
    outs = hand_over(mixed, grad, g_qkv, g_out, up_a, up_b, down_a, down_b, wide_grad, lone_grad)
    return tuple(a.reshape(-1) if a.shape[0] == 1 else a for a in outs)


def solution(mesh):
    tokens = P(None, "dp", "col", "row")
    in_specs = (
        tokens,
        P(None, "dp"),
        P("row"),
        P("row"),
        P(None, "row", "col"),
        P(None, "col"),
        P("col", "row"),
        P("row"),
        P("row"),
        P("row"),
        P("row", "col"),
        P("col"),
        P("col", "row"),
        P("row"),
        tokens,
    )
    out_specs = (
        tokens,
        tokens,
        P("row"),
        P("row"),
        P(None, "row", "col"),
        P(None, "col"),
        P("col", "row"),
        P("row"),
        P("row"),
        P("row"),
        P("row", "col"),
        P("col"),
        P("col", "row"),
        P("row"),
    )
    return jax.shard_map(shards, mesh=mesh, in_specs=in_specs, out_specs=out_specs, check_vma=False)
```
